32 devices in a mesh: dp: 8 (over z, x), tensor: 4 (over y, core).
Axes of the slice: x: 2, y: 2, z: 4, core: 2. Of those that a mesh axis runs over, the one named last changes fastest.
Arguments:
- tokens: bfloat16 [7680, 1024], P(('dp', 'tensor')), may hold values from -6 to 6
- keep_mask: int32 [24, 320], P('dp'), may hold values from 0 to 1, as said below
- grad_out: bfloat16 [7680, 1024], P(('dp', 'tensor')), may hold values from -12 to 12
- in_weight: bfloat16 [1024, 3072], P(None, 'tensor'), may hold values from -0.1875 to 0.1875
- in_bias: float32 [2048], P('tensor'), may hold values from -3 to 3
- out_weight: bfloat16 [1024, 1024], P('tensor'), may hold values from -0.75 to 0.75
- out_bias: float32 [1024], replicated, may hold values from -2 to 2
- up_weight: bfloat16 [1024, 4096], P(None, 'tensor'), may hold values from -0.1875 to 0.1875
- up_bias: float32 [4096], P('tensor'), may hold values from -3 to 3
- down_weight: bfloat16 [4096, 1024], P('tensor'), may hold values from -0.09375 to 0.09375
- down_bias: float32 [1024], replicated, may hold values from -2 to 2
- gain_one: float32 [1024], replicated, may hold values from 0.25 to 1.75
- shift_one: float32 [1024], replicated, may hold values from -2 to 2
- gain_two: float32 [1024], replicated, may hold values from 0.25 to 1.75
- shift_two: float32 [1024], replicated, may hold values from -2 to 2
Outputs:
- output: bfloat16 [7680, 1024], P(('dp', 'tensor'))
- tokens_grad: float32 [7680, 1024], P(('dp', 'tensor'))
- in_weight_grad: float32 [1024, 3072], P(None, 'tensor')
- in_bias_grad: float32 [2048], P('tensor')
- out_weight_grad: float32 [1024, 1024], P('tensor')
- out_bias_grad: float32 [1024], replicated
- up_weight_grad: float32 [1024, 4096], P(None, 'tensor')
- up_bias_grad: float32 [4096], P('tensor')
- down_weight_grad: float32 [4096, 1024], P('tensor')
- down_bias_grad: float32 [1024], replicated
- gain_one_grad: float32 [1024], replicated
- shift_one_grad: float32 [1024], replicated
- gain_two_grad: float32 [1024], replicated
- shift_two_grad: float32 [1024], replicated
The draws below stay inside these ranges and needn't reach their ends.
Inputs may be any that keep to these rules, and one draw needn't show every extreme that they name: `keep_mask`: 1 in the first 64 slots of every image and in at least one of its other 256 slots.
All inputs are finite; a program needn't handle non-finite values.
Results may differ from the reference program's by a relative error of at most 0.012.
The reference program's roundings to bfloat16 on the way count: a program that leaves them out, or rounds other values in their place, can miss the bound.
Values may be sent and summed in bfloat16 or wider, within the bound.
No kernel may reach another device: no remote copies, remote signals or barrier semaphores. Data moves between devices by JAX's collectives and lax.ppermute only.
A program may use at most 128 MiB of HBM per device.

```python
import jax
import jax.numpy as jnp
from jax import lax

D = 1024
HD = 64
FF = 4096
BUF = 64
IMG_TOK = 256
IMG_DEV = 3
SLOTS = 320
IMAGES = 24
TOKENS = 7680


def draw_keep_mask(key, part):
    key = jax.random.fold_in(key, 1)
    count_key, order_key = jax.random.split(key)
    counts = jax.random.randint(count_key, (IMAGES, 1), 1, IMG_TOK + 1)
    rank_rows = jax.vmap(lambda single: jax.random.permutation(single, IMG_TOK))(jax.random.split(order_key, IMAGES))
    kept_part = (rank_rows < counts).astype(jnp.int32)
    buffer_part = jnp.ones((IMAGES, BUF), jnp.int32)
    return jnp.concatenate([buffer_part, kept_part], axis=1)


def draw_grad_out(key, part):
    key = jax.random.fold_in(key, 2)
    noise_key = jax.random.fold_in(key, 0)
    position = jnp.arange(TOKENS, dtype=jnp.float32) / (TOKENS - 1)
    rising = 1.0 + 2.0 * position
    values = jax.random.normal(noise_key, (TOKENS, D), jnp.float32) * rising[:, None]
    return jnp.clip(values, -12.0, 12.0).astype(jnp.bfloat16)


def shard_levels(rng, shape, cuts, smallest, largest):
    def one(dim, shards_of):
        draws = jax.random.uniform(jax.random.fold_in(jax.random.fold_in(rng, 6), dim), (shards_of,), jnp.float32, smallest / len(cuts), largest / len(cuts))
        return jnp.repeat(jnp.exp(draws), shape[dim] // shards_of).reshape((-1,) + (1,) * (len(shape) - dim - 1))

    level = one(*cuts[0])
    for cut in cuts[1:]:
        level = level * one(*cut)
    return level


def gaussian(own_key, shape, width, reach, cuts=(), kind=jnp.bfloat16):
    drawn = width * jax.random.normal(own_key, shape, jnp.float32)
    if cuts:
        drawn = drawn * shard_levels(own_key, shape, cuts, -0.22, 0.18)
    return jnp.clip(drawn, -reach, reach).astype(kind)


def setup_inputs(seed: int = 0) -> dict:
    arg_keys = jax.random.split(jax.random.key(seed), 16)
    return {
        "tokens": gaussian(arg_keys[0], (TOKENS, D), 1.0, 6.0, ((0, 32),)),
        "keep_mask": draw_keep_mask(jax.random.fold_in(arg_keys[15], 71), 0),
        "grad_out": draw_grad_out(jax.random.fold_in(arg_keys[15], 71), 0),
        "in_weight": gaussian(arg_keys[3], (D, 3 * D), D ** -0.5, 0.1875, ((1, 4),)),
        "in_bias": gaussian(arg_keys[4], (2 * D,), 0.5, 3.0, ((0, 4),), jnp.float32),
        "out_weight": gaussian(arg_keys[5], (D, D), (D // 16) ** -0.5, 0.75, ((0, 4),)),
        "out_bias": gaussian(arg_keys[6], (D,), 0.3, 2.0, (), jnp.float32),
        "up_weight": gaussian(arg_keys[7], (D, FF), D ** -0.5, 0.1875, ((1, 4),)),
        "up_bias": gaussian(arg_keys[8], (FF,), 0.5, 3.0, ((0, 4),), jnp.float32),
        "down_weight": gaussian(arg_keys[9], (FF, D), FF ** -0.5, 0.09375, ((0, 4),)),
        "down_bias": gaussian(arg_keys[10], (D,), 0.3, 2.0, (), jnp.float32),
        "gain_one": jnp.clip(1.0 + 0.15 * jax.random.normal(arg_keys[11], (D,), jnp.float32), 0.25, 1.75),
        "shift_one": gaussian(arg_keys[12], (D,), 0.3, 2.0, (), jnp.float32),
        "gain_two": jnp.clip(1.0 + 0.15 * jax.random.normal(arg_keys[13], (D,), jnp.float32), 0.25, 1.75),
        "shift_two": gaussian(arg_keys[14], (D,), 0.3, 2.0, (), jnp.float32),
    }


HIGHEST = lax.Precision.HIGHEST
EPSILON = 1e-06

@jax.custom_vjp
def low(v):
    return lax.optimization_barrier(v.astype(jnp.bfloat16)).astype(jnp.float32)

@jax.custom_vjp
def low_back(v):
    return v

def low_keep(v):
    return (low(v), None)

def low_pass(kept, grad):
    return (grad,)

def back_keep(v):
    return (v, None)

def back_low(kept, grad):
    return (low(grad),)
low.defvjp(low_keep, low_pass)
low_back.defvjp(back_keep, back_low)

def layer_norm(values, gain, shift):
    average = lax.optimization_barrier(jnp.mean(values, axis=-1, keepdims=True))
    centred = values - average
    variance = lax.optimization_barrier(jnp.mean(centred * centred, axis=-1, keepdims=True))
    return centred * lax.rsqrt(variance + EPSILON) * gain + shift

def gelu_exact(values):
    return jax.nn.gelu(values, approximate=False)

def encoder_layer(token_block, keep_rows, in_weight, in_bias, out_weight, out_bias, up_weight, up_bias, down_weight, down_bias, gain_one, shift_one, gain_two, shift_two):
    row_count = token_block.shape[0]
    images = row_count // SLOTS
    head_count = D // HD
    first_normed = low(layer_norm(token_block, gain_one, shift_one))
    projected = low_back(jnp.dot(first_normed, in_weight, precision=HIGHEST)).reshape(row_count, head_count, 3, HD)
    bias_pair = in_bias.reshape(head_count, 2, HD)
    bias_full = jnp.concatenate([bias_pair[:, :1], jnp.zeros((head_count, 1, HD), jnp.float32), bias_pair[:, 1:]], axis=1)
    packed = low(projected + bias_full).reshape(images, SLOTS, head_count, 3, HD)
    query_rows = packed[:, :, :, 0]
    key_rows = packed[:, :, :, 1]
    value_rows = packed[:, :, :, 2]
    scores = low_back(jnp.einsum('ishd,ithd->ihst', query_rows, key_rows, precision=HIGHEST) * HD ** (-0.5))
    key_live = keep_rows.reshape(images, 1, 1, SLOTS) > 0
    scores = jnp.where(key_live, scores, -1000000000.0)
    maximum = lax.optimization_barrier(jnp.max(scores, axis=-1, keepdims=True))
    exponent = jnp.exp(scores - maximum)
    attention = low(exponent / lax.optimization_barrier(jnp.sum(exponent, axis=-1, keepdims=True)))
    heads_out = low_back(low(jnp.einsum('ihst,ithd->ishd', attention, value_rows, precision=HIGHEST)))
    heads_out = heads_out.reshape(row_count, D)
    middle = token_block + low_back(jnp.dot(heads_out, out_weight, precision=HIGHEST)) + out_bias
    second = low(layer_norm(middle, gain_two, shift_two))
    pre_act = low_back(jnp.dot(second, up_weight, precision=HIGHEST)) + up_bias
    act_low = low(gelu_exact(pre_act))
    branch = low_back(jnp.dot(act_low, down_weight, precision=HIGHEST)) + down_bias
    return keep_rows[:, None] * (middle + branch)

def reference(tokens, keep_mask, grad_out, in_weight, in_bias, out_weight, out_bias, up_weight, up_bias, down_weight, down_bias, gain_one, shift_one, gain_two, shift_two):
    params = tuple((entry.astype(jnp.float32) for entry in (in_weight, in_bias, out_weight, out_bias, up_weight, up_bias, down_weight, down_bias, gain_one, shift_one, gain_two, shift_two)))
    block_count = IMAGES // IMG_DEV
    block_rows = IMG_DEV * SLOTS
    token_blocks = tokens.astype(jnp.float32).reshape(block_count, block_rows, D)
    keep_blocks = keep_mask.astype(jnp.float32).reshape(block_count, block_rows)
    grad_blocks = grad_out.astype(jnp.float32).reshape(block_count, block_rows, D)

    def scan_step(totals, blocks_in):
        token_block, keep_block, grad_block = blocks_in

        def apply_layer(block_in, *weights):
            return encoder_layer(block_in, keep_block, *weights)
        result, pullback = jax.vjp(apply_layer, token_block, *params)
        gradients = pullback(grad_block)
        totals = tuple((earlier + added for earlier, added in zip(totals, gradients[1:])))
        return (totals, (result.astype(jnp.bfloat16), gradients[0]))
    initial = tuple((jnp.zeros_like(entry) for entry in params))
    totals, (outputs, token_grads) = lax.scan(scan_step, initial, (token_blocks, keep_blocks, grad_blocks))
    output_all = outputs.reshape(TOKENS, D)
    token_grad = token_grads.reshape(TOKENS, D)
    return (output_all, token_grad, totals[0], totals[1], totals[2], totals[3], totals[4], totals[5], totals[6], totals[7], totals[8], totals[9], totals[10], totals[11])
```

```python
import jax
import jax.numpy as jnp
from jax import lax
from jax.sharding import PartitionSpec as P

HD = 64
SLOTS = 320
EPSILON = 1e-06
BF = jnp.bfloat16
F32 = jnp.float32


def gelu_exact(values):
    return jax.nn.gelu(values, approximate=False)


def mm(left, right, dims):
    return lax.dot_general(left, right, (dims, ((), ())), preferred_element_type=F32)


def swap(values, axis, bit):
    count = lax.axis_size(axis)
    return lax.ppermute(values, axis, [(i, i ^ bit) for i in range(count)])


def gather_rows(own):
    core = swap(own, "tensor", 1)
    far = swap(own, "tensor", 2)
    return own, core, far, swap(far, "tensor", 1)


def scatter_rows(blocks):
    far = blocks[2] + swap(blocks[3].astype(BF), "tensor", 1).astype(F32)
    near = blocks[0] + swap(blocks[1].astype(BF), "tensor", 1).astype(F32)
    return near + swap(far.astype(BF), "tensor", 2).astype(F32)


def reorder(blocks):
    me = lax.axis_index("tensor")
    core = (me & 1) > 0
    far = (me & 2) > 0
    a, b, c, d = blocks
    a, b = jnp.where(core, b, a), jnp.where(core, a, b)
    c, d = jnp.where(core, d, c), jnp.where(core, c, d)
    return (
        jnp.where(far, c, a),
        jnp.where(far, d, b),
        jnp.where(far, a, c),
        jnp.where(far, b, d),
    )


def split_rows(values, count):
    rows = values.shape[0] // count
    return tuple(values[i * rows : (i + 1) * rows] for i in range(count))


def add_small(own, other_packed):
    high, low = unpack(own)
    other_high, other_low = unpack(other_packed)
    return pack((high + low) + (other_high + other_low))


def pack(values):
    high = values.astype(BF)
    low = (values - high.astype(F32)).astype(BF)
    return jnp.concatenate([high, low], axis=0)


def unpack(packed):
    half = packed.shape[0] // 2
    return packed[:half].astype(F32), packed[half:].astype(F32)


def sum_over_data(values, order, small=None):
    count = lax.axis_size("dp")
    me = lax.axis_index("dp")
    bits = [1 << i for i in range(count.bit_length() - 1)]
    halved = [bits[i] for i in order if i < len(bits)]
    rest = bits[len(halved) :]
    for bit in halved:
        low, high = split_rows(values, 2)
        mine = (me & bit) > 0
        sent = jnp.where(mine, low, high).astype(BF)
        values = jnp.where(mine, high, low) + swap(sent, "dp", bit).astype(F32)
    values = values.astype(BF)
    for bit in rest:
        values = (values.astype(F32) + swap(values, "dp", bit).astype(F32)).astype(BF)
        if small is not None:
            small = add_small(small, swap(small, "dp", bit))
    for bit in reversed(halved):
        rows = values.shape[0]
        mine = (me & bit) > 0
        if small is None:
            other = swap(values, "dp", bit)
        else:
            other = swap(jnp.concatenate([values, small], axis=0), "dp", bit)
            small = add_small(small, other[rows:])
            other = other[:rows]
        values = jnp.concatenate(
            [jnp.where(mine, other, values), jnp.where(mine, values, other)], axis=0
        )
    return (values.astype(F32), small)


def normalise(values):
    average = jnp.mean(values, axis=-1, keepdims=True)
    centred = values - average
    factor = lax.rsqrt(jnp.mean(centred * centred, axis=-1, keepdims=True) + EPSILON)
    return centred * factor, factor


def norm_back(grad, gain, z, factor):
    s = grad * gain
    return factor * (
        s - jnp.mean(s, axis=-1, keepdims=True) - z * jnp.mean(s * z, axis=-1, keepdims=True)
    )


def on_device(
    tokens,
    keep_mask,
    grad_out,
    in_weight,
    in_bias,
    out_weight,
    out_bias,
    up_weight,
    up_bias,
    down_weight,
    down_bias,
    gain_one,
    shift_one,
    gain_two,
    shift_two,
):
    rows = tokens.shape[0]
    me = lax.axis_index("tensor")
    keep_flat = keep_mask.reshape(-1)
    keep_blocks = tuple(
        lax.dynamic_slice_in_dim(keep_flat, (me ^ i) * rows, rows)[:, None] for i in range(4)
    )
    keep_own = keep_blocks[0].astype(F32)
    images = keep_mask.shape[0]
    heads = in_weight.shape[1] // (3 * HD)

    token_values = tokens.astype(F32)
    z_one, factor_one = normalise(token_values)
    normed_one = reorder(gather_rows((z_one * gain_one + shift_one).astype(BF)))
    normed_one = jnp.concatenate(normed_one, axis=0)
    cot_own = grad_out.astype(F32) * keep_own
    cot_all = jnp.concatenate(gather_rows(cot_own.astype(BF)), axis=0)
    projected = mm(normed_one, in_weight, ((1,), (0,))).reshape(-1, heads, 3, HD)
    bias_pair = in_bias.reshape(heads, 2, HD)
    bias_full = jnp.concatenate(
        [bias_pair[:, :1], jnp.zeros((heads, 1, HD), F32), bias_pair[:, 1:]], axis=1
    )
    packed = (projected + bias_full).astype(BF).reshape(images, SLOTS, heads, 3, HD)
    q, k, v = packed[:, :, :, 0], packed[:, :, :, 1], packed[:, :, :, 2]
    live = keep_mask.reshape(images, 1, 1, SLOTS) > 0
    scores = jnp.einsum("ishd,ithd->ihst", q, k, preferred_element_type=F32) * HD ** (-0.5)
    scores = jnp.where(live, scores, -1000000000.0)
    maximum = jnp.max(scores, axis=-1, keepdims=True)
    exponent = jnp.exp(scores - maximum)
    probs = exponent / jnp.sum(exponent, axis=-1, keepdims=True)
    heads_out = jnp.einsum("ihst,ithd->ishd", probs.astype(BF), v, preferred_element_type=F32)
    heads_out = heads_out.astype(BF).reshape(images * SLOTS, heads * HD)
    partial = reorder(split_rows(mm(heads_out, out_weight, ((1,), (0,))), 4))
    middle = token_values + scatter_rows(partial) + out_bias
    z_two, factor_two = normalise(middle)
    second = jnp.concatenate(
        gather_rows((z_two * gain_two + shift_two).astype(BF)), axis=0
    )
    pre_act = mm(second, up_weight, ((1,), (0,))) + up_bias
    act_low = gelu_exact(pre_act).astype(BF)

    act_grad = mm(cot_all, down_weight, ((1,), (1,)))
    pre_grad = jax.vjp(gelu_exact, pre_act)[1](act_grad)[0]
    pre_low = pre_grad.astype(BF)
    second_grad = scatter_rows(split_rows(mm(pre_low, up_weight, ((1,), (1,))), 4))
    down_weight_grad = mm(act_low, cot_all, ((0,), (0,)))
    up_weight_grad = mm(second, pre_low, ((0,), (0,)))
    up_bias_grad = jnp.sum(pre_grad, axis=0)
    feed = scatter_rows(split_rows(mm(act_low, down_weight, ((1,), (0,))), 4))
    output = (keep_own * (middle + feed + down_bias)).astype(BF)
    down_sum, _ = sum_over_data(down_weight_grad, (0, 1, 2))
    up_sum, _ = sum_over_data(up_weight_grad, (1, 0, 2))

    middle_grad = cot_own + norm_back(second_grad, gain_two, z_two, factor_two)
    middle_all = jnp.concatenate(reorder(gather_rows(middle_grad.astype(BF))), axis=0)
    out_weight_grad = mm(heads_out, middle_all, ((0,), (0,)))
    heads_grad = (
        mm(middle_all, out_weight, ((1,), (1,))).astype(BF).reshape(images, SLOTS, heads, HD)
    )
    value_grad = jnp.einsum(
        "ihst,ishd->ithd", probs.astype(BF), heads_grad, preferred_element_type=F32
    )
    prob_grad = jnp.einsum("ishd,ithd->ihst", heads_grad, v, preferred_element_type=F32)
    delta = jnp.sum(probs * prob_grad, axis=-1, keepdims=True)
    score_grad = (probs * (prob_grad - delta) * HD ** (-0.5)).astype(BF)
    query_grad = jnp.einsum("ihst,ithd->ishd", score_grad, k, preferred_element_type=F32)
    key_grad = jnp.einsum("ihst,ishd->ithd", score_grad, q, preferred_element_type=F32)
    in_bias_grad = jnp.sum(jnp.stack([query_grad, value_grad], axis=3), axis=(0, 1)).reshape(-1)
    stacked = jnp.stack([query_grad, key_grad, value_grad], axis=3)
    stacked = stacked.reshape(images * SLOTS, heads * 3 * HD).astype(BF)
    first_grad = scatter_rows(
        reorder(split_rows(mm(stacked, in_weight, ((1,), (1,))), 4))
    )
    in_weight_grad = mm(normed_one, stacked, ((0,), (0,)))
    tokens_grad = middle_grad + norm_back(first_grad, gain_one, z_one, factor_one)

    small = jnp.stack(
        [
            jnp.sum(middle_grad, axis=0),
            jnp.sum(cot_own, axis=0),
            jnp.sum(first_grad * z_one, axis=0),
            jnp.sum(first_grad, axis=0),
            jnp.sum(second_grad * z_two, axis=0),
            jnp.sum(second_grad, axis=0),
        ]
    )
    small = pack(small)
    for bit in (1, 2):
        small = add_small(small, swap(small, "tensor", bit))
    shared = sum(unpack(small))
    own_small = jnp.stack([up_bias_grad, jnp.pad(in_bias_grad, (0, up_bias_grad.shape[0] - in_bias_grad.shape[0]))])
    small = pack(jnp.concatenate([shared, own_small], axis=0))
    mixed = jnp.concatenate(
        [
            in_weight_grad,
            jnp.concatenate(
                [out_weight_grad[:, i * 256 : (i + 1) * 256] for i in range(4)], axis=0
            ),
        ],
        axis=1,
    )
    half = mixed.shape[0] // 2
    first_half, small = sum_over_data(mixed[:half], (0, 1, 2), small)
    second_half, _ = sum_over_data(mixed[half:], (1, 0, 2))
    mixed = jnp.concatenate([first_half, second_half], axis=0)
    columns = in_weight.shape[1]
    small = sum(unpack(small))
    out_sum = jnp.concatenate(split_rows(mixed[:, columns:], 4), axis=1)
    return (
        output,
        tokens_grad,
        mixed[:, :columns],
        small[7, : in_bias.shape[0]],
        out_sum,
        small[0],
        up_sum,
        small[6],
        down_sum,
        small[1],
        small[2],
        small[3],
        small[4],
        small[5],
    )


def solution(mesh):
    rows = P(("dp", "tensor"), None)
    placed = (
        rows,
        P("dp", None),
        rows,
        P(None, "tensor"),
        P("tensor"),
        P("tensor", None),
        P(),
        P(None, "tensor"),
        P("tensor"),
        P("tensor", None),
        P(),
        P(),
        P(),
        P(),
        P(),
    )
    given = (
        rows,
        rows,
        P(None, "tensor"),
        P("tensor"),
        P("tensor", None),
        P(),
        P(None, "tensor"),
        P("tensor"),
        P("tensor", None),
        P(),
        P(),
        P(),
        P(),
        P(),
    )
    return jax.shard_map(on_device, mesh=mesh, in_specs=placed, out_specs=given, check_vma=False)
```

```python
import functools

import jax
import jax.numpy as jnp
from jax import lax
from jax.experimental import pallas as pl
from jax.experimental.pallas import tpu as pltpu
from jax.sharding import PartitionSpec as P

HD = 64
SLOTS = 320
HALF = SLOTS // 2
PIECES = 8
EPSILON = 1e-06
BF = jnp.bfloat16
F32 = jnp.float32
MIB = 1 << 20


def mm(left, right, dims=((1,), (0,))):
    return lax.dot_general(left, right, (dims, ((), ())), preferred_element_type=F32)


NT = ((1,), (1,))
TN = ((0,), (0,))


def swap(values, axis, bit):
    count = lax.axis_size(axis)
    return lax.ppermute(values, axis, [(i, i ^ bit) for i in range(count)])


def after(values, *earlier):
    return lax.optimization_barrier((values, *earlier))[0]


def shape(dims, kind=F32):
    return jax.ShapeDtypeStruct(dims, kind)


def whole(dims):
    return pl.BlockSpec(dims, lambda *_: (0,) * len(dims))


def held(dims, kind):
    rows = -(-dims[-2] // 16) * 16 if len(dims) > 1 else 16
    count = rows * (-(-dims[-1] // 128) * 128)
    for size in dims[:-2]:
        count *= size
    return count * jnp.dtype(kind).itemsize


def run(body, operands, outs, grid=(1,), ins=None, out_specs=None, scratch=(), flops=0, room=6):
    ins = ins or [whole(x.shape) for x in operands[1:]]
    out_specs = out_specs or [whole(x.shape) for x in outs]
    arrays = [*operands[1:], *outs]
    moved = sum(x.size * x.dtype.itemsize for x in arrays)
    limit = room * MIB
    for spec, x in zip([*ins, *out_specs], arrays, strict=True):
        limit += (1 if spec.block_shape == x.shape else 2) * held(spec.block_shape, x.dtype)
    for x in scratch:
        limit += held(x.shape, x.dtype)
    ins = [
        pl.BlockSpec(x.block_shape, x.index_map, pipeline_mode=pl.Buffered(1))
        if x.block_shape == y.shape
        else x
        for x, y in zip(ins, operands[1:], strict=True)
    ]
    return pl.pallas_call(
        body,
        out_shape=outs,
        grid_spec=pltpu.PrefetchScalarGridSpec(
            num_scalar_prefetch=1,
            grid=grid,
            in_specs=ins,
            out_specs=out_specs,
            scratch_shapes=scratch,
        ),
        compiler_params=pltpu.CompilerParams(vmem_limit_bytes=limit),
        cost_estimate=pl.CostEstimate(
            flops=int(flops), bytes_accessed=int(moved), transcendentals=0
        ),
    )(*operands)


def row_tiles(rows, size, step):
    def one(i, carry):
        step(pl.ds(pl.multiple_of(i * size, size), size))
        return carry

    lax.fori_loop(0, rows // size, one, 0)


def normalise(values):
    average = jnp.mean(values, axis=-1, keepdims=True)
    centred = values - average
    factor = lax.rsqrt(jnp.mean(centred * centred, axis=-1, keepdims=True) + EPSILON)
    return centred * factor, factor


def norm_back(grad, gain, z, factor):
    s = grad * gain
    return factor * (
        s - jnp.mean(s, axis=-1, keepdims=True) - z * jnp.mean(s * z, axis=-1, keepdims=True)
    )


def fold(values):
    return functools.reduce(
        lambda a, b: a + b, [values[i : i + 8] for i in range(0, values.shape[0], 8)]
    )


def project_side(blocks, gain, shift, weight, bias, normed, put):
    rows = blocks[0].shape[0]
    for i, block in enumerate(blocks):

        def step(at, block=block, i=i):
            z, _ = normalise(block[at, :].astype(F32))
            tile = pl.ds(pl.multiple_of(at.start + i * rows, 16), at.size)
            normed[tile, :] = (z * gain[...] + shift[...]).astype(BF)

        row_tiles(rows, 48, step)
        put(i, (mm(normed[i * rows : (i + 1) * rows, :], weight[...]) + bias[...]).astype(BF))


def project_local(me, tok_a, tok_b, gain, shift, weight, bias, normed, proj):
    rows = tok_a.shape[0]

    def put(i, values):
        proj[i * rows : (i + 1) * rows, :] = values

    project_side((tok_a, tok_b), gain, shift, weight, bias, normed, put)


def attend(side, qkv, keep, probs, heads_out):
    half_lane = lax.broadcasted_iota(jnp.int32, (1, 2 * HD), 1) // HD
    width = qkv.shape[1] // 3

    def one(j, carry):
        place = 3 * side + j
        image = place // 2
        queries = pl.ds(pl.multiple_of(place * HALF, 16), HALF)
        keys = pl.ds(pl.multiple_of(image * SLOTS, 16), SLOTS)
        live = keep[pl.ds(image, 1), :] > 0
        for pair in range(width // (2 * HD)):
            lanes = pl.ds(pair * 2 * HD, 2 * HD)
            q = qkv[queries, lanes] * 0.125
            k = qkv[keys, pl.ds(width + pair * 2 * HD, 2 * HD)]
            v = qkv[keys, pl.ds(2 * width + pair * 2 * HD, 2 * HD)]
            outs = []
            for e in range(2):
                scores = mm(jnp.where(half_lane == e, q, jnp.zeros_like(q)), k, NT)
                scores = jnp.where(live, scores, -1000000000.0)
                power = jnp.exp(scores - jnp.max(scores, axis=-1, keepdims=True))
                p = (power / jnp.sum(power, axis=-1, keepdims=True)).astype(BF)
                probs[j * 4 + pair * 2 + e] = p
                outs.append(mm(p, v))
            heads_out[pl.ds(pl.multiple_of(j * HALF, 16), HALF), lanes] = jnp.where(
                half_lane == 0, outs[0], outs[1]
            ).astype(BF)
        return carry

    lax.fori_loop(0, 3, one, 0)


def out_project(core, heads_out, weight, send, hold):
    rows = send.shape[0]
    send[...] = mm(
        heads_out[pl.ds(pl.multiple_of((1 - core) * rows, 16), rows), :], weight[...]
    ).astype(BF)
    hold[...] = mm(heads_out[pl.ds(pl.multiple_of(core * rows, 16), rows), :], weight[...])


def attend_far(
    me, near, tok_a, tok_b, gain, shift, weight, bias, keep, out_w,
    normed, qkv, probs, heads_out, send, hold,
):
    rows = tok_a.shape[0]
    core, far = me[0] & 1, me[0] >> 1
    for i in range(2):
        at = pl.multiple_of((2 * far + (core ^ i)) * rows, 16)
        qkv[pl.ds(at, rows), :] = near[i * rows : (i + 1) * rows, :]

    def put(i, values):
        at = pl.multiple_of((2 * (1 - far) + (core ^ i)) * rows, 16)
        qkv[pl.ds(at, rows), :] = values

    project_side((tok_a, tok_b), gain, shift, weight, bias, normed, put)
    attend(1 - far, qkv, keep, probs, heads_out)
    out_project(core, heads_out, out_w, send, hold)


def attend_near(me, qkv, keep, out_w, probs, heads_out, send, hold):
    core, far = me[0] & 1, me[0] >> 1
    attend(far, qkv, keep, probs, heads_out)
    out_project(core, heads_out, out_w, send, hold)


def second_norm(me, tok, hold, near, far, bias, gain, shift, middle, second):
    def step(at):
        total = hold[at, :] + near[at, :].astype(F32) + far[at, :].astype(F32)
        values = tok[at, :].astype(F32) + total + bias[...]
        middle[at, :] = values
        z, _ = normalise(values)
        second[at, :] = (z * gain[...] + shift[...]).astype(BF)

    row_tiles(tok.shape[0], 48, step)


def act_back(me, grad_a, grad_b, keep, down, cot, act_grad):
    rows = grad_a.shape[0]

    @pl.when(pl.program_id(0) == 0)
    def _():
        for i, block in enumerate((grad_a, grad_b)):
            at = pl.ds(i * rows, rows)
            cot[at, :] = (block[...].astype(F32) * keep[at, :]).astype(BF)

    act_grad[...] = mm(cot[...], down[...], NT)


def feed_forward(
    me, norm_a, norm_b, up, bias, act_grad, act, pre_low, bias_grad, send, hold, total, pre
):
    step = pl.program_id(0)
    rows = norm_a.shape[0]
    for i, block in enumerate((norm_a, norm_b)):
        pre[pl.ds(i * rows, rows), :] = mm(block[...], up[...])

    def one(i, sums):
        at = pl.ds(pl.multiple_of(i * 32, 32), 32)
        x = pre[at, :] + bias[...]
        share = 0.5 + 0.5 * lax.erf(x * 0.7071067811865476)
        slope = share + x * (0.3989422804014327 * jnp.exp(-0.5 * x * x))
        act[at, :] = (x * share).astype(BF)
        grad = act_grad[at, :] * slope
        pre_low[at, :] = grad.astype(BF)
        return sums + fold(grad)

    sums = lax.fori_loop(0, 2 * rows // 32, one, jnp.zeros((8, pre.shape[1]), F32))
    bias_grad[...] = jnp.sum(sums, axis=0, keepdims=True)
    part = mm(pre_low[...], up[...], NT)

    @pl.when(step == 0)
    def _():
        total[...] = part

    @pl.when(step > 0)
    def _():
        total[...] += part

    @pl.when(step == pl.num_programs(0) - 1)
    def _():
        hold[...] = total[:rows, :]
        send[...] = total[rows:, :].astype(BF)


def feed_out(me, act, down, send, hold):
    rows = send.shape[0]
    send[...] = mm(act[rows:, :], down[...]).astype(BF)
    hold[...] = mm(act[:rows, :], down[...])


def weight_piece(me, left_a, left_b, right_a, right_b, out):
    out[...] = (
        mm(left_a[...], right_a[...], TN) + mm(left_b[...], right_b[...], TN)
    ).astype(out.dtype)


def middle_back(
    me, hold, near, far, middle, grad, keep, gain, middle_grad, middle_low, sums, parts
):
    parts[...] = jnp.zeros_like(parts)

    def step(at):
        second = hold[at, :] + near[at, :].astype(F32) + far[at, :].astype(F32)
        z, factor = normalise(middle[at, :])
        cot = grad[at, :].astype(F32) * keep[at, :]
        total = cot + norm_back(second, gain[...], z, factor)
        middle_grad[at, :] = total
        middle_low[at, :] = total.astype(BF)
        parts[0] += fold(total)
        parts[1] += fold(cot)
        parts[2] += fold(second * z)
        parts[3] += fold(second)

    row_tiles(hold.shape[0], 48, step)
    for i in range(4):
        sums[i : i + 1, :] = jnp.sum(parts[i], axis=0, keepdims=True)


def attend_back(side, mid_blocks, core, qkv, probs, out_w, grads, pg_q, keys_grad):
    rows = mid_blocks[0].shape[0]
    half_lane = lax.broadcasted_iota(jnp.int32, (1, 2 * HD), 1) // HD
    width = qkv.shape[1] // 3
    for i, block in enumerate(mid_blocks):
        at = pl.multiple_of((core ^ i) * rows, 16)
        grads[pl.ds(at, rows), :] = mm(block[...], out_w[...], NT).astype(BF)

    def one(j, carry):
        place = 3 * side + j
        image = place // 2
        inside = pl.ds(pl.multiple_of(j * HALF, 16), HALF)
        queries = pl.ds(pl.multiple_of(place * HALF, 16), HALF)
        keys = pl.ds(pl.multiple_of(image * SLOTS, 16), SLOTS)
        for pair in range(width // (2 * HD)):
            lanes = pl.ds(pair * 2 * HD, 2 * HD)
            q = qkv[queries, lanes]
            k = qkv[keys, pl.ds(width + pair * 2 * HD, 2 * HD)]
            v = qkv[keys, pl.ds(2 * width + pair * 2 * HD, 2 * HD)]
            g = grads[inside, lanes]
            found = []
            for e in range(2):
                p = probs[j * 4 + pair * 2 + e]
                wide = p.astype(F32)
                prob_grad = mm(jnp.where(half_lane == e, g, jnp.zeros_like(g)), v, NT)
                delta = jnp.sum(wide * prob_grad, axis=-1, keepdims=True)
                score_grad = (wide * (prob_grad - delta) * 0.125).astype(BF)
                found.append(
                    (mm(score_grad, k), mm(score_grad, q, TN), mm(p, g, TN))
                )
            q_grad, k_grad, v_grad = (
                jnp.where(half_lane == 0, a, b) for a, b in zip(*found, strict=True)
            )
            pg_q[inside, lanes] = q_grad
            keys_grad[keys, lanes] += k_grad
            keys_grad[keys, pl.ds(width + pair * 2 * HD, 2 * HD)] += v_grad
        return carry

    lax.fori_loop(0, 3, one, 0)


def back_near(me, mid_a, mid_b, qkv, probs, out_w, pg_q, keys_grad, grads):
    core, far = me[0] & 1, me[0] >> 1
    keys_grad[...] = jnp.zeros_like(keys_grad)
    attend_back(far, (mid_a, mid_b), core, qkv, probs, out_w, grads, pg_q, keys_grad)


def back_far(
    me, mid_a, mid_b, qkv, probs, out_w, near_q, near_keys, in_w,
    proj_near, proj_far, flat_near, flat_far, bias_grad, send, hold, grads, far_q, keys_grad,
):
    core, far = me[0] & 1, me[0] >> 1
    rows = mid_a.shape[0]
    width = far_q.shape[1]
    keys_grad[...] = near_keys[...]
    attend_back(1 - far, (mid_a, mid_b), core, qkv, probs, out_w, grads, far_q, keys_grad)
    bias_grad[...] = jnp.concatenate(
        [
            jnp.sum(far_q[...], axis=0, keepdims=True) + jnp.sum(near_q[...], axis=0, keepdims=True),
            jnp.sum(keys_grad[:, width:], axis=0, keepdims=True),
        ],
        axis=1,
    )
    sides = ((proj_near, flat_near, near_q), (proj_far, flat_far, far_q))
    for side, (out, flat, q_part) in enumerate(sides):
        for i in range(2):
            inside = pl.multiple_of((core ^ i) * rows, 16)
            place = pl.multiple_of((2 * (far ^ side) + (core ^ i)) * rows, 16)
            to = pl.ds(i * rows, rows)
            out[to, :width] = q_part[pl.ds(inside, rows), :].astype(BF)
            out[to, width:] = keys_grad[pl.ds(place, rows), :].astype(BF)
        for head in range(width // HD):
            for kind in range(3):
                at = (head * 3 + kind) * HD
                flat[:, at : at + HD] = out[:, kind * width + head * HD :][:, :HD]
    send[...] = mm(proj_far[rows:, :], in_w[...], NT).astype(BF)
    hold[...] = mm(proj_far[:rows, :], in_w[...], NT)


def first_back(me, proj, in_w, send, hold):
    rows = send.shape[0]
    send[...] = mm(proj[rows:, :], in_w[...], NT).astype(BF)
    hold[...] = mm(proj[:rows, :], in_w[...], NT)


def mixed_piece(me, norm_a, norm_b, proj_a, proj_b, heads_a, heads_b, mid_a, mid_b, out):
    width = proj_a.shape[1]
    out[:, :width] = (
        mm(norm_a[...], proj_a[...], TN) + mm(norm_b[...], proj_b[...], TN)
    ).astype(out.dtype)
    both = mm(heads_a[...], mid_a[...], TN) + mm(heads_b[...], mid_b[...], TN)
    half = both.shape[0] // 2
    out[:, width : width + half] = both[:half].astype(out.dtype)
    out[:, width + half :] = both[half:].astype(out.dtype)


def token_back(me, hold, near, far, tok, middle_grad, gain, tokens_grad, sums, parts):
    parts[...] = jnp.zeros_like(parts)

    def step(at):
        first = hold[at, :] + near[at, :].astype(F32) + far[at, :].astype(F32)
        z, factor = normalise(tok[at, :].astype(F32))
        tokens_grad[at, :] = middle_grad[at, :] + norm_back(first, gain[...], z, factor)
        parts[0] += fold(first * z)
        parts[1] += fold(first)

    row_tiles(hold.shape[0], 48, step)
    for i in range(2):
        sums[i : i + 1, :] = jnp.sum(parts[i], axis=0, keepdims=True)


def place_pieces(me, gathered, out):
    out[...] = gathered[...].astype(F32)


def place_mixed(me, first, second, in_out, out_out):
    in_out[:, : first.shape[1]] = first[...].astype(F32)
    rest = in_out.shape[1] - first.shape[1]
    in_out[:, first.shape[1] :] = second[:, :rest].astype(F32)
    half = out_out.shape[0] // 2
    out_out[:half, :] = second[:, rest : rest + half].astype(F32)
    out_out[half:, :] = second[:, rest + half :].astype(F32)


def piece_of(position, order, me):
    relative = 0
    for step, bit in enumerate(order):
        relative = relative | (((position >> (len(order) - 1 - step)) & 1) << bit)
    return relative ^ (me & (PIECES - 1))


def position_of(piece, order, me):
    relative = piece ^ (me & (PIECES - 1))
    place = 0
    for step, bit in enumerate(order):
        place = place | (((relative >> bit) & 1) << (len(order) - 1 - step))
    return place


def pack(values):
    high = values.astype(BF)
    return jnp.concatenate([high, (values - high.astype(F32)).astype(BF)], axis=0)


def unpack(packed):
    half = packed.shape[0] // 2
    return packed[:half].astype(F32) + packed[half:].astype(F32)


class Reduction:
    def __init__(self, send, order):
        self.send, self.order = send, order
        self.count = lax.axis_size("dp").bit_length() - 1
        self.bits = [*order, *range(len(order), self.count), *reversed(order)]
        self.values, self.small, self.came, self.at = None, None, None, 0

    def take(self, *earlier):
        self.came = swap(self.send, "dp", 1 << self.bits[self.at])
        if earlier:
            self.came = after(self.came, *earlier)
        return self.came

    def arrive(self, *earlier):
        if self.came is None:
            self.take()
        arrived = after(self.came, *earlier)
        self.came = None
        self.at += 1
        halving = len(self.order)
        if self.at < halving:
            middle = self.values.shape[0] // 2
            self.send = (self.values[middle:] + arrived[middle:].astype(F32)).astype(BF)
            self.values = self.values[:middle] + arrived[:middle].astype(F32)
        elif self.at == halving:
            self.values = (self.values + arrived.astype(F32)).astype(BF)
            self.send = self.values
        elif self.at <= self.count:
            self.values = (self.values.astype(F32) + arrived.astype(F32)).astype(BF)
            self.send = self.values
        else:
            rows = self.values.shape[0]
            if self.small is not None:
                self.small = pack(unpack(self.small) + unpack(arrived[rows:]))
            self.values = jnp.concatenate([self.values, arrived[:rows]], axis=0)
            self.send = self.values
            if self.small is not None and self.at < len(self.bits):
                self.send = jnp.concatenate([self.values, self.small], axis=0)
        return self.values

    def join(self, small):
        for bit in range(len(self.order), self.count):
            small = pack(unpack(small) + unpack(swap(small, "dp", 1 << bit)))
        self.small = small
        self.send = jnp.concatenate([self.values, small], axis=0)


ORDER_A = (0, 1, 2)
ORDER_B = (1, 0, 2)


def weight_grad(me, lefts, rights, order, kept):
    rows, columns = lefts[0].shape[0], lefts[0].shape[1]
    wide = rights[0].shape[1]
    piece = columns // PIECES
    half = PIECES // 2
    base = 0 if kept else half

    def index(i, scalars):
        return (0, piece_of(base + i, order, scalars[1]))

    return run(
        weight_piece,
        (me, *lefts, *rights),
        [shape((piece * half, wide), F32 if kept else BF)],
        grid=(half,),
        ins=[pl.BlockSpec((rows, piece), index)] * 2 + [whole(x.shape) for x in rights],
        out_specs=[pl.BlockSpec((piece, wide), lambda i, s: (i, 0))],
        flops=2 * 2 * rows * columns * wide // 2,
    )[0]


def mixed_grad(me, normed, proj, heads, mids, order, kept):
    rows, columns = normed[0].shape
    piece = columns // PIECES
    half = PIECES // 2
    base = 0 if kept else half
    wide = proj[0].shape[1] + heads[0].shape[1]

    def index(i, scalars):
        return (0, piece_of(base + i, order, scalars[1]))

    return run(
        mixed_piece,
        (me, *normed, *proj, *heads, *mids),
        [shape((piece * half, wide), F32 if kept else BF)],
        grid=(half,),
        ins=[pl.BlockSpec((rows, piece), index)] * 2
        + [whole(x.shape) for x in (*proj, *heads)]
        + [pl.BlockSpec((rows, piece), index)] * 2,
        out_specs=[pl.BlockSpec((piece, wide), lambda i, s: (i, 0))],
        flops=2 * 2 * rows * columns * wide // 2,
    )[0]


def place(me, gathered, order):
    piece = gathered.shape[0] // PIECES
    wide = gathered.shape[1]
    return run(
        place_pieces,
        (me, gathered),
        [shape(gathered.shape)],
        grid=(PIECES,),
        ins=[pl.BlockSpec((piece, wide), lambda i, s: (position_of(i, order, s[1]), 0))],
        out_specs=[pl.BlockSpec((piece, wide), lambda i, s: (i, 0))],
    )[0]


def on_device(
    tokens,
    keep_mask,
    grad_out,
    in_weight,
    in_bias,
    out_weight,
    out_bias,
    up_weight,
    up_bias,
    down_weight,
    down_bias,
    gain_one,
    shift_one,
    gain_two,
    shift_two,
):
    rows, model = tokens.shape
    me = jnp.stack([lax.axis_index("tensor"), lax.axis_index("dp")]).astype(jnp.int32)
    images = keep_mask.shape[0]
    heads = in_weight.shape[1] // (3 * HD)
    width = heads * HD
    hidden = up_weight.shape[1]

    def line(values):
        return values.reshape(1, -1)

    side = 2 * rows
    block = 256
    steps = hidden // block
    project_flops = 2 * side * model * 3 * width
    attend_flops = 3 * heads * 4 * HALF * SLOTS * 128 + 2 * side * width * model
    back_flops = 3 * heads * 10 * HALF * SLOTS * 128 + 2 * side * width * model

    def act_grad_of(one, other, keep):
        return run(
            act_back,
            (me, one, other, keep, down_weight),
            [shape((side, model), BF), shape((side, hidden))],
            grid=(steps,),
            ins=[
                whole(one.shape),
                whole(one.shape),
                whole(keep.shape),
                pl.BlockSpec((block, model), lambda i, s: (i, 0)),
            ],
            out_specs=[whole((side, model)), pl.BlockSpec((side, block), lambda i, s: (0, i))],
            flops=2 * side * model * hidden,
        )

    def feed(one, other, act_grad):
        column = pl.BlockSpec((side, block), lambda i, s: (0, i))
        single = pl.BlockSpec((1, block), lambda i, s: (0, i))
        return run(
            feed_forward,
            (me, one, other, up_weight, line(up_bias), act_grad),
            [
                shape((side, hidden), BF),
                shape((side, hidden), BF),
                shape((1, hidden)),
                shape((rows, model), BF),
                shape((rows, model)),
            ],
            grid=(steps,),
            ins=[
                whole(one.shape),
                whole(one.shape),
                pl.BlockSpec((model, block), lambda i, s: (0, i)),
                single,
                column,
            ],
            out_specs=[
                column,
                column,
                single,
                whole((rows, model)),
                whole((rows, model)),
            ],
            scratch=[pltpu.VMEM((side, model), F32), pltpu.VMEM((side, block), F32)],
            flops=4 * side * model * hidden,
        )

    def feed_back(act):
        return run(
            feed_out,
            (me, act, down_weight),
            [shape((rows, model), BF), shape((rows, model))],
            flops=2 * side * model * hidden,
        )

    tok_far = swap(tokens, "tensor", 2)
    tok_core = swap(tokens, "tensor", 1)
    grad_core = swap(grad_out, "tensor", 1)
    keep_flat = keep_mask.reshape(-1).astype(F32)
    keeps = [
        lax.dynamic_slice_in_dim(keep_flat, (me[0] ^ i) * rows, rows) for i in range(4)
    ]
    keep_near = jnp.concatenate(keeps[:2])[:, None]
    keep_far = jnp.concatenate(keeps[2:])[:, None]
    in_grouped = in_weight.reshape(model, heads, 3, HD).transpose(0, 2, 1, 3)
    in_grouped = in_grouped.reshape(model, 3 * width)
    pair = in_bias.reshape(heads, 2, HD).transpose(1, 0, 2).reshape(2, width)
    bias_full = jnp.concatenate([pair[:1], jnp.zeros((1, width), F32), pair[1:]], axis=1)
    norm_near, proj_near = run(
        project_local,
        (me, tokens, tok_core, line(gain_one), line(shift_one), in_grouped, bias_full),
        [shape((side, model), BF), shape((side, 3 * width), BF)],
        flops=project_flops,
    )
    tok_far = after(tok_far, proj_near, keep_near, keep_far)

    tok_both = swap(tok_far, "tensor", 1)
    grad_far = swap(after(grad_out, tok_far), "tensor", 2)
    attend_outs = [
        shape((3 * heads, HALF, SLOTS), BF),
        shape((side, width), BF),
        shape((rows, model), BF),
        shape((rows, model), F32),
    ]
    norm_far, qkv, probs_far, heads_far, send, far_hold = run(
        attend_far,
        (
            me, proj_near, tok_far, tok_both, line(gain_one), line(shift_one), in_grouped,
            bias_full, keep_mask, out_weight,
        ),
        [shape((side, model), BF), shape((2 * side, 3 * width), BF), *attend_outs],
        flops=project_flops + attend_flops,
    )
    arrived = after(swap(send, "tensor", 1), grad_far)
    far_sum = (far_hold + arrived.astype(F32)).astype(BF)
    grad_far = after(grad_far, far_sum)
    grad_both = swap(grad_far, "tensor", 1)
    arrived_far = swap(far_sum, "tensor", 2)
    probs_near, heads_near, send, hold = run(
        attend_near,
        (me, after(qkv, far_sum), keep_mask, out_weight),
        attend_outs,
        flops=attend_flops,
    )
    cot_near, act_grad_near = act_grad_of(after(grad_out, hold), grad_core, keep_near)
    arrived_near = after(swap(send, "tensor", 1), arrived_far)
    middle, second = run(
        second_norm,
        (
            me, tokens, after(hold, cot_near), arrived_near, arrived_far, line(out_bias),
            line(gain_two), line(shift_two),
        ),
        [shape((rows, model)), shape((rows, model), BF)],
    )

    second_far = swap(second, "tensor", 2)
    second_core = swap(second, "tensor", 1)
    act_near, pre_near, up_bias_near, near_send, near_hold = feed(
        second, second_core, act_grad_near
    )
    cot_far, act_grad_far = act_grad_of(after(grad_far, near_hold), grad_both, keep_far)
    second_far = after(second_far, cot_far)
    second_both = swap(second_far, "tensor", 1)
    act_far, pre_far, up_bias_far, far_send, far_hold = feed(
        second_far, second_both, act_grad_far
    )
    far_sum = (far_hold + swap(far_send, "tensor", 1).astype(F32)).astype(BF)
    arrived_far = swap(far_sum, "tensor", 2)
    arrived_near = swap(near_send, "tensor", 1)
    acts, cots = (act_near, act_far), (after(cot_near, far_sum), cot_far)
    down_send = weight_grad(me, acts, cots, ORDER_A, False)
    down = Reduction(down_send, ORDER_A)
    seconds, pres = ((second, second_core), (second_far, second_both)), (pre_near, pre_far)
    seconds = tuple(jnp.concatenate(x, axis=0) for x in seconds)
    pres = (after(pre_near, down_send), pre_far)
    up_send = weight_grad(me, seconds, pres, ORDER_B, False)
    up = Reduction(up_send, ORDER_B)
    feed_send, feed_hold = feed_back(after(act_far, up_send))
    feed_far = (feed_hold + swap(feed_send, "tensor", 1).astype(F32)).astype(BF)
    middle_grad, middle_low, middle_sums = run(
        middle_back,
        (
            me, after(near_hold, feed_hold), arrived_near, arrived_far, middle, grad_out,
            keep_near[:rows], line(gain_two),
        ),
        [shape((rows, model)), shape((rows, model), BF), shape((4, model))],
        scratch=[pltpu.VMEM((4, 8, model), F32)],
    )

    mid_far = swap(middle_low, "tensor", 2)
    mid_core = swap(middle_low, "tensor", 1)
    grads = pltpu.VMEM((side, width), BF)
    down.values = weight_grad(me, (after(act_near, middle_low), act_far), cots, ORDER_A, True)
    near_q, near_keys = run(
        back_near,
        (me, after(middle_low, down.values), mid_core, qkv, probs_near, out_weight),
        [shape((side, width)), shape((2 * side, 2 * width))],
        scratch=[grads],
        flops=back_flops,
    )
    up.values = weight_grad(me, seconds, (after(pre_near, near_q), pre_far), ORDER_B, True)
    mid_far = after(mid_far, up.values)
    mid_both = swap(mid_far, "tensor", 1)
    feed_far = swap(after(feed_far, mid_far), "tensor", 2)
    down.arrive(mid_far)
    up.arrive(mid_far)
    proj_near, proj_far, flat_near, flat_far, bias_grad, far_send, far_hold = run(
        back_far,
        (
            me, mid_far, mid_both, after(qkv, down.send, up.send), probs_far, out_weight, near_q,
            near_keys, in_grouped,
        ),
        [
            shape((side, 3 * width), BF),
            shape((side, 3 * width), BF),
            shape((side, 3 * width), BF),
            shape((side, 3 * width), BF),
            shape((1, 2 * width)),
            shape((rows, model), BF),
            shape((rows, model)),
        ],
        scratch=[
            grads,
            pltpu.VMEM((side, width), F32),
            pltpu.VMEM((2 * side, 2 * width), F32),
        ],
        flops=back_flops + project_flops,
    )
    down.take(bias_grad)
    up.take(bias_grad)
    arrived = after(swap(far_send, "tensor", 1), feed_far, down.came, up.came)
    far_sum = (far_hold + arrived.astype(F32)).astype(BF)
    arrived_far = swap(far_sum, "tensor", 2)

    def mix_heads(values):
        core = (me[0] & 1) > 0
        return jnp.where(core, jnp.concatenate([values[rows:], values[:rows]], axis=0), values)

    down.arrive(far_sum)
    up.arrive(far_sum)
    normed = (after(norm_near, down.send, up.send), norm_far)
    split = (3 * width + width) // 2
    first_proj = tuple(x[:, :split] for x in (flat_near, flat_far))
    second_proj = tuple(x[:, split:] for x in (flat_near, flat_far))
    head_rows = (mix_heads(heads_near), mix_heads(heads_far))
    mids = (
        jnp.concatenate([middle_low, mid_core], axis=0),
        jnp.concatenate([mid_far, mid_both], axis=0),
    )
    first_send = weight_grad(me, normed, first_proj, ORDER_A, False)
    first = Reduction(first_send, ORDER_A)
    second_proj = (after(second_proj[0], first_send), second_proj[1])
    mixed_send = mixed_grad(me, normed, second_proj, head_rows, mids, ORDER_A, False)
    mixed = Reduction(mixed_send, ORDER_A)
    down.take(mixed_send)
    up.take(mixed_send)
    near_send, hold = run(
        first_back,
        (me, after(proj_near, mixed_send), in_grouped),
        [shape((rows, model), BF), shape((rows, model))],
        flops=project_flops,
    )
    arrived_near = swap(near_send, "tensor", 1)
    normed = (after(norm_near, hold), norm_far)
    first.values = weight_grad(me, normed, first_proj, ORDER_A, True)
    normed = (after(norm_near, first.values), norm_far)
    mixed.values = mixed_grad(me, normed, second_proj, head_rows, mids, ORDER_A, True)
    down.arrive(mixed.values)
    up.arrive(mixed.values)
    first.arrive(down.values)
    mixed.arrive(up.values)
    tokens_grad, token_sums = run(
        token_back,
        (
            me, after(hold, first.send, mixed.send), arrived_near, arrived_far, tokens,
            middle_grad, line(gain_one),
        ),
        [shape((rows, model)), shape((2, model))],
        scratch=[pltpu.VMEM((2, 8, model), F32)],
    )
    feed_send, feed_hold = feed_back(after(act_near, token_sums))
    feed_rows = feed_hold + swap(feed_send, "tensor", 1).astype(F32) + feed_far.astype(F32)
    output = (keep_near[:rows] * (middle + feed_rows + down_bias)).astype(BF)

    shared = pack(jnp.concatenate([middle_sums, token_sums], axis=0))
    for bit in (1, 2):
        shared = pack(unpack(shared) + unpack(swap(shared, "tensor", bit)))
    own = jnp.concatenate(
        [up_bias_near + up_bias_far, jnp.pad(bias_grad, ((0, 0), (0, hidden - 2 * width)))], axis=0
    )
    small = jnp.concatenate([unpack(shared), own], axis=0)
    small = pack(jnp.concatenate([small[:, :split], small[:, split:]], axis=0))
    first.arrive(output)
    mixed.arrive(output)
    down.arrive(first.send)
    up.arrive(mixed.send)
    first.arrive(down.send)
    mixed.arrive(up.send)
    while first.at < first.count:
        first.arrive()
    first.join(small)
    first.arrive(mixed.send)
    mixed.arrive(first.send)
    down.arrive(first.send)
    up.arrive(mixed.send)
    while first.at < len(first.bits):
        first.arrive()
        mixed.arrive()
    while down.at < len(down.bits):
        down.arrive()
        up.arrive()
    small = unpack(first.small)
    small = jnp.concatenate([small[:8], small[8:]], axis=1)
    piece = model // PIECES
    down_sum = place(me, down.values, ORDER_A)
    up_sum = place(me, up.values, ORDER_B)
    in_sum, out_sum = run(
        place_mixed,
        (me, first.values, mixed.values),
        [shape((model, 3 * width)), shape((width, model))],
        grid=(PIECES,),
        ins=[
            pl.BlockSpec((piece, split), lambda i, s: (position_of(i, ORDER_A, s[1]), 0)),
            pl.BlockSpec((piece, split), lambda i, s: (position_of(i, ORDER_A, s[1]), 0)),
        ],
        out_specs=[
            pl.BlockSpec((piece, 3 * width), lambda i, s: (i, 0)),
            pl.BlockSpec((width, piece), lambda i, s: (0, i)),
        ],
    )
    in_bias_sum = small[7, : 2 * width].reshape(2, heads, HD).transpose(1, 0, 2).reshape(-1)
    return (
        output,
        tokens_grad,
        in_sum,
        in_bias_sum,
        out_sum,
        small[0],
        up_sum,
        small[6],
        down_sum,
        small[1],
        small[4],
        small[5],
        small[2],
        small[3],
    )


def solution(mesh):
    rows = P(("dp", "tensor"), None)
    placed = (
        rows,
        P("dp", None),
        rows,
        P(None, "tensor"),
        P("tensor"),
        P("tensor", None),
        P(),
        P(None, "tensor"),
        P("tensor"),
        P("tensor", None),
        P(),
        P(),
        P(),
        P(),
        P(),
    )
    given = (
        rows,
        rows,
        P(None, "tensor"),
        P("tensor"),
        P("tensor", None),
        P(),
        P(None, "tensor"),
        P("tensor"),
        P("tensor", None),
        P(),
        P(),
        P(),
        P(),
        P(),
    )
    return jax.shard_map(on_device, mesh=mesh, in_specs=placed, out_specs=given, check_vma=False)
```

```python
import functools

import jax
import jax.numpy as jnp
from jax import lax
from jax.experimental import pallas as pl
from jax.experimental.pallas import tpu as pltpu
from jax.sharding import PartitionSpec as P

HD = 64
SLOTS = 320
HALF = SLOTS // 2
PIECES = 8
EPSILON = 1e-06
BF = jnp.bfloat16
F32 = jnp.float32
MIB = 1 << 20


def mm(left, right, dims=((1,), (0,))):
    return lax.dot_general(left, right, (dims, ((), ())), preferred_element_type=F32)


NT = ((1,), (1,))
TN = ((0,), (0,))


def swap(values, axis, bit):
    count = lax.axis_size(axis)
    return lax.ppermute(values, axis, [(i, i ^ bit) for i in range(count)])


def after(values, *earlier):
    return lax.optimization_barrier((values, *earlier))[0]


def shape(dims, kind=F32):
    return jax.ShapeDtypeStruct(dims, kind)


STAY = []


def stay(*arrays):
    STAY.extend(arrays)


def leave(*arrays):
    for array in arrays:
        STAY[:] = [x for x in STAY if x is not array]


def run(body, operands, outs, scratch=(), flops=0, room=12):
    used = list(operands[1:])
    waiting = [x for x in STAY if all(x is not y for y in used)]
    ins = [pltpu.with_memory_space_constraint(x, pltpu.VMEM) for x in [*used, *waiting]]
    moved = sum(x.size * x.dtype.itemsize for x in [*used, *outs])

    def kernel(*refs):
        own = 1 + len(used)
        body(*refs[:own], *refs[own + len(waiting) :])

    return pl.pallas_call(
        kernel,
        out_shape=[pltpu.VMEM(x.shape, x.dtype) for x in outs],
        in_specs=[pl.BlockSpec(memory_space=pltpu.SMEM)]
        + [pl.BlockSpec(memory_space=pltpu.VMEM)] * len(ins),
        out_specs=[pl.BlockSpec(memory_space=pltpu.VMEM)] * len(outs),
        scratch_shapes=scratch,
        compiler_params=pltpu.CompilerParams(vmem_limit_bytes=room * MIB),
        cost_estimate=pl.CostEstimate(
            flops=int(flops * WEIGHT), bytes_accessed=0, transcendentals=0
        ),
    )(operands[0], *ins)


WEIGHT = 20


def add_low(me, left, right, out):
    out[...] = (left[...] + right[...].astype(F32)).astype(BF)


def add_round(left, right):
    return run(add_low, (jnp.zeros((1,), jnp.int32), left, right), [shape(left.shape, BF)])[0]


def add_halves(me, left, right, send, hold):
    middle = send.shape[0]
    send[...] = (left[middle:, :] + right[middle:, :].astype(F32)).astype(BF)
    hold[...] = left[:middle, :] + right[:middle, :].astype(F32)


def run_out(body, operands, outs, scratch=(), room=16):
    ins = [pltpu.with_memory_space_constraint(x, pltpu.VMEM) for x in operands[1:]]
    return pl.pallas_call(
        body,
        out_shape=[pltpu.HBM(x.shape, x.dtype) for x in outs],
        in_specs=[pl.BlockSpec(memory_space=pltpu.SMEM)]
        + [pl.BlockSpec(memory_space=pltpu.VMEM)] * len(ins),
        out_specs=[pl.BlockSpec(memory_space=pltpu.HBM)] * len(outs),
        scratch_shapes=scratch,
        compiler_params=pltpu.CompilerParams(vmem_limit_bytes=room * MIB),
        cost_estimate=pl.CostEstimate(
            flops=0, bytes_accessed=0, transcendentals=0
        ),
    )(operands[0], *ins)


def blocks(count, size, step):
    def one(i, carry):
        step(pl.ds(pl.multiple_of(i * size, size), size), i)
        return carry

    lax.fori_loop(0, count, one, 0)


def row_tiles(rows, size, step):
    def one(i, carry):
        step(pl.ds(pl.multiple_of(i * size, size), size))
        return carry

    lax.fori_loop(0, rows // size, one, 0)


def normalise(values):
    average = jnp.mean(values, axis=-1, keepdims=True)
    centred = values - average
    factor = lax.rsqrt(jnp.mean(centred * centred, axis=-1, keepdims=True) + EPSILON)
    return centred * factor, factor


def norm_back(grad, gain, z, factor):
    s = grad * gain
    return factor * (
        s - jnp.mean(s, axis=-1, keepdims=True) - z * jnp.mean(s * z, axis=-1, keepdims=True)
    )


def fold(values):
    return functools.reduce(
        lambda a, b: a + b, [values[i : i + 8] for i in range(0, values.shape[0], 8)]
    )


GAIN_ONE, SHIFT_ONE, OUT_BIAS, GAIN_TWO, SHIFT_TWO, UP_BIAS, DOWN_BIAS = range(7)


def row(vectors, number):
    return vectors[number : number + 1, :]


def project_side(blocks, vectors, weight, bias, normed, put):
    rows = blocks[0].shape[0]
    for i, block in enumerate(blocks):

        def step(at, block=block, i=i):
            z, _ = normalise(block[at, :].astype(F32))
            tile = pl.ds(pl.multiple_of(at.start + i * rows, 16), at.size)
            normed[tile, :] = (z * row(vectors, GAIN_ONE) + row(vectors, SHIFT_ONE)).astype(BF)

        row_tiles(rows, 48, step)
        put(i, (mm(normed[i * rows : (i + 1) * rows, :], weight[...]) + bias[...]).astype(BF))


def project_local(me, tok_a, tok_b, vectors, weight, bias, normed, proj):
    rows = tok_a.shape[0]

    def put(i, values):
        proj[i * rows : (i + 1) * rows, :] = values

    project_side((tok_a, tok_b), vectors, weight, bias, normed, put)


def attend(side, qkv, keep, probs, heads_out):
    half_lane = lax.broadcasted_iota(jnp.int32, (1, 2 * HD), 1) // HD
    width = qkv.shape[1] // 3

    def one(j, carry):
        place = 3 * side + j
        image = place // 2
        queries = pl.ds(pl.multiple_of(place * HALF, 16), HALF)
        keys = pl.ds(pl.multiple_of(image * SLOTS, 16), SLOTS)
        live = keep[pl.ds(image, 1), :] > 0
        for pair in range(width // (2 * HD)):
            lanes = pl.ds(pair * 2 * HD, 2 * HD)
            q = qkv[queries, lanes] * 0.125
            k = qkv[keys, pl.ds(width + pair * 2 * HD, 2 * HD)]
            v = qkv[keys, pl.ds(2 * width + pair * 2 * HD, 2 * HD)]
            outs = []
            for e in range(2):
                scores = mm(jnp.where(half_lane == e, q, jnp.zeros_like(q)), k, NT)
                scores = jnp.where(live, scores, -1000000000.0)
                power = jnp.exp(scores - jnp.max(scores, axis=-1, keepdims=True))
                p = (power / jnp.sum(power, axis=-1, keepdims=True)).astype(BF)
                probs[j * 4 + pair * 2 + e] = p
                outs.append(mm(p, v))
            heads_out[pl.ds(pl.multiple_of(j * HALF, 16), HALF), lanes] = jnp.where(
                half_lane == 0, outs[0], outs[1]
            ).astype(BF)
        return carry

    lax.fori_loop(0, 3, one, 0)


def out_project(core, heads_out, weight, send, hold):
    rows = send.shape[0]
    send[...] = mm(
        heads_out[pl.ds(pl.multiple_of((1 - core) * rows, 16), rows), :], weight[...]
    ).astype(BF)
    hold[...] = mm(heads_out[pl.ds(pl.multiple_of(core * rows, 16), rows), :], weight[...])


def attend_far(
    me, near, tok_a, tok_b, vectors, weight, bias, keep, out_w,
    normed, qkv, probs, heads_out, send, hold,
):
    rows = tok_a.shape[0]
    core, far = me[0] & 1, me[0] >> 1
    for i in range(2):
        at = pl.multiple_of((2 * far + (core ^ i)) * rows, 16)
        qkv[pl.ds(at, rows), :] = near[i * rows : (i + 1) * rows, :]

    def put(i, values):
        at = pl.multiple_of((2 * (1 - far) + (core ^ i)) * rows, 16)
        qkv[pl.ds(at, rows), :] = values

    project_side((tok_a, tok_b), vectors, weight, bias, normed, put)
    attend(1 - far, qkv, keep, probs, heads_out)
    out_project(core, heads_out, out_w, send, hold)


def attend_near(me, qkv, keep, out_w, probs, heads_out, send, hold):
    core, far = me[0] & 1, me[0] >> 1
    attend(far, qkv, keep, probs, heads_out)
    out_project(core, heads_out, out_w, send, hold)


def second_norm(me, tok, hold, near, far, vectors, middle, second):
    def step(at):
        total = hold[at, :] + near[at, :].astype(F32) + far[at, :].astype(F32)
        values = tok[at, :].astype(F32) + total + row(vectors, OUT_BIAS)
        middle[at, :] = values
        z, _ = normalise(values)
        second[at, :] = (z * row(vectors, GAIN_TWO) + row(vectors, SHIFT_TWO)).astype(BF)

    row_tiles(tok.shape[0], 48, step)


def act_back(me, cot_a, cot_b, down, act_grad):
    rows = cot_a.shape[0]

    def step(at, i):
        act_grad[:rows, at] = mm(cot_a[...], down[at, :], NT)
        act_grad[rows:, at] = mm(cot_b[...], down[at, :], NT)

    blocks(down.shape[0] // 256, 256, step)


def feed_forward(
    me, norm_a, norm_b, up, vectors, act_grad, act, pre_low, bias_grad, send, hold, total, pre
):
    rows = norm_a.shape[0]

    def step(at, number):
        for i, block in enumerate((norm_a, norm_b)):
            pre[pl.ds(i * rows, rows), :] = mm(block[...], up[:, at])
        own_bias = vectors[UP_BIAS : UP_BIAS + 1, at]

        def one(i, sums):
            tile = pl.ds(pl.multiple_of(i * 32, 32), 32)
            x = pre[tile, :] + own_bias
            share = 0.5 + 0.5 * lax.erf(x * 0.7071067811865476)
            slope = share + x * (0.3989422804014327 * jnp.exp(-0.5 * x * x))
            act[tile, at] = (x * share).astype(BF)
            grad = act_grad[tile, at] * slope
            pre_low[tile, at] = grad.astype(BF)
            return sums + fold(grad)

        sums = lax.fori_loop(0, 2 * rows // 32, one, jnp.zeros((8, pre.shape[1]), F32))
        bias_grad[:, at] = jnp.sum(sums, axis=0, keepdims=True)
        part = mm(pre_low[:, at], up[:, at], NT)

        @pl.when(number == 0)
        def _():
            total[...] = part

        @pl.when(number > 0)
        def _():
            total[...] += part

    blocks(up.shape[1] // 256, 256, step)
    hold[...] = total[:rows, :]
    send[...] = total[rows:, :].astype(BF)


def feed_out(me, act, down, send, hold):
    rows = send.shape[0]
    send[...] = mm(act[rows:, :], down[...]).astype(BF)
    hold[...] = mm(act[:rows, :], down[...])


def gather_pieces(me, lefts, order, base, turned):
    piece = lefts[0].shape[1] // PIECES
    for i in range(PIECES // 2):
        at = pl.ds(pl.multiple_of(piece_of(base + i, order, me[1]) * piece, piece), piece)
        for left, to in zip(lefts, turned, strict=True):
            to[i * piece : (i + 1) * piece, :] = left[:, at].T


def weight_pieces(order, base, low, count, me, *refs):
    lefts, rights = refs[: count[0]], refs[count[0] : sum(count)]
    out, turned = refs[sum(count)], refs[sum(count) + 1 :]
    gather_pieces(me, lefts, order, base, turned)
    rows = min(lefts[0].shape[0], rights[0].shape[0])
    left_each, right_each = lefts[0].shape[0] // rows, rights[0].shape[0] // rows

    def step(at, i):
        found = None
        from_ = pl.ds(pl.multiple_of(at.start + low, 128), at.size)
        for k in range(max(count)):
            left, right = turned[k // left_each], rights[k // right_each]
            inner = (k % left_each) * rows
            part = mm(
                left[:, inner : inner + rows], right[pl.ds((k % right_each) * rows, rows), from_]
            )
            found = part if found is None else found + part
        out[:, at] = found.astype(out.dtype)

    blocks(out.shape[1] // 256, 256, step)


def mixed_pieces(order, base, low, me, *refs):
    lefts, rights, heads, mids, out = refs[:2], refs[2:4], refs[4:6], refs[6:10], refs[10]
    turned = refs[11:13]
    gather_pieces(me, lefts, order, base, turned)
    width = rights[0].shape[1] - low
    for at in range(0, width, 256):
        found = mm(turned[0][...], rights[0][:, low + at : low + at + 256])
        found = found + mm(turned[1][...], rights[1][:, low + at : low + at + 256])
        out[:, at : at + 256] = found.astype(out.dtype)
    core = me[0] & 1
    rows = mids[0].shape[0]
    piece = mids[0].shape[1] // PIECES
    half = heads[0].shape[1] // 2
    for i in range(PIECES // 2):
        at = pl.ds(pl.multiple_of(piece_of(base + i, order, me[1]) * piece, piece), piece)
        both = None
        for k in range(4):
            inside = pl.ds(pl.multiple_of((core ^ (k % 2)) * rows, 16), rows)
            part = mm(heads[k // 2][inside, :], mids[k][:, at], TN)
            both = part if both is None else both + part
        to = pl.ds(i * piece, piece)
        out[to, width : width + half] = both[:half].astype(out.dtype)
        out[to, width + half :] = both[half:].astype(out.dtype)


def middle_back(me, hold, near, far, middle, cot_low, vectors, middle_grad, middle_low, sums, parts):
    parts[...] = jnp.zeros_like(parts)

    def step(at):
        second = hold[at, :] + near[at, :].astype(F32) + far[at, :].astype(F32)
        z, factor = normalise(middle[at, :])
        cot = cot_low[at, :].astype(F32)
        total = cot + norm_back(second, row(vectors, GAIN_TWO), z, factor)
        middle_grad[at, :] = total
        middle_low[at, :] = total.astype(BF)
        parts[0] += fold(total)
        parts[1] += fold(cot)
        parts[2] += fold(second * z)
        parts[3] += fold(second)

    row_tiles(hold.shape[0], 48, step)
    for i in range(4):
        sums[i : i + 1, :] = jnp.sum(parts[i], axis=0, keepdims=True)


def attend_back(side, mid_blocks, core, qkv, probs, out_w, grads, pg_q, keys_grad):
    rows = mid_blocks[0].shape[0]
    half_lane = lax.broadcasted_iota(jnp.int32, (1, 2 * HD), 1) // HD
    width = qkv.shape[1] // 3
    for i, block in enumerate(mid_blocks):
        at = pl.multiple_of((core ^ i) * rows, 16)
        grads[pl.ds(at, rows), :] = mm(block[...], out_w[...], NT).astype(BF)

    def one(j, carry):
        place = 3 * side + j
        image = place // 2
        inside = pl.ds(pl.multiple_of(j * HALF, 16), HALF)
        queries = pl.ds(pl.multiple_of(place * HALF, 16), HALF)
        keys = pl.ds(pl.multiple_of(image * SLOTS, 16), SLOTS)
        for pair in range(width // (2 * HD)):
            lanes = pl.ds(pair * 2 * HD, 2 * HD)
            q = qkv[queries, lanes]
            k = qkv[keys, pl.ds(width + pair * 2 * HD, 2 * HD)]
            v = qkv[keys, pl.ds(2 * width + pair * 2 * HD, 2 * HD)]
            g = grads[inside, lanes]
            found = []
            for e in range(2):
                p = probs[j * 4 + pair * 2 + e]
                wide = p.astype(F32)
                prob_grad = mm(jnp.where(half_lane == e, g, jnp.zeros_like(g)), v, NT)
                delta = jnp.sum(wide * prob_grad, axis=-1, keepdims=True)
                score_grad = (wide * (prob_grad - delta) * 0.125).astype(BF)
                found.append(
                    (mm(score_grad, k), mm(score_grad, q, TN), mm(p, g, TN))
                )
            q_grad, k_grad, v_grad = (
                jnp.where(half_lane == 0, a, b) for a, b in zip(*found, strict=True)
            )
            pg_q[inside, lanes] = q_grad
            keys_grad[keys, lanes] += k_grad
            keys_grad[keys, pl.ds(width + pair * 2 * HD, 2 * HD)] += v_grad
        return carry

    lax.fori_loop(0, 3, one, 0)


def back_near(me, mid_a, mid_b, qkv, probs, out_w, pg_q, keys_grad, grads):
    core, far = me[0] & 1, me[0] >> 1
    keys_grad[...] = jnp.zeros_like(keys_grad)
    attend_back(far, (mid_a, mid_b), core, qkv, probs, out_w, grads, pg_q, keys_grad)


def back_far(
    me, mid_a, mid_b, qkv, probs, out_w, near_q, near_keys, in_w,
    proj_near, proj_far, flat_near, flat_far, bias_grad, send, hold, grads, far_q, keys_grad,
):
    core, far = me[0] & 1, me[0] >> 1
    rows = mid_a.shape[0]
    width = far_q.shape[1]
    keys_grad[...] = near_keys[...]
    attend_back(1 - far, (mid_a, mid_b), core, qkv, probs, out_w, grads, far_q, keys_grad)
    bias_grad[...] = jnp.concatenate(
        [
            jnp.sum(far_q[...], axis=0, keepdims=True) + jnp.sum(near_q[...], axis=0, keepdims=True),
            jnp.sum(keys_grad[:, width:], axis=0, keepdims=True),
        ],
        axis=1,
    )
    sides = ((proj_near, flat_near, near_q), (proj_far, flat_far, far_q))
    for side, (out, flat, q_part) in enumerate(sides):
        for i in range(2):
            inside = pl.multiple_of((core ^ i) * rows, 16)
            place = pl.multiple_of((2 * (far ^ side) + (core ^ i)) * rows, 16)
            to = pl.ds(i * rows, rows)
            out[to, :width] = q_part[pl.ds(inside, rows), :].astype(BF)
            out[to, width:] = keys_grad[pl.ds(place, rows), :].astype(BF)
        for head in range(width // HD):
            for kind in range(3):
                at = (head * 3 + kind) * HD
                flat[:, at : at + HD] = out[:, kind * width + head * HD :][:, :HD]
    send[...] = mm(proj_far[rows:, :], in_w[...], NT).astype(BF)
    hold[...] = mm(proj_far[:rows, :], in_w[...], NT)


def first_back(me, proj, in_w, send, hold):
    rows = send.shape[0]
    send[...] = mm(proj[rows:, :], in_w[...], NT).astype(BF)
    hold[...] = mm(proj[:rows, :], in_w[...], NT)


def mixed_piece(me, norm_a, norm_b, proj_a, proj_b, heads_a, heads_b, mid_a, mid_b, out):
    width = proj_a.shape[1]
    out[:, :width] = (
        mm(norm_a[...], proj_a[...], TN) + mm(norm_b[...], proj_b[...], TN)
    ).astype(out.dtype)
    both = mm(heads_a[...], mid_a[...], TN) + mm(heads_b[...], mid_b[...], TN)
    half = both.shape[0] // 2
    out[:, width : width + half] = both[:half].astype(out.dtype)
    out[:, width + half :] = both[half:].astype(out.dtype)


def token_back(me, hold, near, far, tok, middle_grad, vectors, tokens_grad, sums, parts):
    parts[...] = jnp.zeros_like(parts)

    def step(at):
        first = hold[at, :] + near[at, :].astype(F32) + far[at, :].astype(F32)
        z, factor = normalise(tok[at, :].astype(F32))
        tokens_grad[at, :] = middle_grad[at, :] + norm_back(
            first, row(vectors, GAIN_ONE), z, factor
        )
        parts[0] += fold(first * z)
        parts[1] += fold(first)

    row_tiles(hold.shape[0], 48, step)
    for i in range(2):
        sums[i : i + 1, :] = jnp.sum(parts[i], axis=0, keepdims=True)


def place_pieces(order, me, *refs):
    parts, out, wide, sems = refs[:-3], refs[-3], refs[-2], refs[-1]
    piece = out.shape[0] // PIECES
    copies = []
    for i in range(PIECES):
        part, row = locate(parts, i * piece)
        wide[i] = part[row : row + piece, :].astype(F32)
        to = pl.ds(pl.multiple_of(piece_of(i, order, me[1]) * piece, piece), piece)
        copies.append(pltpu.make_async_copy(wide.at[i], out.at[to, :], sems.at[i]))
        copies[-1].start()
    for copy in copies:
        copy.wait()


def locate(parts, row):
    for part in parts:
        if row < part.shape[0]:
            return part, row
        row -= part.shape[0]


def place_mixed(order, other, me, *refs):
    count = (len(refs) - 5) // 2
    first, second = refs[:count], refs[count : 2 * count]
    in_out, out_out, wide, flat, sems = refs[2 * count :]
    piece = in_out.shape[0] // PIECES
    half = out_out.shape[0] // 2
    split = first[0].shape[1]
    rest = in_out.shape[1] - split
    copies = []
    for i in range(PIECES):
        place = piece_of(i, order, me[1])
        to = pl.ds(pl.multiple_of(place * piece, piece), piece)
        part, row = locate(first, i * piece)
        wide[i, :, :split] = part[row : row + piece, :].astype(F32)
        copies.append(
            pltpu.make_async_copy(wide.at[i, :, :split], in_out.at[to, :split], sems.at[i])
        )
        copies[-1].start()
        place = piece_of(i, other, me[1])
        to = pl.ds(pl.multiple_of(place * piece, piece), piece)
        part, row = locate(second, i * piece)
        wide[i, :, split:] = part[row : row + piece, :rest].astype(F32)
        flat[i, :half, :] = part[row : row + piece, rest : rest + half].astype(F32)
        flat[i, half:, :] = part[row : row + piece, rest + half :].astype(F32)
        copies.append(
            pltpu.make_async_copy(wide.at[i, :, split:], in_out.at[to, split:], sems.at[PIECES + i])
        )
        copies[-1].start()
        copies.append(
            pltpu.make_async_copy(flat.at[i], out_out.at[:, to], sems.at[2 * PIECES + i])
        )
        copies[-1].start()
    for copy in copies:
        copy.wait()


def piece_of(position, order, me):
    relative = 0
    for step, bit in enumerate(order):
        relative = relative | (((position >> (len(order) - 1 - step)) & 1) << bit)
    return relative ^ (me & (PIECES - 1))


def pack(values):
    high = values.astype(BF)
    return jnp.concatenate([high, (values - high.astype(F32)).astype(BF)], axis=0)


def add_small(own, other):
    return pack(unpack(own) + unpack(other))


def unpack(packed):
    half = packed.shape[0] // 2
    return packed[:half].astype(F32) + packed[half:].astype(F32)


class Reduction:
    def __init__(self, send, order):
        self.send, self.order = send, order
        self.count = lax.axis_size("dp").bit_length() - 1
        self.bits = [*order, *range(len(order), self.count), *reversed(order)]
        self.values, self.small, self.came, self.at = None, None, None, 0

    def take(self, *earlier):
        self.came = swap(self.send, "dp", 1 << self.bits[self.at])
        if earlier:
            self.came = after(self.came, *earlier)
        return self.came

    def arrive(self, *earlier):
        if self.came is None:
            self.take()
        arrived = after(self.came, *earlier)
        self.came = None
        self.at += 1
        halving = len(self.order)
        if self.at < halving:
            dims = (self.values.shape[0] // 2, self.values.shape[1])
            leave(self.values)
            self.send, self.values = run(
                add_halves,
                (jnp.zeros((1,), jnp.int32), self.values, arrived),
                [shape(dims, BF), shape(dims)],
            )
            stay(self.values)
        elif self.at == halving:
            leave(self.values)
            self.values = add_round(self.values, arrived)
            self.send = self.values
        elif self.at <= self.count:
            self.values = (self.values.astype(F32) + arrived.astype(F32)).astype(BF)
            self.send = self.values
        else:
            rows = self.values.shape[0]
            if self.small is not None:
                self.small = pack(unpack(self.small) + unpack(arrived[rows:]))
            if self.at == len(self.bits):
                self.parts = (self.values, arrived)
                return arrived
            self.values = jnp.concatenate([self.values, arrived[:rows]], axis=0)
            self.send = self.values
            if self.small is not None:
                self.send = jnp.concatenate([self.values, self.small], axis=0)
        return self.send

    def join(self, small):
        for bit in range(len(self.order), self.count):
            small = pack(unpack(small) + unpack(swap(small, "dp", 1 << bit)))
        self.small = small
        self.send = jnp.concatenate([self.values, small], axis=0)


ORDER_A = (0, 1, 2)
ORDER_B = (1, 0, 2)


def weight_grad(me, lefts, rights, order, kept, low=0, wide=None):
    rows, columns = lefts[0].shape
    wide = wide or rights[0].shape[1]
    half = columns // 2
    return run(
        functools.partial(
            weight_pieces, order, 0 if kept else PIECES // 2, low, (len(lefts), len(rights))
        ),
        (me, *lefts, *rights),
        [shape((half, wide), F32 if kept else BF)],
        scratch=[pltpu.VMEM((half, rows), BF)] * len(lefts),
        flops=2 * len(lefts) * rows * half * wide,
    )[0]


def mixed_grad(me, normed, proj, heads, mids, order, kept, low):
    rows, columns = normed[0].shape
    half = columns // 2
    wide = proj[0].shape[1] - low + heads[0].shape[1]
    return run(
        functools.partial(mixed_pieces, order, 0 if kept else PIECES // 2, low),
        (me, *normed, *proj, *heads, *mids),
        [shape((half, wide), F32 if kept else BF)],
        scratch=[pltpu.VMEM((half, rows), BF)] * 2,
        flops=2 * 2 * rows * half * wide,
    )[0]


def place(me, parts, order):
    rows, wide = 2 * parts[0].shape[0], parts[0].shape[1]
    return run_out(
        functools.partial(place_pieces, order),
        (me, *parts),
        [shape((rows, wide))],
        scratch=[
            pltpu.VMEM((PIECES, rows // PIECES, wide), F32),
            pltpu.SemaphoreType.DMA((PIECES,)),
        ],
    )[0]


def on_device(
    tokens,
    keep_mask,
    grad_out,
    in_weight,
    in_bias,
    out_weight,
    out_bias,
    up_weight,
    up_bias,
    down_weight,
    down_bias,
    gain_one,
    shift_one,
    gain_two,
    shift_two,
):
    rows, model = tokens.shape
    leave(*STAY)
    me = jnp.stack([lax.axis_index("tensor"), lax.axis_index("dp")]).astype(jnp.int32)
    images = keep_mask.shape[0]
    heads = in_weight.shape[1] // (3 * HD)
    width = heads * HD
    hidden = up_weight.shape[1]

    def line(values):
        return values.reshape(1, -1)

    side = 2 * rows
    block = 256
    project_flops = 2 * side * model * 3 * width
    attend_flops = 3 * heads * 4 * HALF * SLOTS * 128 + 2 * side * width * model
    back_flops = 3 * heads * 10 * HALF * SLOTS * 128 + 2 * side * width * model

    def act_grad_of(one, other):
        return run(
            act_back,
            (me, one, other, down_weight),
            [shape((side, hidden))],
            flops=2 * side * model * hidden,
        )[0]

    def feed(one, other, act_grad):
        return run(
            feed_forward,
            (me, one, other, up_weight, vectors, act_grad),
            [
                shape((side, hidden), BF),
                shape((side, hidden), BF),
                shape((1, hidden)),
                shape((rows, model), BF),
                shape((rows, model)),
            ],
            scratch=[pltpu.VMEM((side, model), F32), pltpu.VMEM((side, block), F32)],
            flops=4 * side * model * hidden,
        )

    def feed_back(me, act):
        return run(
            feed_out,
            (me, act, down_weight),
            [shape((rows, model), BF), shape((rows, model))],
            flops=2 * side * model * hidden,
        )

    tok_far = swap(tokens, "tensor", 2)
    tok_core = swap(tokens, "tensor", 1)
    keep_flat = keep_mask.reshape(-1).astype(F32)
    keep_own = lax.dynamic_slice_in_dim(keep_flat, me[0] * rows, rows)[:, None]
    cot = (grad_out.astype(F32) * keep_own).astype(BF)
    cot_core = swap(cot, "tensor", 1)
    in_grouped = in_weight.reshape(model, heads, 3, HD).transpose(0, 2, 1, 3)
    in_grouped = in_grouped.reshape(model, 3 * width)
    pair = in_bias.reshape(heads, 2, HD).transpose(1, 0, 2).reshape(2, width)
    bias_full = jnp.concatenate([pair[:1], jnp.zeros((1, width), F32), pair[1:]], axis=1)
    vectors = jnp.stack(
        [gain_one, shift_one, out_bias, gain_two, shift_two, up_bias, down_bias, down_bias]
    )
    stay(in_grouped, bias_full, vectors, out_weight, down_weight, up_weight, tokens, cot)
    norm_near, proj_near = run(
        project_local,
        (me, tokens, tok_core, vectors, in_grouped, bias_full),
        [shape((side, model), BF), shape((side, 3 * width), BF)],
        flops=project_flops,
    )
    stay(norm_near)
    tok_far = after(tok_far, proj_near)

    tok_both = swap(tok_far, "tensor", 1)
    cot_far = swap(after(cot, tok_far), "tensor", 2)
    attend_outs = [
        shape((3 * heads, HALF, SLOTS), BF),
        shape((side, width), BF),
        shape((rows, model), BF),
        shape((rows, model), F32),
    ]
    norm_far, qkv, probs_far, heads_far, send, far_hold = run(
        attend_far,
        (
            me, proj_near, tok_far, tok_both, vectors, in_grouped, bias_full, keep_mask, out_weight,
        ),
        [shape((side, model), BF), shape((2 * side, 3 * width), BF), *attend_outs],
        flops=project_flops + attend_flops,
    )
    stay(norm_far, qkv, probs_far, heads_far)
    leave(bias_full)
    arrived = after(swap(send, "tensor", 1), cot_far)
    far_sum = add_round(far_hold, arrived)
    cot_far = after(cot_far, far_sum)
    cot_both = swap(cot_far, "tensor", 1)
    arrived_far = swap(far_sum, "tensor", 2)
    probs_near, heads_near, send, hold = run(
        attend_near,
        (after(me, far_sum), qkv, keep_mask, out_weight),
        attend_outs,
        flops=attend_flops,
    )
    stay(probs_near, heads_near, hold)
    act_grad_near = act_grad_of(cot, cot_core)
    stay(act_grad_near, cot_core)
    arrived_near = after(swap(send, "tensor", 1), arrived_far)
    middle, second = run(
        second_norm,
        (
            after(me, act_grad_near), tokens, hold, arrived_near, arrived_far, vectors,
        ),
        [shape((rows, model)), shape((rows, model), BF)],
    )

    leave(hold)
    stay(middle, second)

    second_far = swap(second, "tensor", 2)
    second_core = swap(second, "tensor", 1)
    act_near, pre_near, up_bias_near, near_send, near_hold = feed(
        second, second_core, act_grad_near
    )
    leave(act_grad_near)
    stay(act_near, pre_near, near_hold, second_core)
    act_grad_far = act_grad_of(cot_far, cot_both)
    stay(cot_far, cot_both, act_grad_far)
    second_far = after(second_far, act_grad_far)
    second_both = swap(second_far, "tensor", 1)
    act_far, pre_far, up_bias_far, far_send, far_hold = feed(
        second_far, second_both, act_grad_far
    )
    far_sum = add_round(far_hold, swap(far_send, "tensor", 1))
    arrived_far = swap(far_sum, "tensor", 2)
    leave(act_grad_far, up_weight)
    stay(act_far, pre_far, second_far, second_both)
    acts, cots = (act_near, act_far), (cot, cot_core, cot_far, cot_both)
    down_send = weight_grad(after(me, far_sum), acts, cots, ORDER_A, False)
    down = Reduction(down_send, ORDER_A)
    seconds = (second, second_core, second_far, second_both)
    pres = (pre_near, pre_far)
    up_send = weight_grad(after(me, down_send), seconds, pres, ORDER_B, False)
    up = Reduction(up_send, ORDER_B)
    arrived_near = swap(near_send, "tensor", 1)
    feed_send, feed_hold = feed_back(after(me, up_send), act_far)
    feed_far = add_round(feed_hold, swap(feed_send, "tensor", 1))
    middle_grad, middle_low, middle_sums = run(
        middle_back,
        (
            after(me, feed_hold), near_hold, arrived_near, arrived_far, middle, cot, vectors,
        ),
        [shape((rows, model)), shape((rows, model), BF), shape((4, model))],
        scratch=[pltpu.VMEM((4, 8, model), F32)],
    )

    mid_far = swap(middle_low, "tensor", 2)
    mid_core = swap(middle_low, "tensor", 1)
    grads = pltpu.VMEM((side, width), BF)
    leave(near_hold)
    stay(middle_grad, middle_low)
    down.values = weight_grad(after(me, middle_low), acts, cots, ORDER_A, True)
    leave(act_far, cot_core, cot_far, cot_both)
    stay(down.values)
    near_q, near_keys = run(
        back_near,
        (after(me, down.values), middle_low, mid_core, qkv, probs_near, out_weight),
        [shape((side, width)), shape((2 * side, 2 * width))],
        scratch=[grads],
        flops=back_flops,
    )
    leave(probs_near)
    stay(near_q, near_keys, mid_core)
    up.values = weight_grad(after(me, near_q), seconds, pres, ORDER_B, True)
    leave(second, second_core, second_far, second_both, pre_near, pre_far)
    stay(up.values)
    mid_far = after(mid_far, up.values)
    mid_both = swap(mid_far, "tensor", 1)
    feed_far = swap(after(feed_far, mid_far), "tensor", 2)
    down.arrive(mid_far)
    up.arrive(mid_far)
    proj_near, proj_far, flat_near, flat_far, bias_grad, far_send, far_hold = run(
        back_far,
        (
            after(me, down.send, up.send), mid_far, mid_both, qkv, probs_far,
            out_weight, near_q, near_keys, in_grouped,
        ),
        [
            shape((side, 3 * width), BF),
            shape((side, 3 * width), BF),
            shape((side, 3 * width), BF),
            shape((side, 3 * width), BF),
            shape((1, 2 * width)),
            shape((rows, model), BF),
            shape((rows, model)),
        ],
        scratch=[
            grads,
            pltpu.VMEM((side, width), F32),
            pltpu.VMEM((2 * side, 2 * width), F32),
        ],
        flops=back_flops + project_flops,
    )
    leave(qkv, probs_far, near_q, near_keys, out_weight)
    stay(proj_near, flat_near, flat_far, mid_far, mid_both)
    down.take(bias_grad)
    up.take(bias_grad)
    arrived = after(swap(far_send, "tensor", 1), feed_far, down.came, up.came)
    far_sum = add_round(far_hold, arrived)
    arrived_far = swap(far_sum, "tensor", 2)

    down.arrive(far_sum)
    up.arrive(far_sum)
    near_send, hold = run(
        first_back,
        (after(me, down.send, up.send), proj_near, in_grouped),
        [shape((rows, model), BF), shape((rows, model))],
        flops=project_flops,
    )
    leave(in_grouped, proj_near)
    stay(hold)
    normed = (norm_near, norm_far)
    split = (3 * width + width) // 2
    flat = (flat_near, flat_far)
    head_rows = (heads_near, heads_far)
    mids = (middle_low, mid_core, mid_far, mid_both)
    arrived_near = swap(near_send, "tensor", 1)
    first_send = weight_grad(after(me, hold), normed, flat, ORDER_A, False, 0, split)
    first = Reduction(first_send, ORDER_A)
    mixed_send = mixed_grad(
        after(me, first_send), normed, flat, head_rows, mids, ORDER_B, False, split
    )
    mixed = Reduction(mixed_send, ORDER_B)
    first.values = weight_grad(after(me, mixed_send), normed, flat, ORDER_A, True, 0, split)
    stay(first.values)
    mixed.values = mixed_grad(
        after(me, first.values), normed, flat, head_rows, mids, ORDER_B, True, split
    )
    leave(norm_near, norm_far, flat_near, flat_far, heads_near, heads_far)
    leave(middle_low, mid_core, mid_far, mid_both)
    stay(mixed.values)
    tokens_grad, token_sums = run(
        token_back,
        (
            after(me, mixed.values), hold, arrived_near, arrived_far, tokens, middle_grad, vectors,
        ),
        [shape((rows, model)), shape((2, model))],
        scratch=[pltpu.VMEM((2, 8, model), F32)],
    )
    leave(hold, tokens, middle_grad, vectors)
    feed_send, feed_hold = feed_back(after(me, token_sums), act_near)
    feed_rows = feed_hold + swap(feed_send, "tensor", 1).astype(F32) + feed_far.astype(F32)
    output = (keep_own * (middle + feed_rows + down_bias)).astype(BF)
    leave(*STAY)
    stay(down.values, up.values, first.values, mixed.values)

    now = down.arrive(feed_hold)
    now = first.arrive(now)
    shared = pack(jnp.concatenate([middle_sums, token_sums], axis=0))
    shared = add_small(shared, swap(shared, "tensor", 1))
    shared = unpack(add_small(shared, swap(shared, "tensor", 2)))
    own = jnp.concatenate(
        [up_bias_near + up_bias_far, jnp.pad(bias_grad, ((0, 0), (0, hidden - 2 * width)))], axis=0
    )
    small = jnp.concatenate([shared, own], axis=0)
    small = pack(jnp.concatenate([small[:, :split], small[:, split:]], axis=0))
    now = mixed.arrive(now)
    now = up.arrive(now)
    now = down.arrive(now)
    now = mixed.arrive(now)
    now = first.arrive(now)
    now = up.arrive(now)
    now = down.arrive(now)
    now = mixed.arrive(now)
    now = first.arrive(now)
    while first.at < first.count:
        now = first.arrive(now)
    first.join(small)
    now = mixed.arrive(now)
    now = first.arrive(now)
    now = up.arrive(now)
    last = [mixed, first, down, up]
    while any(x.at < len(x.bits) for x in last):
        for x in last:
            if x.at < len(x.bits):
                now = x.arrive(now)
    small = unpack(first.small)
    small = jnp.concatenate([small[:8], small[8:]], axis=1)
    piece = model // PIECES
    down_sum = place(me, down.parts, ORDER_A)
    up_sum = place(me, up.parts, ORDER_B)
    in_sum, out_sum = run_out(
        functools.partial(place_mixed, ORDER_A, ORDER_B),
        (me, *first.parts, *mixed.parts),
        [shape((model, 3 * width)), shape((width, model))],
        scratch=[
            pltpu.VMEM((PIECES, piece, 3 * width), F32),
            pltpu.VMEM((PIECES, width, piece), F32),
            pltpu.SemaphoreType.DMA((3 * PIECES,)),
        ],
    )
    in_bias_sum = small[7, : 2 * width].reshape(2, heads, HD).transpose(1, 0, 2).reshape(-1)
    return (
        output,
        tokens_grad,
        in_sum,
        in_bias_sum,
        out_sum,
        small[0],
        up_sum,
        small[6],
        down_sum,
        small[1],
        small[4],
        small[5],
        small[2],
        small[3],
    )


def solution(mesh):
    rows = P(("dp", "tensor"), None)
    placed = (
        rows,
        P("dp", None),
        rows,
        P(None, "tensor"),
        P("tensor"),
        P("tensor", None),
        P(),
        P(None, "tensor"),
        P("tensor"),
        P("tensor", None),
        P(),
        P(),
        P(),
        P(),
        P(),
    )
    given = (
        rows,
        rows,
        P(None, "tensor"),
        P("tensor"),
        P("tensor", None),
        P(),
        P(None, "tensor"),
        P("tensor"),
        P("tensor", None),
        P(),
        P(),
        P(),
        P(),
        P(),
    )
    return jax.shard_map(on_device, mesh=mesh, in_specs=placed, out_specs=given, check_vma=False)
```

```python
import functools

import jax
import jax.numpy as jnp
from jax import lax
from jax.experimental import pallas as pl
from jax.experimental.pallas import tpu as pltpu
from jax.sharding import PartitionSpec as P

HD = 64
SLOTS = 320
HALF = SLOTS // 2
PIECES = 8
EPSILON = 1e-06
BF = jnp.bfloat16
F32 = jnp.float32
MIB = 1 << 20


def mm(left, right, dims=((1,), (0,))):
    return lax.dot_general(left, right, (dims, ((), ())), preferred_element_type=F32)


NT = ((1,), (1,))
TN = ((0,), (0,))


def swap(values, axis, bit):
    count = lax.axis_size(axis)
    return lax.ppermute(values, axis, [(i, i ^ bit) for i in range(count)])


def after(values, *earlier):
    return lax.optimization_barrier((values, *earlier))[0]


def shape(dims, kind=F32):
    return jax.ShapeDtypeStruct(dims, kind)


STAY = []


def stay(*arrays):
    STAY.extend(arrays)


def leave(*arrays):
    for array in arrays:
        STAY[:] = [x for x in STAY if x is not array]


def run(body, operands, outs, scratch=(), flops=0, room=12):
    used = list(operands[1:])
    waiting = [x for x in STAY if all(x is not y for y in used)]
    ins = [pltpu.with_memory_space_constraint(x, pltpu.VMEM) for x in [*used, *waiting]]
    moved = sum(x.size * x.dtype.itemsize for x in [*used, *outs])

    def kernel(*refs):
        own = 1 + len(used)
        body(*refs[:own], *refs[own + len(waiting) :])

    return pl.pallas_call(
        kernel,
        out_shape=[pltpu.VMEM(x.shape, x.dtype) for x in outs],
        in_specs=[pl.BlockSpec(memory_space=pltpu.SMEM)]
        + [pl.BlockSpec(memory_space=pltpu.VMEM)] * len(ins),
        out_specs=[pl.BlockSpec(memory_space=pltpu.VMEM)] * len(outs),
        scratch_shapes=scratch,
        compiler_params=pltpu.CompilerParams(vmem_limit_bytes=room * MIB),
        cost_estimate=pl.CostEstimate(
            flops=int(flops * WEIGHT), bytes_accessed=0, transcendentals=0
        ),
    )(operands[0], *ins)


WEIGHT = 20


def add_low(me, left, right, out):
    out[...] = (left[...] + right[...].astype(F32)).astype(BF)


def add_round(left, right):
    return run(add_low, (jnp.zeros((1,), jnp.int32), left, right), [shape(left.shape, BF)])[0]


def add_halves(me, left, right, send, hold):
    middle = send.shape[0]
    send[...] = (left[middle:, :] + right[middle:, :].astype(F32)).astype(BF)
    hold[...] = left[:middle, :] + right[:middle, :].astype(F32)


def run_out(body, operands, outs, scratch=(), room=16):
    ins = [pltpu.with_memory_space_constraint(x, pltpu.VMEM) for x in operands[1:]]
    return pl.pallas_call(
        body,
        out_shape=[pltpu.HBM(x.shape, x.dtype) for x in outs],
        in_specs=[pl.BlockSpec(memory_space=pltpu.SMEM)]
        + [pl.BlockSpec(memory_space=pltpu.VMEM)] * len(ins),
        out_specs=[pl.BlockSpec(memory_space=pltpu.HBM)] * len(outs),
        scratch_shapes=scratch,
        compiler_params=pltpu.CompilerParams(vmem_limit_bytes=room * MIB),
        cost_estimate=pl.CostEstimate(
            flops=0, bytes_accessed=0, transcendentals=0
        ),
    )(operands[0], *ins)


def blocks(count, size, step):
    def one(i, carry):
        step(pl.ds(pl.multiple_of(i * size, size), size), i)
        return carry

    lax.fori_loop(0, count, one, 0)


def row_tiles(rows, size, step):
    def one(i, carry):
        step(pl.ds(pl.multiple_of(i * size, size), size))
        return carry

    lax.fori_loop(0, rows // size, one, 0)


def normalise(values):
    average = jnp.mean(values, axis=-1, keepdims=True)
    centred = values - average
    factor = lax.rsqrt(jnp.mean(centred * centred, axis=-1, keepdims=True) + EPSILON)
    return centred * factor, factor


def norm_back(grad, gain, z, factor):
    s = grad * gain
    return factor * (
        s - jnp.mean(s, axis=-1, keepdims=True) - z * jnp.mean(s * z, axis=-1, keepdims=True)
    )


def fold(values):
    return functools.reduce(
        lambda a, b: a + b, [values[i : i + 8] for i in range(0, values.shape[0], 8)]
    )


GAIN_ONE, SHIFT_ONE, OUT_BIAS, GAIN_TWO, SHIFT_TWO, UP_BIAS, DOWN_BIAS = range(7)


def row(vectors, number):
    return vectors[number : number + 1, :]


def project_side(blocks, vectors, weight, bias, normed, put):
    rows = blocks[0].shape[0]
    width = weight.shape[1] // 3
    for i, block in enumerate(blocks):

        def step(at, block=block, i=i):
            z, _ = normalise(block[at, :].astype(F32))
            tile = pl.ds(pl.multiple_of(at.start + i * rows, 16), at.size)
            normed[tile, :] = (z * row(vectors, GAIN_ONE) + row(vectors, SHIFT_ONE)).astype(BF)

        row_tiles(rows, 48, step)
        found = (mm(normed[i * rows : (i + 1) * rows, :], weight[...]) + bias[...]).astype(BF)
        kinds = [
            [found[:, (3 * head + kind) * HD :][:, :HD] for head in range(width // HD)]
            for kind in range(3)
        ]
        put(i, jnp.concatenate(sum(kinds, []), axis=1))


def project_local(me, tok_a, tok_b, vectors, weight, bias, normed, proj):
    rows = tok_a.shape[0]

    def put(i, values):
        proj[i * rows : (i + 1) * rows, :] = values

    project_side((tok_a, tok_b), vectors, weight, bias, normed, put)


def attend(side, qkv, keep, probs, heads_out):
    half_lane = lax.broadcasted_iota(jnp.int32, (1, 2 * HD), 1) // HD
    width = qkv.shape[1] // 3

    def one(j, carry):
        place = 3 * side + j
        image = place // 2
        queries = pl.ds(pl.multiple_of(place * HALF, 16), HALF)
        keys = pl.ds(pl.multiple_of(image * SLOTS, 16), SLOTS)
        live = keep[pl.ds(image, 1), :] > 0
        for pair in range(width // (2 * HD)):
            lanes = pl.ds(pair * 2 * HD, 2 * HD)
            q = qkv[queries, lanes] * 0.125
            k = qkv[keys, pl.ds(width + pair * 2 * HD, 2 * HD)]
            v = qkv[keys, pl.ds(2 * width + pair * 2 * HD, 2 * HD)]
            outs = []
            for e in range(2):
                scores = mm(jnp.where(half_lane == e, q, jnp.zeros_like(q)), k, NT)
                scores = jnp.where(live, scores, -1000000000.0)
                power = jnp.exp(scores - jnp.max(scores, axis=-1, keepdims=True))
                p = (power / jnp.sum(power, axis=-1, keepdims=True)).astype(BF)
                probs[j * 4 + pair * 2 + e] = p
                outs.append(mm(p, v))
            heads_out[pl.ds(pl.multiple_of(j * HALF, 16), HALF), lanes] = jnp.where(
                half_lane == 0, outs[0], outs[1]
            ).astype(BF)
        return carry

    lax.fori_loop(0, 3, one, 0)


def out_project(core, heads_out, weight, send, hold):
    rows = send.shape[0]
    send[...] = mm(
        heads_out[pl.ds(pl.multiple_of((1 - core) * rows, 16), rows), :], weight[...]
    ).astype(BF)
    hold[...] = mm(heads_out[pl.ds(pl.multiple_of(core * rows, 16), rows), :], weight[...])


def project_one(me, tok, vectors, weight, bias, normed, proj):
    def put(i, values):
        proj[...] = values

    project_side((tok,), vectors, weight, bias, normed, put)


def attend_far(
    me, near, first, tok, vectors, weight, bias, keep, out_w,
    normed, qkv, probs, heads_out, send, hold,
):
    rows = tok.shape[0]
    core, far = me[0] & 1, me[0] >> 1
    for i in range(2):
        at = pl.multiple_of((2 * far + (core ^ i)) * rows, 16)
        qkv[pl.ds(at, rows), :] = near[i * rows : (i + 1) * rows, :]
    at = pl.multiple_of((2 * (1 - far) + core) * rows, 16)
    qkv[pl.ds(at, rows), :] = first[...]

    def put(i, values):
        at = pl.multiple_of((2 * (1 - far) + (1 - core)) * rows, 16)
        qkv[pl.ds(at, rows), :] = values

    project_side((tok,), vectors, weight, bias, normed, put)
    attend(1 - far, qkv, keep, probs, heads_out)
    out_project(core, heads_out, out_w, send, hold)


def attend_near(me, qkv, keep, out_w, probs, heads_out, send, hold):
    core, far = me[0] & 1, me[0] >> 1
    attend(far, qkv, keep, probs, heads_out)
    out_project(core, heads_out, out_w, send, hold)


def second_norm(me, tok, hold, near, far, vectors, middle, second):
    def step(at):
        total = hold[at, :] + near[at, :].astype(F32) + far[at, :].astype(F32)
        values = tok[at, :].astype(F32) + total + row(vectors, OUT_BIAS)
        middle[at, :] = values
        z, _ = normalise(values)
        second[at, :] = (z * row(vectors, GAIN_TWO) + row(vectors, SHIFT_TWO)).astype(BF)

    row_tiles(tok.shape[0], 48, step)


def act_back(me, cot_a, cot_b, down, act_grad):
    rows = cot_a.shape[0]

    def step(at, i):
        act_grad[:rows, at] = mm(cot_a[...], down[at, :], NT)
        act_grad[rows:, at] = mm(cot_b[...], down[at, :], NT)

    blocks(down.shape[0] // 256, 256, step)


def feed_forward(low, count, me, *refs):
    norms = refs[:count]
    up, vectors, act_grad, act, pre_low, bias_grad = refs[count : count + 6]
    outs, total, pre = refs[count + 6 : 2 * count + 6], refs[-2], refs[-1]
    rows = norms[0].shape[0]
    wide = pre.shape[2]
    number = up.shape[1] // wide
    bias_grad[...] = jnp.zeros_like(bias_grad)
    total[...] = jnp.zeros_like(total)

    def columns(i):
        return pl.ds(pl.multiple_of(i * wide, wide), wide)

    def elements(slot, at, block):
        own_bias = vectors[UP_BIAS : UP_BIAS + 1, at]
        sums = None
        for i in range(0, rows, 16):
            to = pl.ds(block * rows + i, 16)
            x = pre[slot, i : i + 16, :] + own_bias
            share = 0.5 + 0.5 * lax.erf(x * 0.7071067811865476)
            slope = share + x * (0.3989422804014327 * jnp.exp(-0.5 * x * x))
            act[to, at] = (x * share).astype(BF)
            grad = act_grad[pl.ds(low + block * rows + i, 16), at] * slope
            pre_low[to, at] = grad.astype(BF)
            part = grad[:8] + grad[8:]
            sums = part if sums is None else sums + part
        bias_grad[:, at] += jnp.sum(sums, axis=0, keepdims=True)

    pre[0] = mm(norms[0][...], up[:, :wide])

    def one(i, carry):
        if count == 2:
            steps = ((i, 0), (i, 1), (jnp.minimum(i + 1, number - 1), 0))
        else:
            steps = ((2 * i, 0), (2 * i + 1, 0), (jnp.minimum(2 * i + 2, number - 1), 0))
        for slot in range(2):
            column, block = steps[slot]
            later, other = steps[slot + 1]
            pre[1 - slot] = mm(norms[other][...], up[:, columns(later)])
            elements(slot, columns(column), block)
            inside = pl.ds(block * rows, rows)
            total[inside, :] += mm(pre_low[inside, columns(column)], up[:, columns(column)], NT)
        return carry

    lax.fori_loop(0, number * count // 2, one, 0)
    for i, out in enumerate(outs):
        out[...] = total[i * rows : (i + 1) * rows, :].astype(out.dtype)


def feed_out(count, me, *refs):
    acts, (down, send, hold) = refs[:count], refs[count:]
    rows = send.shape[0]
    one = acts[-1][rows:, :] if count == 1 else acts[1][...]
    send[...] = mm(one, down[...]).astype(BF)
    hold[...] = mm(acts[0][:rows, :], down[...])


def gather_pieces(me, lefts, order, base, turned):
    piece = lefts[0].shape[1] // PIECES
    for i in range(PIECES // 2):
        at = pl.ds(pl.multiple_of(piece_of(base + i, order, me[1]) * piece, piece), piece)
        for left, to in zip(lefts, turned, strict=True):
            to[i * piece : (i + 1) * piece, :] = left[:, at].T


def segments(lefts, rights):
    found, left, right, a, b = [], 0, 0, 0, 0
    while left < len(lefts):
        rows = min(lefts[left].shape[0] - a, rights[right].shape[0] - b)
        found.append((left, a, right, b, rows))
        a, b = a + rows, b + rows
        if a == lefts[left].shape[0]:
            left, a = left + 1, 0
        if b == rights[right].shape[0]:
            right, b = right + 1, 0
    return found


def weight_pieces(order, base, low, count, me, *refs):
    lefts, rights = refs[: count[0]], refs[count[0] : sum(count)]
    out, turned = refs[sum(count)], refs[sum(count) + 1 :]
    gather_pieces(me, lefts, order, base, turned)

    def step(at, i):
        found = None
        from_ = pl.ds(pl.multiple_of(at.start + low, 128), at.size)
        for left, a, right, b, rows in segments(lefts, rights):
            part = mm(turned[left][:, a : a + rows], rights[right][b : b + rows, from_])
            found = part if found is None else found + part
        out[:, at] = found.astype(out.dtype)

    blocks(out.shape[1] // 256, 256, step)


def mixed_pieces(order, base, low, me, *refs):
    lefts, rights, heads, mids, out = refs[:3], refs[3:5], refs[5:7], refs[7:11], refs[11]
    turned = refs[12:]
    gather_pieces(me, lefts, order, base, turned)
    width = rights[0].shape[1] - low
    for at in range(0, width, 256):
        found = None
        for left, a, right, b, rows in segments(lefts, rights):
            part = mm(
                turned[left][:, a : a + rows],
                rights[right][b : b + rows, low + at : low + at + 256],
            )
            found = part if found is None else found + part
        out[:, at : at + 256] = found.astype(out.dtype)
    core = me[0] & 1
    rows = mids[0].shape[0]
    piece = mids[0].shape[1] // PIECES
    half = heads[0].shape[1] // 2
    for i in range(PIECES // 2):
        at = pl.ds(pl.multiple_of(piece_of(base + i, order, me[1]) * piece, piece), piece)
        both = None
        for k in range(4):
            inside = pl.ds(pl.multiple_of((core ^ (k % 2)) * rows, 16), rows)
            part = mm(heads[k // 2][inside, :], mids[k][:, at], TN)
            both = part if both is None else both + part
        to = pl.ds(i * piece, piece)
        out[to, width : width + half] = both[:half].astype(out.dtype)
        out[to, width + half :] = both[half:].astype(out.dtype)


def middle_back(me, hold, near, far, middle, cot_low, vectors, middle_grad, middle_low, sums, parts):
    parts[...] = jnp.zeros_like(parts)

    def step(at):
        second = hold[at, :] + near[at, :].astype(F32) + far[at, :].astype(F32)
        z, factor = normalise(middle[at, :])
        cot = cot_low[at, :].astype(F32)
        total = cot + norm_back(second, row(vectors, GAIN_TWO), z, factor)
        middle_grad[at, :] = total
        middle_low[at, :] = total.astype(BF)
        parts[0] += fold(total)
        parts[1] += fold(cot)
        parts[2] += fold(second * z)
        parts[3] += fold(second)

    row_tiles(hold.shape[0], 48, step)
    for i in range(4):
        sums[i : i + 1, :] = jnp.sum(parts[i], axis=0, keepdims=True)


def attend_back(side, mid_blocks, core, qkv, probs, out_w, grads, pg_q, keys_grad):
    rows = mid_blocks[0].shape[0]
    half_lane = lax.broadcasted_iota(jnp.int32, (1, 2 * HD), 1) // HD
    width = qkv.shape[1] // 3
    for i, block in enumerate(mid_blocks):
        at = pl.multiple_of((core ^ i) * rows, 16)
        grads[pl.ds(at, rows), :] = mm(block[...], out_w[...], NT).astype(BF)

    def one(j, carry):
        place = 3 * side + j
        image = place // 2
        inside = pl.ds(pl.multiple_of(j * HALF, 16), HALF)
        queries = pl.ds(pl.multiple_of(place * HALF, 16), HALF)
        keys = pl.ds(pl.multiple_of(image * SLOTS, 16), SLOTS)
        for pair in range(width // (2 * HD)):
            lanes = pl.ds(pair * 2 * HD, 2 * HD)
            q = qkv[queries, lanes]
            k = qkv[keys, pl.ds(width + pair * 2 * HD, 2 * HD)]
            v = qkv[keys, pl.ds(2 * width + pair * 2 * HD, 2 * HD)]
            g = grads[inside, lanes]
            found = []
            for e in range(2):
                p = probs[j * 4 + pair * 2 + e]
                wide = p.astype(F32)
                prob_grad = mm(jnp.where(half_lane == e, g, jnp.zeros_like(g)), v, NT)
                delta = jnp.sum(wide * prob_grad, axis=-1, keepdims=True)
                score_grad = (wide * (prob_grad - delta) * 0.125).astype(BF)
                found.append(
                    (mm(score_grad, k), mm(score_grad, q, TN), mm(p, g, TN))
                )
            q_grad, k_grad, v_grad = (
                jnp.where(half_lane == 0, a, b) for a, b in zip(*found, strict=True)
            )
            pg_q[inside, lanes] = q_grad
            keys_grad[keys, lanes] += k_grad
            keys_grad[keys, pl.ds(width + pair * 2 * HD, 2 * HD)] += v_grad
        return carry

    lax.fori_loop(0, 3, one, 0)


def back_near(me, mid_a, mid_b, qkv, probs, out_w, pg_q, keys_grad, grads):
    core, far = me[0] & 1, me[0] >> 1
    keys_grad[...] = jnp.zeros_like(keys_grad)
    attend_back(far, (mid_a, mid_b), core, qkv, probs, out_w, grads, pg_q, keys_grad)


def back_far(
    me, mid_a, mid_b, qkv, probs, out_w, near_q, near_keys, in_w,
    flat_near, flat_far, bias_grad, send, hold, grads, far_q, keys_grad, group,
):
    core, far = me[0] & 1, me[0] >> 1
    rows = mid_a.shape[0]
    width = far_q.shape[1]
    keys_grad[...] = near_keys[...]
    attend_back(1 - far, (mid_a, mid_b), core, qkv, probs, out_w, grads, far_q, keys_grad)
    bias_grad[...] = jnp.concatenate(
        [
            jnp.sum(far_q[...], axis=0, keepdims=True) + jnp.sum(near_q[...], axis=0, keepdims=True),
            jnp.sum(keys_grad[:, width:], axis=0, keepdims=True),
        ],
        axis=1,
    )
    for side, (flat, q_part) in enumerate(((flat_near, near_q), (flat_far, far_q))):
        for i in range(2):
            inside = pl.multiple_of((core ^ i) * rows, 16)
            place = pl.multiple_of((2 * (far ^ side) + (core ^ i)) * rows, 16)
            to = pl.ds(i * rows, rows)
            group[to, :width] = q_part[pl.ds(inside, rows), :].astype(BF)
            group[to, width:] = keys_grad[pl.ds(place, rows), :].astype(BF)
        for head in range(width // HD):
            for kind in range(3):
                at = (head * 3 + kind) * HD
                flat[:, at : at + HD] = group[:, kind * width + head * HD :][:, :HD]
    send[...] = mm(flat_far[rows:, :], in_w[...], NT).astype(BF)
    hold[...] = mm(flat_far[:rows, :], in_w[...], NT)


def first_back(me, proj, in_w, send, hold):
    rows = send.shape[0]
    send[...] = mm(proj[rows:, :], in_w[...], NT).astype(BF)
    hold[...] = mm(proj[:rows, :], in_w[...], NT)


def mixed_piece(me, norm_a, norm_b, proj_a, proj_b, heads_a, heads_b, mid_a, mid_b, out):
    width = proj_a.shape[1]
    out[:, :width] = (
        mm(norm_a[...], proj_a[...], TN) + mm(norm_b[...], proj_b[...], TN)
    ).astype(out.dtype)
    both = mm(heads_a[...], mid_a[...], TN) + mm(heads_b[...], mid_b[...], TN)
    half = both.shape[0] // 2
    out[:, width : width + half] = both[:half].astype(out.dtype)
    out[:, width + half :] = both[half:].astype(out.dtype)


def token_back(me, hold, near, far, tok, middle_grad, vectors, tokens_grad, sums, parts):
    parts[...] = jnp.zeros_like(parts)

    def step(at):
        first = hold[at, :] + near[at, :].astype(F32) + far[at, :].astype(F32)
        z, factor = normalise(tok[at, :].astype(F32))
        tokens_grad[at, :] = middle_grad[at, :] + norm_back(
            first, row(vectors, GAIN_ONE), z, factor
        )
        parts[0] += fold(first * z)
        parts[1] += fold(first)

    row_tiles(hold.shape[0], 48, step)
    for i in range(2):
        sums[i : i + 1, :] = jnp.sum(parts[i], axis=0, keepdims=True)


def place_pieces(order, me, *refs):
    parts, out, wide, sems = refs[:-3], refs[-3], refs[-2], refs[-1]
    piece = out.shape[0] // PIECES
    copies = []
    for i in range(PIECES):
        part, row = locate(parts, i * piece)
        wide[i] = part[row : row + piece, :].astype(F32)
        to = pl.ds(pl.multiple_of(piece_of(i, order, me[1]) * piece, piece), piece)
        copies.append(pltpu.make_async_copy(wide.at[i], out.at[to, :], sems.at[i]))
        copies[-1].start()
    for copy in copies:
        copy.wait()


def locate(parts, row):
    for part in parts:
        if row < part.shape[0]:
            return part, row
        row -= part.shape[0]


def place_mixed(order, other, me, *refs):
    count = (len(refs) - 5) // 2
    first, second = refs[:count], refs[count : 2 * count]
    in_out, out_out, wide, flat, sems = refs[2 * count :]
    piece = in_out.shape[0] // PIECES
    half = out_out.shape[0] // 2
    split = first[0].shape[1]
    rest = in_out.shape[1] - split
    copies = []
    for i in range(PIECES):
        place = piece_of(i, order, me[1])
        to = pl.ds(pl.multiple_of(place * piece, piece), piece)
        part, row = locate(first, i * piece)
        wide[i, :, :split] = part[row : row + piece, :].astype(F32)
        copies.append(
            pltpu.make_async_copy(wide.at[i, :, :split], in_out.at[to, :split], sems.at[i])
        )
        copies[-1].start()
        place = piece_of(i, other, me[1])
        to = pl.ds(pl.multiple_of(place * piece, piece), piece)
        part, row = locate(second, i * piece)
        wide[i, :, split:] = part[row : row + piece, :rest].astype(F32)
        flat[i, :half, :] = part[row : row + piece, rest : rest + half].astype(F32)
        flat[i, half:, :] = part[row : row + piece, rest + half :].astype(F32)
        copies.append(
            pltpu.make_async_copy(wide.at[i, :, split:], in_out.at[to, split:], sems.at[PIECES + i])
        )
        copies[-1].start()
        copies.append(
            pltpu.make_async_copy(flat.at[i], out_out.at[:, to], sems.at[2 * PIECES + i])
        )
        copies[-1].start()
    for copy in copies:
        copy.wait()


def piece_of(position, order, me):
    relative = 0
    for step, bit in enumerate(order):
        relative = relative | (((position >> (len(order) - 1 - step)) & 1) << bit)
    return relative ^ (me & (PIECES - 1))


def pack(values):
    high = values.astype(BF)
    return jnp.concatenate([high, (values - high.astype(F32)).astype(BF)], axis=0)


def add_small(own, other):
    return pack(unpack(own) + unpack(other))


def unpack(packed):
    half = packed.shape[0] // 2
    return packed[:half].astype(F32) + packed[half:].astype(F32)


class Reduction:
    def __init__(self, send, order):
        self.send, self.order = send, order
        self.count = lax.axis_size("dp").bit_length() - 1
        self.bits = [*order, *range(len(order), self.count), *reversed(order)]
        self.values, self.small, self.came, self.at = None, None, None, 0

    def take(self, *earlier):
        self.came = swap(self.send, "dp", 1 << self.bits[self.at])
        if earlier:
            self.came = after(self.came, *earlier)
        return self.came

    def arrive(self, *earlier):
        if self.came is None:
            self.take()
        arrived = after(self.came, *earlier)
        self.came = None
        self.at += 1
        halving = len(self.order)
        if self.at < halving:
            dims = (self.values.shape[0] // 2, self.values.shape[1])
            leave(self.values)
            self.send, self.values = run(
                add_halves,
                (jnp.zeros((1,), jnp.int32), self.values, arrived),
                [shape(dims, BF), shape(dims)],
            )
            stay(self.values)
        elif self.at == halving:
            leave(self.values)
            self.values = add_round(self.values, arrived)
            self.send = self.values
        elif self.at <= self.count:
            self.values = (self.values.astype(F32) + arrived.astype(F32)).astype(BF)
            self.send = self.values
        else:
            rows = self.values.shape[0]
            if self.small is not None:
                self.small = pack(unpack(self.small) + unpack(arrived[rows:]))
            if self.at == len(self.bits):
                self.parts = (self.values, arrived)
                return arrived
            self.values = jnp.concatenate([self.values, arrived[:rows]], axis=0)
            self.send = self.values
            if self.small is not None:
                self.send = jnp.concatenate([self.values, self.small], axis=0)
        return self.send

    def join(self, small):
        for bit in range(len(self.order), self.count):
            small = pack(unpack(small) + unpack(swap(small, "dp", 1 << bit)))
        self.small = small
        self.send = jnp.concatenate([self.values, small], axis=0)


ORDER_A = (0, 1, 2)
ORDER_B = (1, 0, 2)


def weight_grad(me, lefts, rights, order, kept, low=0, wide=None):
    half = lefts[0].shape[1] // 2
    wide = wide or rights[0].shape[1]
    count = (len(lefts), len(rights))
    return run(
        functools.partial(weight_pieces, order, 0 if kept else PIECES // 2, low, count),
        (me, *lefts, *rights),
        [shape((half, wide), F32 if kept else BF)],
        scratch=[pltpu.VMEM((half, x.shape[0]), BF) for x in lefts],
        flops=2 * 960 * half * wide,
    )[0]


def mixed_grad(me, normed, proj, heads, mids, order, kept, low):
    half = normed[0].shape[1] // 2
    wide = proj[0].shape[1] - low + heads[0].shape[1]
    return run(
        functools.partial(mixed_pieces, order, 0 if kept else PIECES // 2, low),
        (me, *normed, *proj, *heads, *mids),
        [shape((half, wide), F32 if kept else BF)],
        scratch=[pltpu.VMEM((half, x.shape[0]), BF) for x in normed],
        flops=2 * 960 * half * wide,
    )[0]


def place(me, parts, order):
    rows, wide = 2 * parts[0].shape[0], parts[0].shape[1]
    return run_out(
        functools.partial(place_pieces, order),
        (me, *parts),
        [shape((rows, wide))],
        scratch=[
            pltpu.VMEM((PIECES, rows // PIECES, wide), F32),
            pltpu.SemaphoreType.DMA((PIECES,)),
        ],
    )[0]


def on_device(
    tokens,
    keep_mask,
    grad_out,
    in_weight,
    in_bias,
    out_weight,
    out_bias,
    up_weight,
    up_bias,
    down_weight,
    down_bias,
    gain_one,
    shift_one,
    gain_two,
    shift_two,
):
    rows, model = tokens.shape
    leave(*STAY)
    me = jnp.stack([lax.axis_index("tensor"), lax.axis_index("dp")]).astype(jnp.int32)
    images = keep_mask.shape[0]
    heads = in_weight.shape[1] // (3 * HD)
    width = heads * HD
    hidden = up_weight.shape[1]

    def line(values):
        return values.reshape(1, -1)

    side = 2 * rows
    block = 256
    project_flops = 2 * side * model * 3 * width
    attend_flops = 3 * heads * 4 * HALF * SLOTS * 128 + 2 * side * width * model
    back_flops = 3 * heads * 10 * HALF * SLOTS * 128 + 2 * side * width * model

    def act_grad_of(one, other):
        return run(
            act_back,
            (me, one, other, down_weight),
            [shape((side, hidden))],
            flops=2 * side * model * hidden,
        )[0]

    def feed(norms, act_grad, low, kinds):
        tall = rows * len(norms)
        return run(
            functools.partial(feed_forward, low, len(norms)),
            (me, *norms, up_weight, vectors, act_grad),
            [
                shape((tall, hidden), BF),
                shape((tall, hidden), BF),
                shape((1, hidden)),
                *[shape((rows, model), kind) for kind in kinds],
            ],
            scratch=[pltpu.VMEM((tall, model), F32), pltpu.VMEM((2, rows, block), F32)],
            flops=4 * tall * model * hidden,
        )

    def feed_back(me, *acts):
        return run(
            functools.partial(feed_out, len(acts)),
            (me, *acts, down_weight),
            [shape((rows, model), BF), shape((rows, model))],
            flops=2 * side * model * hidden,
        )

    tok_far = swap(tokens, "tensor", 2)
    tok_core = swap(tokens, "tensor", 1)
    keep_flat = keep_mask.reshape(-1).astype(F32)
    keep_own = lax.dynamic_slice_in_dim(keep_flat, me[0] * rows, rows)[:, None]
    cot = (grad_out.astype(F32) * keep_own).astype(BF)
    cot_core = swap(cot, "tensor", 1)
    pair = in_bias.reshape(heads, 2, HD)
    bias_full = jnp.concatenate([pair[:, :1], jnp.zeros((heads, 1, HD), F32), pair[:, 1:]], axis=1)
    bias_full = bias_full.reshape(1, 3 * width)
    vectors = jnp.stack(
        [gain_one, shift_one, out_bias, gain_two, shift_two, up_bias, down_bias, down_bias]
    )
    stay(in_weight, bias_full, vectors, tokens, cot)
    norm_near, proj_near = run(
        project_local,
        (me, tokens, tok_core, vectors, in_weight, bias_full),
        [shape((side, model), BF), shape((side, 3 * width), BF)],
        flops=project_flops,
    )
    stay(norm_near, out_weight)
    tok_far = after(tok_far, proj_near)

    tok_both = swap(tok_far, "tensor", 1)
    cot_far = swap(after(cot, tok_far), "tensor", 2)
    attend_outs = [
        shape((3 * heads, HALF, SLOTS), BF),
        shape((side, width), BF),
        shape((rows, model), BF),
        shape((rows, model), F32),
    ]
    norm_y, proj_y = run(
        project_one,
        (me, tok_far, vectors, in_weight, bias_full),
        [shape((rows, model), BF), shape((rows, 3 * width), BF)],
        flops=project_flops // 2,
    )
    stay(norm_y)
    norm_both, qkv, probs_far, heads_far, send, far_hold = run(
        attend_far,
        (
            me, proj_near, proj_y, tok_both, vectors, in_weight, bias_full, keep_mask, out_weight,
        ),
        [shape((rows, model), BF), shape((2 * side, 3 * width), BF), *attend_outs],
        flops=project_flops + attend_flops,
    )
    stay(norm_both, qkv, probs_far, heads_far, down_weight, up_weight)
    leave(bias_full)
    arrived = after(swap(send, "tensor", 1), cot_far)
    far_sum = add_round(far_hold, arrived)
    cot_far = after(cot_far, far_sum)
    cot_both = swap(cot_far, "tensor", 1)
    arrived_far = swap(far_sum, "tensor", 2)
    probs_near, heads_near, send, hold = run(
        attend_near,
        (after(me, far_sum), qkv, keep_mask, out_weight),
        attend_outs,
        flops=attend_flops,
    )
    stay(probs_near, heads_near, hold)
    act_grad_near = act_grad_of(cot, cot_core)
    stay(act_grad_near, cot_core)
    arrived_near = after(swap(send, "tensor", 1), arrived_far)
    middle, second = run(
        second_norm,
        (
            after(me, act_grad_near), tokens, hold, arrived_near, arrived_far, vectors,
        ),
        [shape((rows, model)), shape((rows, model), BF)],
    )

    leave(hold)
    stay(middle, second)

    second_far = swap(second, "tensor", 2)
    second_core = swap(second, "tensor", 1)
    act_near, pre_near, up_bias_near, near_hold, near_send = feed(
        (second, second_core), act_grad_near, 0, (F32, BF)
    )
    leave(act_grad_near)
    stay(act_near, pre_near, near_hold, second_core)
    act_grad_far = act_grad_of(cot_far, cot_both)
    stay(cot_far, cot_both, act_grad_far)
    second_far = after(second_far, act_grad_far)
    second_both = swap(second_far, "tensor", 1)
    act_y, pre_y, up_bias_y, far_hold = feed((second_far,), act_grad_far, 0, (F32,))
    stay(act_y, pre_y, second_far, far_hold)
    act_both, pre_both, up_bias_both, far_send = feed((second_both,), act_grad_far, rows, (BF,))
    leave(far_hold)
    far_sum = add_round(far_hold, swap(far_send, "tensor", 1))
    arrived_far = swap(far_sum, "tensor", 2)
    leave(act_grad_far, up_weight)
    stay(act_both, pre_both, second_both)
    acts, cots = (act_near, act_y, act_both), (cot, cot_core, cot_far, cot_both)
    down_send = weight_grad(after(me, far_sum), acts, cots, ORDER_A, False)
    down = Reduction(down_send, ORDER_A)
    seconds = (second, second_core, second_far, second_both)
    pres = (pre_near, pre_y, pre_both)
    up_send = weight_grad(after(me, down_send), seconds, pres, ORDER_B, False)
    up = Reduction(up_send, ORDER_B)
    arrived_near = swap(near_send, "tensor", 1)
    feed_send, feed_hold = feed_back(after(me, up_send), act_y, act_both)
    feed_far = add_round(feed_hold, swap(feed_send, "tensor", 1))
    middle_grad, middle_low, middle_sums = run(
        middle_back,
        (
            after(me, feed_hold), near_hold, arrived_near, arrived_far, middle, cot, vectors,
        ),
        [shape((rows, model)), shape((rows, model), BF), shape((4, model))],
        scratch=[pltpu.VMEM((4, 8, model), F32)],
    )

    mid_far = swap(middle_low, "tensor", 2)
    mid_core = swap(middle_low, "tensor", 1)
    grads = pltpu.VMEM((side, width), BF)
    leave(near_hold)
    stay(middle_grad, middle_low)
    down.values = weight_grad(after(me, middle_low), acts, cots, ORDER_A, True)
    leave(act_y, act_both, cot_core, cot_far, cot_both)
    stay(down.values)
    near_q, near_keys = run(
        back_near,
        (after(me, down.values), middle_low, mid_core, qkv, probs_near, out_weight),
        [shape((side, width)), shape((2 * side, 2 * width))],
        scratch=[grads],
        flops=back_flops,
    )
    leave(probs_near)
    stay(near_q, near_keys, mid_core)
    up.values = weight_grad(after(me, near_q), seconds, pres, ORDER_B, True)
    leave(second, second_core, second_far, second_both, pre_near, pre_y, pre_both)
    stay(up.values)
    mid_far = after(mid_far, up.values)
    mid_both = swap(mid_far, "tensor", 1)
    feed_far = swap(after(feed_far, mid_far), "tensor", 2)
    down.arrive(mid_far)
    up.arrive(mid_far)
    flat_near, flat_far, bias_grad, far_send, far_hold = run(
        back_far,
        (
            after(me, down.send, up.send), mid_far, mid_both, qkv, probs_far,
            out_weight, near_q, near_keys, in_weight,
        ),
        [
            shape((side, 3 * width), BF),
            shape((side, 3 * width), BF),
            shape((1, 2 * width)),
            shape((rows, model), BF),
            shape((rows, model)),
        ],
        scratch=[
            grads,
            pltpu.VMEM((side, width), F32),
            pltpu.VMEM((2 * side, 2 * width), F32),
            pltpu.VMEM((side, 3 * width), BF),
        ],
        flops=back_flops + project_flops,
    )
    leave(qkv, probs_far, near_q, near_keys, out_weight)
    stay(flat_near, flat_far, mid_far, mid_both)
    down.take(bias_grad)
    up.take(bias_grad)
    arrived = after(swap(far_send, "tensor", 1), feed_far, down.came, up.came)
    far_sum = add_round(far_hold, arrived)
    arrived_far = swap(far_sum, "tensor", 2)

    down.arrive(far_sum)
    up.arrive(far_sum)
    near_send, hold = run(
        first_back,
        (after(me, down.send, up.send), flat_near, in_weight),
        [shape((rows, model), BF), shape((rows, model))],
        flops=project_flops,
    )
    leave(in_weight)
    stay(hold)
    normed = (norm_near, norm_y, norm_both)
    split = (3 * width + width) // 2
    flat = (flat_near, flat_far)
    head_rows = (heads_near, heads_far)
    mids = (middle_low, mid_core, mid_far, mid_both)
    arrived_near = swap(near_send, "tensor", 1)
    first_send = weight_grad(after(me, hold), normed, flat, ORDER_A, False, 0, split)
    first = Reduction(first_send, ORDER_A)
    mixed_send = mixed_grad(
        after(me, first_send), normed, flat, head_rows, mids, ORDER_B, False, split
    )
    mixed = Reduction(mixed_send, ORDER_B)
    first.values = weight_grad(after(me, mixed_send), normed, flat, ORDER_A, True, 0, split)
    stay(first.values)
    mixed.values = mixed_grad(
        after(me, first.values), normed, flat, head_rows, mids, ORDER_B, True, split
    )
    leave(norm_near, norm_y, norm_both, flat_near, flat_far, heads_near, heads_far)
    leave(middle_low, mid_core, mid_far, mid_both)
    stay(mixed.values)
    tokens_grad, token_sums = run(
        token_back,
        (
            after(me, mixed.values), hold, arrived_near, arrived_far, tokens, middle_grad, vectors,
        ),
        [shape((rows, model)), shape((2, model))],
        scratch=[pltpu.VMEM((2, 8, model), F32)],
    )
    leave(hold, tokens, middle_grad, vectors)
    feed_send, feed_hold = feed_back(after(me, token_sums), act_near)
    feed_rows = feed_hold + swap(feed_send, "tensor", 1).astype(F32) + feed_far.astype(F32)
    output = (keep_own * (middle + feed_rows + down_bias)).astype(BF)
    leave(*STAY)
    stay(down.values, up.values, first.values, mixed.values)

    now = down.arrive(feed_hold)
    now = first.arrive(now)
    shared = pack(jnp.concatenate([middle_sums, token_sums], axis=0))
    shared = add_small(shared, swap(shared, "tensor", 1))
    shared = unpack(add_small(shared, swap(shared, "tensor", 2)))
    own = jnp.concatenate(
        [up_bias_near + up_bias_y + up_bias_both, jnp.pad(bias_grad, ((0, 0), (0, hidden - 2 * width)))], axis=0
    )
    small = jnp.concatenate([shared, own], axis=0)
    small = pack(jnp.concatenate([small[:, :split], small[:, split:]], axis=0))
    now = mixed.arrive(now)
    now = up.arrive(now)
    now = down.arrive(now)
    now = mixed.arrive(now)
    now = first.arrive(now)
    now = up.arrive(now)
    now = down.arrive(now)
    now = mixed.arrive(now)
    now = first.arrive(now)
    while first.at < first.count:
        now = first.arrive(now)
    first.join(small)
    now = mixed.arrive(now)
    now = first.arrive(now)
    now = up.arrive(now)
    last = [mixed, first, down, up]
    while any(x.at < len(x.bits) for x in last):
        for x in last:
            if x.at < len(x.bits):
                now = x.arrive(now)
    small = unpack(first.small)
    small = jnp.concatenate([small[:8], small[8:]], axis=1)
    piece = model // PIECES
    down_sum = place(me, down.parts, ORDER_A)
    up_sum = place(me, up.parts, ORDER_B)
    in_sum, out_sum = run_out(
        functools.partial(place_mixed, ORDER_A, ORDER_B),
        (me, *first.parts, *mixed.parts),
        [shape((model, 3 * width)), shape((width, model))],
        scratch=[
            pltpu.VMEM((PIECES, piece, 3 * width), F32),
            pltpu.VMEM((PIECES, width, piece), F32),
            pltpu.SemaphoreType.DMA((3 * PIECES,)),
        ],
    )
    in_bias_sum = small[7, : 2 * width].reshape(2, heads, HD).transpose(1, 0, 2).reshape(-1)
    return (
        output,
        tokens_grad,
        in_sum,
        in_bias_sum,
        out_sum,
        small[0],
        up_sum,
        small[6],
        down_sum,
        small[1],
        small[4],
        small[5],
        small[2],
        small[3],
    )


def solution(mesh):
    rows = P(("dp", "tensor"), None)
    placed = (
        rows,
        P("dp", None),
        rows,
        P(None, "tensor"),
        P("tensor"),
        P("tensor", None),
        P(),
        P(None, "tensor"),
        P("tensor"),
        P("tensor", None),
        P(),
        P(),
        P(),
        P(),
        P(),
    )
    given = (
        rows,
        rows,
        P(None, "tensor"),
        P("tensor"),
        P("tensor", None),
        P(),
        P(None, "tensor"),
        P("tensor"),
        P("tensor", None),
        P(),
        P(),
        P(),
        P(),
        P(),
    )
    return jax.shard_map(on_device, mesh=mesh, in_specs=placed, out_specs=given, check_vma=False)
```

```python
import functools

import jax
import jax.numpy as jnp
from jax import lax
from jax.experimental import pallas as pl
from jax.experimental.pallas import tpu as pltpu
from jax.sharding import PartitionSpec as P

HD = 64
SLOTS = 320
HALF = SLOTS // 2
PIECES = 8
EPSILON = 1e-06
BF = jnp.bfloat16
F32 = jnp.float32
MIB = 1 << 20


def mm(left, right, dims=((1,), (0,))):
    return lax.dot_general(left, right, (dims, ((), ())), preferred_element_type=F32)


NT = ((1,), (1,))
TN = ((0,), (0,))


def swap(values, axis, bit):
    count = lax.axis_size(axis)
    return lax.ppermute(values, axis, [(i, i ^ bit) for i in range(count)])


def after(values, *earlier):
    return lax.optimization_barrier((values, *earlier))[0]


def shape(dims, kind=F32):
    return jax.ShapeDtypeStruct(dims, kind)


STAY = []


def stay(*arrays):
    STAY.extend(arrays)


def leave(*arrays):
    for array in arrays:
        STAY[:] = [x for x in STAY if x is not array]


def run(body, operands, outs, scratch=(), flops=0, room=12):
    used = list(operands[1:])
    waiting = [x for x in STAY if all(x is not y for y in used)]
    ins = [pltpu.with_memory_space_constraint(x, pltpu.VMEM) for x in [*used, *waiting]]
    moved = sum(x.size * x.dtype.itemsize for x in [*used, *outs])

    def kernel(*refs):
        own = 1 + len(used)
        body(*refs[:own], *refs[own + len(waiting) :])

    return pl.pallas_call(
        kernel,
        out_shape=[pltpu.VMEM(x.shape, x.dtype) for x in outs],
        in_specs=[pl.BlockSpec(memory_space=pltpu.SMEM)]
        + [pl.BlockSpec(memory_space=pltpu.VMEM)] * len(ins),
        out_specs=[pl.BlockSpec(memory_space=pltpu.VMEM)] * len(outs),
        scratch_shapes=scratch,
        compiler_params=pltpu.CompilerParams(vmem_limit_bytes=room * MIB),
        cost_estimate=pl.CostEstimate(
            flops=int(flops * WEIGHT), bytes_accessed=0, transcendentals=0
        ),
    )(operands[0], *ins)


WEIGHT = 20


def add_low(me, left, right, out):
    out[...] = (left[...] + right[...].astype(F32)).astype(BF)


def add_round(left, right):
    return run(add_low, (jnp.zeros((1,), jnp.int32), left, right), [shape(left.shape, BF)])[0]


def add_halves(me, left, right, send, hold):
    middle = send.shape[0]
    send[...] = (left[middle:, :] + right[middle:, :].astype(F32)).astype(BF)
    hold[...] = left[:middle, :] + right[:middle, :].astype(F32)


def run_out(body, operands, outs, scratch=(), room=16):
    ins = [pltpu.with_memory_space_constraint(x, pltpu.VMEM) for x in operands[1:]]
    return pl.pallas_call(
        body,
        out_shape=[pltpu.HBM(x.shape, x.dtype) for x in outs],
        in_specs=[pl.BlockSpec(memory_space=pltpu.SMEM)]
        + [pl.BlockSpec(memory_space=pltpu.VMEM)] * len(ins),
        out_specs=[pl.BlockSpec(memory_space=pltpu.HBM)] * len(outs),
        scratch_shapes=scratch,
        compiler_params=pltpu.CompilerParams(vmem_limit_bytes=room * MIB),
        cost_estimate=pl.CostEstimate(
            flops=int(1e9 * WEIGHT), bytes_accessed=0, transcendentals=0
        ),
    )(operands[0], *ins)


def blocks(count, size, step):
    def one(i, carry):
        step(pl.ds(pl.multiple_of(i * size, size), size), i)
        return carry

    lax.fori_loop(0, count, one, 0)


def row_tiles(rows, size, step):
    def one(i, carry):
        step(pl.ds(pl.multiple_of(i * size, size), size))
        return carry

    lax.fori_loop(0, rows // size, one, 0)


def normalise(values):
    average = jnp.mean(values, axis=-1, keepdims=True)
    centred = values - average
    factor = lax.rsqrt(jnp.mean(centred * centred, axis=-1, keepdims=True) + EPSILON)
    return centred * factor, factor


def norm_back(grad, gain, z, factor):
    s = grad * gain
    return factor * (
        s - jnp.mean(s, axis=-1, keepdims=True) - z * jnp.mean(s * z, axis=-1, keepdims=True)
    )


def fold(values):
    return functools.reduce(
        lambda a, b: a + b, [values[i : i + 8] for i in range(0, values.shape[0], 8)]
    )


GAIN_ONE, SHIFT_ONE, OUT_BIAS, GAIN_TWO, SHIFT_TWO, UP_BIAS, DOWN_BIAS = range(7)


def row(vectors, number):
    return vectors[number : number + 1, :]


def project_side(blocks, vectors, weight, bias, normed, put):
    rows = blocks[0].shape[0]
    width = weight.shape[1] // 3
    for i, block in enumerate(blocks):

        def step(at, block=block, i=i):
            z, _ = normalise(block[at, :].astype(F32))
            tile = pl.ds(pl.multiple_of(at.start + i * rows, 16), at.size)
            normed[tile, :] = (z * row(vectors, GAIN_ONE) + row(vectors, SHIFT_ONE)).astype(BF)

        row_tiles(rows, 48, step)
        found = (mm(normed[i * rows : (i + 1) * rows, :], weight[...]) + bias[...]).astype(BF)
        kinds = [
            [found[:, (3 * head + kind) * HD :][:, :HD] for head in range(width // HD)]
            for kind in range(3)
        ]
        put(i, jnp.concatenate(sum(kinds, []), axis=1))


def project_local(me, tok_a, tok_b, vectors, weight, bias, normed, proj):
    rows = tok_a.shape[0]

    def put(i, values):
        proj[i * rows : (i + 1) * rows, :] = values

    project_side((tok_a, tok_b), vectors, weight, bias, normed, put)


def attend(side, qkv, keep, probs, heads_out):
    half_lane = lax.broadcasted_iota(jnp.int32, (1, 2 * HD), 1) // HD
    width = qkv.shape[1] // 3

    def one(j, carry):
        place = 3 * side + j
        image = place // 2
        queries = pl.ds(pl.multiple_of(place * HALF, 16), HALF)
        keys = pl.ds(pl.multiple_of(image * SLOTS, 16), SLOTS)
        live = keep[pl.ds(image, 1), :] > 0
        for pair in range(width // (2 * HD)):
            lanes = pl.ds(pair * 2 * HD, 2 * HD)
            q = qkv[queries, lanes] * 0.125
            k = qkv[keys, pl.ds(width + pair * 2 * HD, 2 * HD)]
            v = qkv[keys, pl.ds(2 * width + pair * 2 * HD, 2 * HD)]
            outs = []
            for e in range(2):
                scores = mm(jnp.where(half_lane == e, q, jnp.zeros_like(q)), k, NT)
                scores = jnp.where(live, scores, -1000000000.0)
                power = jnp.exp(scores - jnp.max(scores, axis=-1, keepdims=True))
                p = (power / jnp.sum(power, axis=-1, keepdims=True)).astype(BF)
                probs[j * 4 + pair * 2 + e] = p
                outs.append(mm(p, v))
            heads_out[pl.ds(pl.multiple_of(j * HALF, 16), HALF), lanes] = jnp.where(
                half_lane == 0, outs[0], outs[1]
            ).astype(BF)
        return carry

    lax.fori_loop(0, 3, one, 0)


def out_project(core, heads_out, weight, send, hold):
    rows = send.shape[0]
    send[...] = mm(
        heads_out[pl.ds(pl.multiple_of((1 - core) * rows, 16), rows), :], weight[...]
    ).astype(BF)
    hold[...] = mm(heads_out[pl.ds(pl.multiple_of(core * rows, 16), rows), :], weight[...])


def project_one(me, tok, vectors, weight, bias, normed, proj):
    def put(i, values):
        proj[...] = values

    project_side((tok,), vectors, weight, bias, normed, put)


def attend_far(
    me, near, first, tok, vectors, weight, bias, keep, out_w,
    normed, qkv, probs, heads_out, send, hold,
):
    rows = tok.shape[0]
    core, far = me[0] & 1, me[0] >> 1
    for i in range(2):
        at = pl.multiple_of((2 * far + (core ^ i)) * rows, 16)
        qkv[pl.ds(at, rows), :] = near[i * rows : (i + 1) * rows, :]
    at = pl.multiple_of((2 * (1 - far) + core) * rows, 16)
    qkv[pl.ds(at, rows), :] = first[...]

    def put(i, values):
        at = pl.multiple_of((2 * (1 - far) + (1 - core)) * rows, 16)
        qkv[pl.ds(at, rows), :] = values

    project_side((tok,), vectors, weight, bias, normed, put)
    attend(1 - far, qkv, keep, probs, heads_out)
    out_project(core, heads_out, out_w, send, hold)


def attend_near(me, qkv, keep, out_w, probs, heads_out, send, hold):
    core, far = me[0] & 1, me[0] >> 1
    attend(far, qkv, keep, probs, heads_out)
    out_project(core, heads_out, out_w, send, hold)


def second_norm(me, tok, hold, near, far, vectors, middle, second):
    def step(at):
        total = hold[at, :] + near[at, :].astype(F32) + far[at, :].astype(F32)
        values = tok[at, :].astype(F32) + total + row(vectors, OUT_BIAS)
        middle[at, :] = values
        z, _ = normalise(values)
        second[at, :] = (z * row(vectors, GAIN_TWO) + row(vectors, SHIFT_TWO)).astype(BF)

    row_tiles(tok.shape[0], 48, step)


def act_back(me, cot_a, cot_b, down, act_grad):
    rows = cot_a.shape[0]

    def step(at, i):
        act_grad[:rows, at] = mm(cot_a[...], down[at, :], NT)
        act_grad[rows:, at] = mm(cot_b[...], down[at, :], NT)

    blocks(down.shape[0] // 256, 256, step)


def feed_forward(low, count, me, *refs):
    norms = refs[:count]
    up, vectors, act_grad, act, pre_low, bias_grad = refs[count : count + 6]
    outs, total, pre = refs[count + 6 : 2 * count + 6], refs[-2], refs[-1]
    rows = norms[0].shape[0]
    wide = pre.shape[2]
    number = up.shape[1] // wide
    bias_grad[...] = jnp.zeros_like(bias_grad)
    total[...] = jnp.zeros_like(total)

    def columns(i):
        return pl.ds(pl.multiple_of(i * wide, wide), wide)

    def elements(slot, at, block):
        own_bias = vectors[UP_BIAS : UP_BIAS + 1, at]
        sums = None
        for i in range(0, rows, 16):
            to = pl.ds(block * rows + i, 16)
            x = pre[slot, i : i + 16, :] + own_bias
            share = 0.5 + 0.5 * lax.erf(x * 0.7071067811865476)
            slope = share + x * (0.3989422804014327 * jnp.exp(-0.5 * x * x))
            act[to, at] = (x * share).astype(BF)
            grad = act_grad[pl.ds(low + block * rows + i, 16), at] * slope
            pre_low[to, at] = grad.astype(BF)
            part = grad[:8] + grad[8:]
            sums = part if sums is None else sums + part
        bias_grad[:, at] += jnp.sum(sums, axis=0, keepdims=True)

    pre[0] = mm(norms[0][...], up[:, :wide])

    def one(i, carry):
        if count == 2:
            steps = ((i, 0), (i, 1), (jnp.minimum(i + 1, number - 1), 0))
        else:
            steps = ((2 * i, 0), (2 * i + 1, 0), (jnp.minimum(2 * i + 2, number - 1), 0))
        for slot in range(2):
            column, block = steps[slot]
            later, other = steps[slot + 1]
            pre[1 - slot] = mm(norms[other][...], up[:, columns(later)])
            elements(slot, columns(column), block)
            inside = pl.ds(block * rows, rows)
            total[inside, :] += mm(pre_low[inside, columns(column)], up[:, columns(column)], NT)
        return carry

    lax.fori_loop(0, number * count // 2, one, 0)
    for i, out in enumerate(outs):
        out[...] = total[i * rows : (i + 1) * rows, :].astype(out.dtype)


def feed_out(count, me, *refs):
    acts, (down, send, hold) = refs[:count], refs[count:]
    rows = send.shape[0]
    one = acts[-1][rows:, :] if count == 1 else acts[1][...]
    send[...] = mm(one, down[...]).astype(BF)
    hold[...] = mm(acts[0][:rows, :], down[...])


def gather_pieces(me, lefts, order, base, turned):
    piece = lefts[0].shape[1] // PIECES
    for i in range(PIECES // 2):
        at = pl.ds(pl.multiple_of(piece_of(base + i, order, me[1]) * piece, piece), piece)
        for left, to in zip(lefts, turned, strict=True):
            to[i * piece : (i + 1) * piece, :] = left[:, at].T


def segments(lefts, rights):
    found, left, right, a, b = [], 0, 0, 0, 0
    while left < len(lefts):
        rows = min(lefts[left].shape[0] - a, rights[right].shape[0] - b)
        found.append((left, a, right, b, rows))
        a, b = a + rows, b + rows
        if a == lefts[left].shape[0]:
            left, a = left + 1, 0
        if b == rights[right].shape[0]:
            right, b = right + 1, 0
    return found


def weight_pieces(order, base, low, count, me, *refs):
    lefts, rights = refs[: count[0]], refs[count[0] : sum(count)]
    out, turned = refs[sum(count)], refs[sum(count) + 1 :]
    gather_pieces(me, lefts, order, base, turned)

    def step(at, i):
        found = None
        from_ = pl.ds(pl.multiple_of(at.start + low, 128), at.size)
        for left, a, right, b, rows in segments(lefts, rights):
            part = mm(turned[left][:, a : a + rows], rights[right][b : b + rows, from_])
            found = part if found is None else found + part
        out[:, at] = found.astype(out.dtype)

    blocks(out.shape[1] // 256, 256, step)


def mixed_pieces(order, base, low, me, *refs):
    lefts, rights, heads, mids, out = refs[:3], refs[3:5], refs[5:7], refs[7:11], refs[11]
    turned = refs[12:]
    gather_pieces(me, lefts, order, base, turned)
    width = rights[0].shape[1] - low
    for at in range(0, width, 256):
        found = None
        for left, a, right, b, rows in segments(lefts, rights):
            part = mm(
                turned[left][:, a : a + rows],
                rights[right][b : b + rows, low + at : low + at + 256],
            )
            found = part if found is None else found + part
        out[:, at : at + 256] = found.astype(out.dtype)
    core = me[0] & 1
    rows = mids[0].shape[0]
    piece = mids[0].shape[1] // PIECES
    half = heads[0].shape[1] // 2
    for i in range(PIECES // 2):
        at = pl.ds(pl.multiple_of(piece_of(base + i, order, me[1]) * piece, piece), piece)
        both = None
        for k in range(4):
            inside = pl.ds(pl.multiple_of((core ^ (k % 2)) * rows, 16), rows)
            part = mm(heads[k // 2][inside, :], mids[k][:, at], TN)
            both = part if both is None else both + part
        to = pl.ds(i * piece, piece)
        out[to, width : width + half] = both[:half].astype(out.dtype)
        out[to, width + half :] = both[half:].astype(out.dtype)


def middle_back(me, hold, near, far, middle, cot_low, vectors, middle_grad, middle_low, sums, parts):
    parts[...] = jnp.zeros_like(parts)

    def step(at):
        second = hold[at, :] + near[at, :].astype(F32) + far[at, :].astype(F32)
        z, factor = normalise(middle[at, :])
        cot = cot_low[at, :].astype(F32)
        total = cot + norm_back(second, row(vectors, GAIN_TWO), z, factor)
        middle_grad[at, :] = total
        middle_low[at, :] = total.astype(BF)
        parts[0] += fold(total)
        parts[1] += fold(cot)
        parts[2] += fold(second * z)
        parts[3] += fold(second)

    row_tiles(hold.shape[0], 48, step)
    for i in range(4):
        sums[i : i + 1, :] = jnp.sum(parts[i], axis=0, keepdims=True)


def attend_back(side, mid_blocks, core, qkv, probs, out_w, grads, pg_q, keys_grad):
    rows = mid_blocks[0].shape[0]
    half_lane = lax.broadcasted_iota(jnp.int32, (1, 2 * HD), 1) // HD
    width = qkv.shape[1] // 3
    for i, block in enumerate(mid_blocks):
        at = pl.multiple_of((core ^ i) * rows, 16)
        grads[pl.ds(at, rows), :] = mm(block[...], out_w[...], NT).astype(BF)

    def one(j, carry):
        place = 3 * side + j
        image = place // 2
        inside = pl.ds(pl.multiple_of(j * HALF, 16), HALF)
        queries = pl.ds(pl.multiple_of(place * HALF, 16), HALF)
        keys = pl.ds(pl.multiple_of(image * SLOTS, 16), SLOTS)
        for pair in range(width // (2 * HD)):
            lanes = pl.ds(pair * 2 * HD, 2 * HD)
            q = qkv[queries, lanes]
            k = qkv[keys, pl.ds(width + pair * 2 * HD, 2 * HD)]
            v = qkv[keys, pl.ds(2 * width + pair * 2 * HD, 2 * HD)]
            g = grads[inside, lanes]
            found = []
            for e in range(2):
                p = probs[j * 4 + pair * 2 + e]
                wide = p.astype(F32)
                prob_grad = mm(jnp.where(half_lane == e, g, jnp.zeros_like(g)), v, NT)
                delta = jnp.sum(wide * prob_grad, axis=-1, keepdims=True)
                score_grad = (wide * (prob_grad - delta) * 0.125).astype(BF)
                found.append(
                    (mm(score_grad, k), mm(score_grad, q, TN), mm(p, g, TN))
                )
            q_grad, k_grad, v_grad = (
                jnp.where(half_lane == 0, a, b) for a, b in zip(*found, strict=True)
            )
            pg_q[inside, lanes] = q_grad
            keys_grad[keys, lanes] += k_grad
            keys_grad[keys, pl.ds(width + pair * 2 * HD, 2 * HD)] += v_grad
        return carry

    lax.fori_loop(0, 3, one, 0)


def back_near(me, mid_a, mid_b, qkv, probs, out_w, pg_q, keys_grad, grads):
    core, far = me[0] & 1, me[0] >> 1
    keys_grad[...] = jnp.zeros_like(keys_grad)
    attend_back(far, (mid_a, mid_b), core, qkv, probs, out_w, grads, pg_q, keys_grad)


def back_far(
    me, mid_a, mid_b, qkv, probs, out_w, near_q, near_keys, in_w,
    flat_near, flat_far, bias_grad, send, hold, grads, far_q, keys_grad, group,
):
    core, far = me[0] & 1, me[0] >> 1
    rows = mid_a.shape[0]
    width = far_q.shape[1]
    keys_grad[...] = near_keys[...]
    attend_back(1 - far, (mid_a, mid_b), core, qkv, probs, out_w, grads, far_q, keys_grad)
    bias_grad[...] = jnp.concatenate(
        [
            jnp.sum(far_q[...], axis=0, keepdims=True) + jnp.sum(near_q[...], axis=0, keepdims=True),
            jnp.sum(keys_grad[:, width:], axis=0, keepdims=True),
        ],
        axis=1,
    )
    for side, (flat, q_part) in enumerate(((flat_near, near_q), (flat_far, far_q))):
        for i in range(2):
            inside = pl.multiple_of((core ^ i) * rows, 16)
            place = pl.multiple_of((2 * (far ^ side) + (core ^ i)) * rows, 16)
            to = pl.ds(i * rows, rows)
            group[to, :width] = q_part[pl.ds(inside, rows), :].astype(BF)
            group[to, width:] = keys_grad[pl.ds(place, rows), :].astype(BF)
        for head in range(width // HD):
            for kind in range(3):
                at = (head * 3 + kind) * HD
                flat[:, at : at + HD] = group[:, kind * width + head * HD :][:, :HD]
    send[...] = mm(flat_far[rows:, :], in_w[...], NT).astype(BF)
    hold[...] = mm(flat_far[:rows, :], in_w[...], NT)


def first_back(me, proj, in_w, send, hold):
    rows = send.shape[0]
    send[...] = mm(proj[rows:, :], in_w[...], NT).astype(BF)
    hold[...] = mm(proj[:rows, :], in_w[...], NT)


def mixed_piece(me, norm_a, norm_b, proj_a, proj_b, heads_a, heads_b, mid_a, mid_b, out):
    width = proj_a.shape[1]
    out[:, :width] = (
        mm(norm_a[...], proj_a[...], TN) + mm(norm_b[...], proj_b[...], TN)
    ).astype(out.dtype)
    both = mm(heads_a[...], mid_a[...], TN) + mm(heads_b[...], mid_b[...], TN)
    half = both.shape[0] // 2
    out[:, width : width + half] = both[:half].astype(out.dtype)
    out[:, width + half :] = both[half:].astype(out.dtype)


def token_back(me, hold, near, far, tok, middle_grad, vectors, tokens_grad, sums, parts):
    parts[...] = jnp.zeros_like(parts)

    def step(at):
        first = hold[at, :] + near[at, :].astype(F32) + far[at, :].astype(F32)
        z, factor = normalise(tok[at, :].astype(F32))
        tokens_grad[at, :] = middle_grad[at, :] + norm_back(
            first, row(vectors, GAIN_ONE), z, factor
        )
        parts[0] += fold(first * z)
        parts[1] += fold(first)

    row_tiles(hold.shape[0], 48, step)
    for i in range(2):
        sums[i : i + 1, :] = jnp.sum(parts[i], axis=0, keepdims=True)


def place_pieces(order, me, *refs):
    parts, out, wide, sems = refs[:-3], refs[-3], refs[-2], refs[-1]
    piece = out.shape[0] // PIECES
    copies = []
    for i in range(PIECES):
        part, row = locate(parts, i * piece)
        wide[i] = part[row : row + piece, :].astype(F32)
        to = pl.ds(pl.multiple_of(piece_of(i, order, me[1]) * piece, piece), piece)
        copies.append(pltpu.make_async_copy(wide.at[i], out.at[to, :], sems.at[i]))
        copies[-1].start()
    for copy in copies:
        copy.wait()


def locate(parts, row):
    for part in parts:
        if row < part.shape[0]:
            return part, row
        row -= part.shape[0]


def place_mixed(order, other, me, *refs):
    count = (len(refs) - 5) // 2
    first, second = refs[:count], refs[count : 2 * count]
    in_out, out_out, wide, flat, sems = refs[2 * count :]
    piece = in_out.shape[0] // PIECES
    half = out_out.shape[0] // 2
    split = first[0].shape[1]
    rest = in_out.shape[1] - split
    copies = []
    for i in range(PIECES):
        place = piece_of(i, order, me[1])
        to = pl.ds(pl.multiple_of(place * piece, piece), piece)
        part, row = locate(first, i * piece)
        wide[i, :, :split] = part[row : row + piece, :].astype(F32)
        copies.append(
            pltpu.make_async_copy(wide.at[i, :, :split], in_out.at[to, :split], sems.at[i])
        )
        copies[-1].start()
        place = piece_of(i, other, me[1])
        to = pl.ds(pl.multiple_of(place * piece, piece), piece)
        part, row = locate(second, i * piece)
        wide[i, :, split:] = part[row : row + piece, :rest].astype(F32)
        flat[i, :half, :] = part[row : row + piece, rest : rest + half].astype(F32)
        flat[i, half:, :] = part[row : row + piece, rest + half :].astype(F32)
        copies.append(
            pltpu.make_async_copy(wide.at[i, :, split:], in_out.at[to, split:], sems.at[PIECES + i])
        )
        copies[-1].start()
        copies.append(
            pltpu.make_async_copy(flat.at[i], out_out.at[:, to], sems.at[2 * PIECES + i])
        )
        copies[-1].start()
    for copy in copies:
        copy.wait()


def piece_of(position, order, me):
    relative = 0
    for step, bit in enumerate(order):
        relative = relative | (((position >> (len(order) - 1 - step)) & 1) << bit)
    return relative ^ (me & (PIECES - 1))


def pack(values):
    high = values.astype(BF)
    return jnp.concatenate([high, (values - high.astype(F32)).astype(BF)], axis=0)


def add_small(own, other):
    return pack(unpack(own) + unpack(other))


def unpack(packed):
    half = packed.shape[0] // 2
    return packed[:half].astype(F32) + packed[half:].astype(F32)


class Reduction:
    def __init__(self, send, order):
        self.send, self.order = send, order
        self.count = lax.axis_size("dp").bit_length() - 1
        self.bits = [*order, *range(len(order), self.count), *reversed(order)]
        self.values, self.small, self.came, self.at = None, None, None, 0

    def take(self, *earlier):
        self.came = swap(self.send, "dp", 1 << self.bits[self.at])
        if earlier:
            self.came = after(self.came, *earlier)
        return self.came

    def arrive(self, *earlier):
        found = self.step(*earlier)
        while len(self.order) <= self.at < self.count:
            found = self.step(found)
        return found

    def step(self, *earlier):
        if self.came is None:
            self.take()
        arrived = after(self.came, *earlier)
        self.came = None
        self.at += 1
        halving = len(self.order)
        if self.at < halving:
            dims = (self.values.shape[0] // 2, self.values.shape[1])
            leave(self.values)
            self.send, self.values = run(
                add_halves,
                (jnp.zeros((1,), jnp.int32), self.values, arrived),
                [shape(dims, BF), shape(dims)],
            )
            stay(self.values)
        elif self.at == halving:
            leave(self.values)
            self.values = add_round(self.values, arrived)
            self.send = self.values
        elif self.at <= self.count:
            self.values = (self.values.astype(F32) + arrived.astype(F32)).astype(BF)
            self.send = self.values
        else:
            rows = self.values.shape[0]
            if self.small is not None:
                self.small = pack(unpack(self.small) + unpack(arrived[rows:]))
            if self.at == len(self.bits):
                self.parts = (self.values, arrived)
                return arrived
            self.values = jnp.concatenate([self.values, arrived[:rows]], axis=0)
            self.send = self.values
            if self.small is not None:
                self.send = jnp.concatenate([self.values, self.small], axis=0)
        return self.send

    def join(self, small):
        for bit in range(len(self.order), self.count):
            small = pack(unpack(small) + unpack(swap(small, "dp", 1 << bit)))
        self.small = small
        self.send = jnp.concatenate([self.values, small], axis=0)


ORDER_A = (0, 1, 2)
ORDER_B = (1, 0, 2)


def weight_grad(me, lefts, rights, order, kept, low=0, wide=None):
    half = lefts[0].shape[1] // 2
    wide = wide or rights[0].shape[1]
    count = (len(lefts), len(rights))
    return run(
        functools.partial(weight_pieces, order, 0 if kept else PIECES // 2, low, count),
        (me, *lefts, *rights),
        [shape((half, wide), F32 if kept else BF)],
        scratch=[pltpu.VMEM((half, x.shape[0]), BF) for x in lefts],
        flops=2 * 960 * half * wide,
    )[0]


def mixed_grad(me, normed, proj, heads, mids, order, kept, low):
    half = normed[0].shape[1] // 2
    wide = proj[0].shape[1] - low + heads[0].shape[1]
    return run(
        functools.partial(mixed_pieces, order, 0 if kept else PIECES // 2, low),
        (me, *normed, *proj, *heads, *mids),
        [shape((half, wide), F32 if kept else BF)],
        scratch=[pltpu.VMEM((half, x.shape[0]), BF) for x in normed],
        flops=2 * 960 * half * wide,
    )[0]


def place(me, parts, order):
    rows, wide = 2 * parts[0].shape[0], parts[0].shape[1]
    return run_out(
        functools.partial(place_pieces, order),
        (me, *parts),
        [shape((rows, wide))],
        scratch=[
            pltpu.VMEM((PIECES, rows // PIECES, wide), F32),
            pltpu.SemaphoreType.DMA((PIECES,)),
        ],
    )[0]


def on_device(
    tokens,
    keep_mask,
    grad_out,
    in_weight,
    in_bias,
    out_weight,
    out_bias,
    up_weight,
    up_bias,
    down_weight,
    down_bias,
    gain_one,
    shift_one,
    gain_two,
    shift_two,
):
    rows, model = tokens.shape
    leave(*STAY)
    me = jnp.stack([lax.axis_index("tensor"), lax.axis_index("dp")]).astype(jnp.int32)
    images = keep_mask.shape[0]
    heads = in_weight.shape[1] // (3 * HD)
    width = heads * HD
    hidden = up_weight.shape[1]

    def line(values):
        return values.reshape(1, -1)

    side = 2 * rows
    block = 256
    project_flops = 2 * side * model * 3 * width
    attend_flops = 3 * heads * 4 * HALF * SLOTS * 128 + 2 * side * width * model
    back_flops = 3 * heads * 10 * HALF * SLOTS * 128 + 2 * side * width * model

    def act_grad_of(one, other):
        return run(
            act_back,
            (me, one, other, down_weight),
            [shape((side, hidden))],
            flops=2 * side * model * hidden,
        )[0]

    def feed(norms, act_grad, low, kinds):
        tall = rows * len(norms)
        return run(
            functools.partial(feed_forward, low, len(norms)),
            (me, *norms, up_weight, vectors, act_grad),
            [
                shape((tall, hidden), BF),
                shape((tall, hidden), BF),
                shape((1, hidden)),
                *[shape((rows, model), kind) for kind in kinds],
            ],
            scratch=[pltpu.VMEM((tall, model), F32), pltpu.VMEM((2, rows, block), F32)],
            flops=4 * tall * model * hidden,
        )

    def feed_back(me, *acts):
        return run(
            functools.partial(feed_out, len(acts)),
            (me, *acts, down_weight),
            [shape((rows, model), BF), shape((rows, model))],
            flops=2 * side * model * hidden,
        )

    tok_far = swap(tokens, "tensor", 2)
    tok_core = swap(tokens, "tensor", 1)
    keep_flat = keep_mask.reshape(-1).astype(F32)
    keep_own = lax.dynamic_slice_in_dim(keep_flat, me[0] * rows, rows)[:, None]
    cot = (grad_out.astype(F32) * keep_own).astype(BF)
    cot_core = swap(cot, "tensor", 1)
    pair = in_bias.reshape(heads, 2, HD)
    bias_full = jnp.concatenate([pair[:, :1], jnp.zeros((heads, 1, HD), F32), pair[:, 1:]], axis=1)
    bias_full = bias_full.reshape(1, 3 * width)
    vectors = jnp.stack(
        [gain_one, shift_one, out_bias, gain_two, shift_two, up_bias, down_bias, down_bias]
    )
    stay(in_weight, bias_full, vectors, tokens, cot)
    norm_near, proj_near = run(
        project_local,
        (me, tokens, tok_core, vectors, in_weight, bias_full),
        [shape((side, model), BF), shape((side, 3 * width), BF)],
        flops=project_flops,
    )
    stay(norm_near, out_weight)
    tok_far = after(tok_far, proj_near)

    tok_both = swap(tok_far, "tensor", 1)
    cot_far = swap(after(cot, tok_far), "tensor", 2)
    attend_outs = [
        shape((3 * heads, HALF, SLOTS), BF),
        shape((side, width), BF),
        shape((rows, model), BF),
        shape((rows, model), F32),
    ]
    norm_y, proj_y = run(
        project_one,
        (me, tok_far, vectors, in_weight, bias_full),
        [shape((rows, model), BF), shape((rows, 3 * width), BF)],
        flops=project_flops // 2,
    )
    stay(norm_y)
    norm_both, qkv, probs_far, heads_far, send, far_hold = run(
        attend_far,
        (
            me, proj_near, proj_y, tok_both, vectors, in_weight, bias_full, keep_mask, out_weight,
        ),
        [shape((rows, model), BF), shape((2 * side, 3 * width), BF), *attend_outs],
        flops=project_flops + attend_flops,
    )
    stay(norm_both, qkv, probs_far, heads_far, down_weight, up_weight)
    leave(bias_full)
    arrived = after(swap(send, "tensor", 1), cot_far)
    far_sum = add_round(far_hold, arrived)
    cot_far = after(cot_far, far_sum)
    cot_both = swap(cot_far, "tensor", 1)
    arrived_far = swap(far_sum, "tensor", 2)
    probs_near, heads_near, send, hold = run(
        attend_near,
        (after(me, far_sum), qkv, keep_mask, out_weight),
        attend_outs,
        flops=attend_flops,
    )
    stay(probs_near, heads_near, hold)
    act_grad_near = act_grad_of(cot, cot_core)
    stay(act_grad_near, cot_core)
    arrived_near = after(swap(send, "tensor", 1), arrived_far)
    middle, second = run(
        second_norm,
        (
            after(me, act_grad_near), tokens, hold, arrived_near, arrived_far, vectors,
        ),
        [shape((rows, model)), shape((rows, model), BF)],
    )

    leave(hold)
    stay(middle, second)

    second_far = swap(second, "tensor", 2)
    second_core = swap(second, "tensor", 1)
    act_near, pre_near, up_bias_near, near_hold, near_send = feed(
        (second, second_core), act_grad_near, 0, (F32, BF)
    )
    leave(act_grad_near)
    stay(act_near, pre_near, near_hold, second_core)
    act_grad_far = act_grad_of(cot_far, cot_both)
    stay(cot_far, cot_both, act_grad_far)
    second_far = after(second_far, act_grad_far)
    second_both = swap(second_far, "tensor", 1)
    act_y, pre_y, up_bias_y, far_hold = feed((second_far,), act_grad_far, 0, (F32,))
    stay(act_y, pre_y, second_far, far_hold)
    act_both, pre_both, up_bias_both, far_send = feed((second_both,), act_grad_far, rows, (BF,))
    leave(far_hold)
    far_sum = add_round(far_hold, swap(far_send, "tensor", 1))
    arrived_far = swap(far_sum, "tensor", 2)
    leave(act_grad_far, up_weight)
    stay(act_both, pre_both, second_both)
    acts, cots = (act_near, act_y, act_both), (cot, cot_core, cot_far, cot_both)
    down_send = weight_grad(after(me, far_sum), acts, cots, ORDER_A, False)
    down = Reduction(down_send, ORDER_A)
    seconds = (second, second_core, second_far, second_both)
    pres = (pre_near, pre_y, pre_both)
    up_send = weight_grad(after(me, down_send), seconds, pres, ORDER_B, False)
    up = Reduction(up_send, ORDER_B)
    arrived_near = swap(near_send, "tensor", 1)
    feed_send, feed_hold = feed_back(after(me, up_send), act_y, act_both)
    feed_far = add_round(feed_hold, swap(feed_send, "tensor", 1))
    middle_grad, middle_low, middle_sums = run(
        middle_back,
        (
            after(me, feed_hold), near_hold, arrived_near, arrived_far, middle, cot, vectors,
        ),
        [shape((rows, model)), shape((rows, model), BF), shape((4, model))],
        scratch=[pltpu.VMEM((4, 8, model), F32)],
    )

    mid_far = swap(middle_low, "tensor", 2)
    mid_core = swap(middle_low, "tensor", 1)
    grads = pltpu.VMEM((side, width), BF)
    leave(near_hold)
    stay(middle_grad, middle_low)
    down.values = weight_grad(after(me, middle_low), acts, cots, ORDER_A, True)
    leave(act_y, act_both, cot_core, cot_far, cot_both)
    stay(down.values)
    near_q, near_keys = run(
        back_near,
        (after(me, down.values), middle_low, mid_core, qkv, probs_near, out_weight),
        [shape((side, width)), shape((2 * side, 2 * width))],
        scratch=[grads],
        flops=back_flops,
    )
    leave(probs_near)
    stay(near_q, near_keys, mid_core)
    up.values = weight_grad(after(me, near_q), seconds, pres, ORDER_B, True)
    leave(second, second_core, second_far, second_both, pre_near, pre_y, pre_both)
    stay(up.values)
    mid_far = after(mid_far, up.values)
    mid_both = swap(mid_far, "tensor", 1)
    feed_far = swap(after(feed_far, mid_far), "tensor", 2)
    down.arrive(mid_far)
    up.arrive(mid_far)
    flat_near, flat_far, bias_grad, far_send, far_hold = run(
        back_far,
        (
            after(me, down.send, up.send), mid_far, mid_both, qkv, probs_far,
            out_weight, near_q, near_keys, in_weight,
        ),
        [
            shape((side, 3 * width), BF),
            shape((side, 3 * width), BF),
            shape((1, 2 * width)),
            shape((rows, model), BF),
            shape((rows, model)),
        ],
        scratch=[
            grads,
            pltpu.VMEM((side, width), F32),
            pltpu.VMEM((2 * side, 2 * width), F32),
            pltpu.VMEM((side, 3 * width), BF),
        ],
        flops=back_flops + project_flops,
    )
    leave(qkv, probs_far, near_q, near_keys, out_weight)
    stay(flat_near, flat_far, mid_far, mid_both)
    down.take(bias_grad)
    up.take(bias_grad)
    arrived = after(swap(far_send, "tensor", 1), feed_far, down.came, up.came)
    far_sum = add_round(far_hold, arrived)
    arrived_far = swap(far_sum, "tensor", 2)

    down.arrive(far_sum)
    up.arrive(far_sum)
    near_send, hold = run(
        first_back,
        (after(me, down.send, up.send), flat_near, in_weight),
        [shape((rows, model), BF), shape((rows, model))],
        flops=project_flops,
    )
    leave(in_weight)
    stay(hold)
    normed = (norm_near, norm_y, norm_both)
    split = (3 * width + width) // 2
    flat = (flat_near, flat_far)
    head_rows = (heads_near, heads_far)
    mids = (middle_low, mid_core, mid_far, mid_both)
    arrived_near = swap(near_send, "tensor", 1)
    first_send = weight_grad(after(me, hold), normed, flat, ORDER_A, False, 0, split)
    first = Reduction(first_send, ORDER_A)
    mixed_send = mixed_grad(
        after(me, first_send), normed, flat, head_rows, mids, ORDER_B, False, split
    )
    mixed = Reduction(mixed_send, ORDER_B)
    first.values = weight_grad(after(me, mixed_send), normed, flat, ORDER_A, True, 0, split)
    stay(first.values)
    mixed.values = mixed_grad(
        after(me, first.values, arrived_near), normed, flat, head_rows, mids, ORDER_B, True, split
    )
    leave(norm_near, norm_y, norm_both, flat_near, flat_far, heads_near, heads_far)
    leave(middle_low, mid_core, mid_far, mid_both)
    stay(mixed.values)
    tokens_grad, token_sums = run(
        token_back,
        (
            after(me, mixed.values), hold, arrived_near, arrived_far, tokens, middle_grad, vectors,
        ),
        [shape((rows, model)), shape((2, model))],
        scratch=[pltpu.VMEM((2, 8, model), F32)],
    )
    leave(hold, tokens, middle_grad, vectors)
    feed_send, feed_hold = feed_back(after(me, token_sums), act_near)
    feed_rows = feed_hold + swap(feed_send, "tensor", 1).astype(F32) + feed_far.astype(F32)
    output = (keep_own * (middle + feed_rows + down_bias)).astype(BF)
    leave(*STAY)
    stay(down.values, up.values, first.values, mixed.values)

    now = down.arrive(feed_hold)
    shared = pack(jnp.concatenate([middle_sums, token_sums], axis=0))
    shared = add_small(shared, after(swap(shared, "tensor", 1), now))
    now = first.arrive(now)
    now = mixed.arrive(now)
    shared = unpack(add_small(shared, after(swap(shared, "tensor", 2), now)))
    own = jnp.concatenate(
        [up_bias_near + up_bias_y + up_bias_both, jnp.pad(bias_grad, ((0, 0), (0, hidden - 2 * width)))], axis=0
    )
    small = jnp.concatenate([shared, own], axis=0)
    small = pack(jnp.concatenate([small[:, :split], small[:, split:]], axis=0))
    now = up.arrive(now)
    now = down.arrive(now)
    now = mixed.arrive(now)
    now = first.arrive(now)
    now = up.arrive(now)
    now = mixed.arrive(now)
    now = first.arrive(now)
    while first.at < first.count:
        now = first.arrive(now)
    first.join(small)
    now = down.arrive(now)
    now = up.arrive(now)
    now = mixed.arrive(now)
    now = first.arrive(now)
    now = mixed.arrive(now)
    now = first.arrive(now)
    now = down.arrive(now)
    down_sum = place(after(me, now), down.parts, ORDER_A)
    up.arrive(down_sum)
    up_sum = place(me, up.parts, ORDER_B)
    now = mixed.arrive(up_sum)
    first.arrive(now)
    small = unpack(first.small)
    small = jnp.concatenate([small[:8], small[8:]], axis=1)
    piece = model // PIECES
    in_sum, out_sum = run_out(
        functools.partial(place_mixed, ORDER_A, ORDER_B),
        (me, *first.parts, *mixed.parts),
        [shape((model, 3 * width)), shape((width, model))],
        scratch=[
            pltpu.VMEM((PIECES, piece, 3 * width), F32),
            pltpu.VMEM((PIECES, width, piece), F32),
            pltpu.SemaphoreType.DMA((3 * PIECES,)),
        ],
    )
    in_bias_sum = small[7, : 2 * width].reshape(2, heads, HD).transpose(1, 0, 2).reshape(-1)
    return (
        output,
        tokens_grad,
        in_sum,
        in_bias_sum,
        out_sum,
        small[0],
        up_sum,
        small[6],
        down_sum,
        small[1],
        small[4],
        small[5],
        small[2],
        small[3],
    )


def solution(mesh):
    rows = P(("dp", "tensor"), None)
    placed = (
        rows,
        P("dp", None),
        rows,
        P(None, "tensor"),
        P("tensor"),
        P("tensor", None),
        P(),
        P(None, "tensor"),
        P("tensor"),
        P("tensor", None),
        P(),
        P(),
        P(),
        P(),
        P(),
    )
    given = (
        rows,
        rows,
        P(None, "tensor"),
        P("tensor"),
        P("tensor", None),
        P(),
        P(None, "tensor"),
        P("tensor"),
        P("tensor", None),
        P(),
        P(),
        P(),
        P(),
        P(),
    )
    return jax.shard_map(on_device, mesh=mesh, in_specs=placed, out_specs=given, check_vma=False)
```

```python
import functools

import jax
import jax.numpy as jnp
from jax import lax
from jax.experimental import pallas as pl
from jax.experimental.pallas import tpu as pltpu
from jax.sharding import PartitionSpec as P

HD = 64
SLOTS = 320
HALF = SLOTS // 2
PIECES = 8
EPSILON = 1e-06
BF = jnp.bfloat16
F32 = jnp.float32
MIB = 1 << 20


def mm(left, right, dims=((1,), (0,))):
    return lax.dot_general(left, right, (dims, ((), ())), preferred_element_type=F32)


NT = ((1,), (1,))
TN = ((0,), (0,))


def swap(values, axis, bit):
    count = lax.axis_size(axis)
    return lax.ppermute(values, axis, [(i, i ^ bit) for i in range(count)])


def after(values, *earlier):
    return lax.optimization_barrier((values, *earlier))[0]


def shape(dims, kind=F32):
    return jax.ShapeDtypeStruct(dims, kind)


STAY = []


def stay(*arrays):
    STAY.extend(arrays)


def leave(*arrays):
    for array in arrays:
        STAY[:] = [x for x in STAY if x is not array]


def run(body, operands, outs, scratch=(), flops=0, room=12):
    used = list(operands[1:])
    waiting = [x for x in STAY if all(x is not y for y in used)]
    ins = [pltpu.with_memory_space_constraint(x, pltpu.VMEM) for x in [*used, *waiting]]
    moved = sum(x.size * x.dtype.itemsize for x in [*used, *outs])

    def kernel(*refs):
        own = 1 + len(used)
        body(*refs[:own], *refs[own + len(waiting) :])

    return pl.pallas_call(
        kernel,
        out_shape=[pltpu.VMEM(x.shape, x.dtype) for x in outs],
        in_specs=[pl.BlockSpec(memory_space=pltpu.SMEM)]
        + [pl.BlockSpec(memory_space=pltpu.VMEM)] * len(ins),
        out_specs=[pl.BlockSpec(memory_space=pltpu.VMEM)] * len(outs),
        scratch_shapes=scratch,
        compiler_params=pltpu.CompilerParams(vmem_limit_bytes=room * MIB),
        cost_estimate=pl.CostEstimate(
            flops=int(flops * WEIGHT), bytes_accessed=0, transcendentals=0
        ),
    )(operands[0], *ins)


WEIGHT = 20


def add_low(me, left, right, out):
    out[...] = (left[...] + right[...].astype(F32)).astype(BF)


def add_round(left, right):
    return run(add_low, (jnp.zeros((1,), jnp.int32), left, right), [shape(left.shape, BF)])[0]


def add_halves(me, left, right, send, hold):
    middle = send.shape[0]
    send[...] = (left[middle:, :] + right[middle:, :].astype(F32)).astype(BF)
    hold[...] = left[:middle, :] + right[:middle, :].astype(F32)


def run_out(body, operands, outs, scratch=(), room=16):
    ins = [pltpu.with_memory_space_constraint(x, pltpu.VMEM) for x in operands[1:]]
    return pl.pallas_call(
        body,
        out_shape=[pltpu.HBM(x.shape, x.dtype) for x in outs],
        in_specs=[pl.BlockSpec(memory_space=pltpu.SMEM)]
        + [pl.BlockSpec(memory_space=pltpu.VMEM)] * len(ins),
        out_specs=[pl.BlockSpec(memory_space=pltpu.HBM)] * len(outs),
        scratch_shapes=scratch,
        compiler_params=pltpu.CompilerParams(vmem_limit_bytes=room * MIB),
        cost_estimate=pl.CostEstimate(
            flops=int(1e9 * WEIGHT), bytes_accessed=0, transcendentals=0
        ),
    )(operands[0], *ins)


def blocks(count, size, step):
    def one(i, carry):
        step(pl.ds(pl.multiple_of(i * size, size), size), i)
        return carry

    lax.fori_loop(0, count, one, 0)


def row_tiles(rows, size, step):
    def one(i, carry):
        step(pl.ds(pl.multiple_of(i * size, size), size))
        return carry

    lax.fori_loop(0, rows // size, one, 0)


def normalise(values):
    average = jnp.mean(values, axis=-1, keepdims=True)
    centred = values - average
    factor = lax.rsqrt(jnp.mean(centred * centred, axis=-1, keepdims=True) + EPSILON)
    return centred * factor, factor


def norm_back(grad, gain, z, factor):
    s = grad * gain
    return factor * (
        s - jnp.mean(s, axis=-1, keepdims=True) - z * jnp.mean(s * z, axis=-1, keepdims=True)
    )


def fold(values):
    return functools.reduce(
        lambda a, b: a + b, [values[i : i + 8] for i in range(0, values.shape[0], 8)]
    )


GAIN_ONE, SHIFT_ONE, OUT_BIAS, GAIN_TWO, SHIFT_TWO, UP_BIAS, DOWN_BIAS = range(7)


def row(vectors, number):
    return vectors[number : number + 1, :]


def project_side(blocks, vectors, weight, bias, normed, put):
    rows = blocks[0].shape[0]
    width = weight.shape[1] // 3
    for i, block in enumerate(blocks):

        def step(at, block=block, i=i):
            z, _ = normalise(block[at, :].astype(F32))
            tile = pl.ds(pl.multiple_of(at.start + i * rows, 16), at.size)
            normed[tile, :] = (z * row(vectors, GAIN_ONE) + row(vectors, SHIFT_ONE)).astype(BF)

        row_tiles(rows, 48, step)
        found = (mm(normed[i * rows : (i + 1) * rows, :], weight[...]) + bias[...]).astype(BF)
        kinds = [
            [found[:, (3 * head + kind) * HD :][:, :HD] for head in range(width // HD)]
            for kind in range(3)
        ]
        put(i, jnp.concatenate(sum(kinds, []), axis=1))


def project_local(me, tok_a, tok_b, vectors, weight, bias, normed, proj):
    rows = tok_a.shape[0]

    def put(i, values):
        proj[i * rows : (i + 1) * rows, :] = values

    project_side((tok_a, tok_b), vectors, weight, bias, normed, put)


def attend(side, qkv, keep, probs, heads_out):
    half_lane = lax.broadcasted_iota(jnp.int32, (1, 2 * HD), 1) // HD
    width = qkv.shape[1] // 3

    def one(j, carry):
        place = 3 * side + j
        image = place // 2
        queries = pl.ds(pl.multiple_of(place * HALF, 16), HALF)
        keys = pl.ds(pl.multiple_of(image * SLOTS, 16), SLOTS)
        live = keep[pl.ds(image, 1), :] > 0
        for pair in range(width // (2 * HD)):
            lanes = pl.ds(pair * 2 * HD, 2 * HD)
            q = qkv[queries, lanes] * 0.125
            k = qkv[keys, pl.ds(width + pair * 2 * HD, 2 * HD)]
            v = qkv[keys, pl.ds(2 * width + pair * 2 * HD, 2 * HD)]
            outs = []
            for e in range(2):
                scores = mm(jnp.where(half_lane == e, q, jnp.zeros_like(q)), k, NT)
                scores = jnp.where(live, scores, -1000000000.0)
                power = jnp.exp(scores - jnp.max(scores, axis=-1, keepdims=True))
                p = (power / jnp.sum(power, axis=-1, keepdims=True)).astype(BF)
                probs[j * 4 + pair * 2 + e] = p
                outs.append(mm(p, v))
            heads_out[pl.ds(pl.multiple_of(j * HALF, 16), HALF), lanes] = jnp.where(
                half_lane == 0, outs[0], outs[1]
            ).astype(BF)
        return carry

    lax.fori_loop(0, 3, one, 0)


def out_project(core, heads_out, weight, send, hold):
    rows = send.shape[0]
    send[...] = mm(
        heads_out[pl.ds(pl.multiple_of((1 - core) * rows, 16), rows), :], weight[...]
    ).astype(BF)
    hold[...] = mm(heads_out[pl.ds(pl.multiple_of(core * rows, 16), rows), :], weight[...])


def project_one(me, tok, vectors, weight, bias, normed, proj):
    def put(i, values):
        proj[...] = values

    project_side((tok,), vectors, weight, bias, normed, put)


def attend_far(
    me, near, first, tok, vectors, weight, bias, keep, out_w,
    normed, qkv, probs, heads_out, send, hold,
):
    rows = tok.shape[0]
    core, far = me[0] & 1, me[0] >> 1
    for i in range(2):
        at = pl.multiple_of((2 * far + (core ^ i)) * rows, 16)
        qkv[pl.ds(at, rows), :] = near[i * rows : (i + 1) * rows, :]
    at = pl.multiple_of((2 * (1 - far) + core) * rows, 16)
    qkv[pl.ds(at, rows), :] = first[...]

    def put(i, values):
        at = pl.multiple_of((2 * (1 - far) + (1 - core)) * rows, 16)
        qkv[pl.ds(at, rows), :] = values

    project_side((tok,), vectors, weight, bias, normed, put)
    attend(1 - far, qkv, keep, probs, heads_out)
    out_project(core, heads_out, out_w, send, hold)


def attend_near(me, qkv, keep, out_w, probs, heads_out, send, hold):
    core, far = me[0] & 1, me[0] >> 1
    attend(far, qkv, keep, probs, heads_out)
    out_project(core, heads_out, out_w, send, hold)


def second_norm(me, tok, hold, near, far, vectors, middle, second):
    def step(at):
        total = hold[at, :] + near[at, :].astype(F32) + far[at, :].astype(F32)
        values = tok[at, :].astype(F32) + total + row(vectors, OUT_BIAS)
        middle[at, :] = values
        z, _ = normalise(values)
        second[at, :] = (z * row(vectors, GAIN_TWO) + row(vectors, SHIFT_TWO)).astype(BF)

    row_tiles(tok.shape[0], 48, step)


def act_back(me, cot_a, cot_b, down, act_grad):
    rows = cot_a.shape[0]

    def step(at, i):
        act_grad[:rows, at] = mm(cot_a[...], down[at, :], NT)
        act_grad[rows:, at] = mm(cot_b[...], down[at, :], NT)

    blocks(down.shape[0] // 256, 256, step)


def feed_forward(low, count, me, *refs):
    norms = refs[:count]
    up, vectors, act_grad, act, pre_low, bias_grad = refs[count : count + 6]
    outs, total, pre = refs[count + 6 : 2 * count + 6], refs[-2], refs[-1]
    rows = norms[0].shape[0]
    wide = pre.shape[2]
    number = up.shape[1] // wide
    bias_grad[...] = jnp.zeros_like(bias_grad)
    total[...] = jnp.zeros_like(total)

    def columns(i):
        return pl.ds(pl.multiple_of(i * wide, wide), wide)

    def elements(slot, at, block):
        own_bias = vectors[UP_BIAS : UP_BIAS + 1, at]
        sums = None
        for i in range(0, rows, 16):
            to = pl.ds(block * rows + i, 16)
            x = pre[slot, i : i + 16, :] + own_bias
            share = 0.5 + 0.5 * lax.erf(x * 0.7071067811865476)
            slope = share + x * (0.3989422804014327 * jnp.exp(-0.5 * x * x))
            act[to, at] = (x * share).astype(BF)
            grad = act_grad[pl.ds(low + block * rows + i, 16), at] * slope
            pre_low[to, at] = grad.astype(BF)
            part = grad[:8] + grad[8:]
            sums = part if sums is None else sums + part
        bias_grad[:, at] += jnp.sum(sums, axis=0, keepdims=True)

    pre[0] = mm(norms[0][...], up[:, :wide])

    def one(i, carry):
        if count == 2:
            steps = ((i, 0), (i, 1), (jnp.minimum(i + 1, number - 1), 0))
        else:
            steps = ((2 * i, 0), (2 * i + 1, 0), (jnp.minimum(2 * i + 2, number - 1), 0))
        for slot in range(2):
            column, block = steps[slot]
            later, other = steps[slot + 1]
            pre[1 - slot] = mm(norms[other][...], up[:, columns(later)])
            elements(slot, columns(column), block)
            inside = pl.ds(block * rows, rows)
            total[inside, :] += mm(pre_low[inside, columns(column)], up[:, columns(column)], NT)
        return carry

    lax.fori_loop(0, number * count // 2, one, 0)
    for i, out in enumerate(outs):
        out[...] = total[i * rows : (i + 1) * rows, :].astype(out.dtype)


def feed_out(count, me, *refs):
    acts, (down, send, hold) = refs[:count], refs[count:]
    rows = send.shape[0]
    one = acts[-1][rows:, :] if count == 1 else acts[1][...]
    send[...] = mm(one, down[...]).astype(BF)
    hold[...] = mm(acts[0][:rows, :], down[...])


def gather_pieces(me, lefts, order, base, turned):
    piece = lefts[0].shape[1] // PIECES
    for i in range(PIECES // 2):
        at = pl.ds(pl.multiple_of(piece_of(base + i, order, me[1]) * piece, piece), piece)
        for left, to in zip(lefts, turned, strict=True):
            to[i * piece : (i + 1) * piece, :] = left[:, at].T


def segments(lefts, rights):
    found, left, right, a, b = [], 0, 0, 0, 0
    while left < len(lefts):
        rows = min(lefts[left].shape[0] - a, rights[right].shape[0] - b)
        found.append((left, a, right, b, rows))
        a, b = a + rows, b + rows
        if a == lefts[left].shape[0]:
            left, a = left + 1, 0
        if b == rights[right].shape[0]:
            right, b = right + 1, 0
    return found


def weight_pieces(order, base, low, count, me, *refs):
    lefts, rights = refs[: count[0]], refs[count[0] : sum(count)]
    out, turned = refs[sum(count)], refs[sum(count) + 1 :]
    gather_pieces(me, lefts, order, base, turned)

    def step(at, i):
        found = None
        from_ = pl.ds(pl.multiple_of(at.start + low, 128), at.size)
        for left, a, right, b, rows in segments(lefts, rights):
            part = mm(turned[left][:, a : a + rows], rights[right][b : b + rows, from_])
            found = part if found is None else found + part
        out[:, at] = found.astype(out.dtype)

    blocks(out.shape[1] // 256, 256, step)


def mixed_pieces(order, base, low, me, *refs):
    lefts, rights, heads, mids, out = refs[:3], refs[3:5], refs[5:7], refs[7:11], refs[11]
    turned = refs[12:]
    gather_pieces(me, lefts, order, base, turned)
    width = rights[0].shape[1] - low
    for at in range(0, width, 256):
        found = None
        for left, a, right, b, rows in segments(lefts, rights):
            part = mm(
                turned[left][:, a : a + rows],
                rights[right][b : b + rows, low + at : low + at + 256],
            )
            found = part if found is None else found + part
        out[:, at : at + 256] = found.astype(out.dtype)
    core = me[0] & 1
    rows = mids[0].shape[0]
    piece = mids[0].shape[1] // PIECES
    half = heads[0].shape[1] // 2
    for i in range(PIECES // 2):
        at = pl.ds(pl.multiple_of(piece_of(base + i, order, me[1]) * piece, piece), piece)
        both = None
        for k in range(4):
            inside = pl.ds(pl.multiple_of((core ^ (k % 2)) * rows, 16), rows)
            part = mm(heads[k // 2][inside, :], mids[k][:, at], TN)
            both = part if both is None else both + part
        to = pl.ds(i * piece, piece)
        out[to, width : width + half] = both[:half].astype(out.dtype)
        out[to, width + half :] = both[half:].astype(out.dtype)


def middle_back(me, hold, near, far, middle, cot_low, vectors, middle_grad, middle_low, sums, parts):
    parts[...] = jnp.zeros_like(parts)

    def step(at):
        second = hold[at, :] + near[at, :].astype(F32) + far[at, :].astype(F32)
        z, factor = normalise(middle[at, :])
        cot = cot_low[at, :].astype(F32)
        total = cot + norm_back(second, row(vectors, GAIN_TWO), z, factor)
        middle_grad[at, :] = total
        middle_low[at, :] = total.astype(BF)
        parts[0] += fold(total)
        parts[1] += fold(cot)
        parts[2] += fold(second * z)
        parts[3] += fold(second)

    row_tiles(hold.shape[0], 48, step)
    for i in range(4):
        sums[i : i + 1, :] = jnp.sum(parts[i], axis=0, keepdims=True)


def attend_back(side, mid_blocks, core, qkv, probs, out_w, grads, pg_q, keys_grad):
    rows = mid_blocks[0].shape[0]
    half_lane = lax.broadcasted_iota(jnp.int32, (1, 2 * HD), 1) // HD
    width = qkv.shape[1] // 3
    for i, block in enumerate(mid_blocks):
        at = pl.multiple_of((core ^ i) * rows, 16)
        grads[pl.ds(at, rows), :] = mm(block[...], out_w[...], NT).astype(BF)

    def one(j, carry):
        place = 3 * side + j
        image = place // 2
        inside = pl.ds(pl.multiple_of(j * HALF, 16), HALF)
        queries = pl.ds(pl.multiple_of(place * HALF, 16), HALF)
        keys = pl.ds(pl.multiple_of(image * SLOTS, 16), SLOTS)
        for pair in range(width // (2 * HD)):
            lanes = pl.ds(pair * 2 * HD, 2 * HD)
            q = qkv[queries, lanes]
            k = qkv[keys, pl.ds(width + pair * 2 * HD, 2 * HD)]
            v = qkv[keys, pl.ds(2 * width + pair * 2 * HD, 2 * HD)]
            g = grads[inside, lanes]
            found = []
            for e in range(2):
                p = probs[j * 4 + pair * 2 + e]
                wide = p.astype(F32)
                prob_grad = mm(jnp.where(half_lane == e, g, jnp.zeros_like(g)), v, NT)
                delta = jnp.sum(wide * prob_grad, axis=-1, keepdims=True)
                score_grad = (wide * (prob_grad - delta) * 0.125).astype(BF)
                found.append(
                    (mm(score_grad, k), mm(score_grad, q, TN), mm(p, g, TN))
                )
            q_grad, k_grad, v_grad = (
                jnp.where(half_lane == 0, a, b) for a, b in zip(*found, strict=True)
            )
            pg_q[inside, lanes] = q_grad
            keys_grad[keys, lanes] += k_grad
            keys_grad[keys, pl.ds(width + pair * 2 * HD, 2 * HD)] += v_grad
        return carry

    lax.fori_loop(0, 3, one, 0)


def back_near(me, mid_a, mid_b, qkv, probs, out_w, pg_q, keys_grad, grads):
    core, far = me[0] & 1, me[0] >> 1
    keys_grad[...] = jnp.zeros_like(keys_grad)
    attend_back(far, (mid_a, mid_b), core, qkv, probs, out_w, grads, pg_q, keys_grad)


def back_far(
    me, mid_a, mid_b, qkv, probs, out_w, near_q, near_keys, in_w,
    flat_near, flat_far, bias_grad, send, hold, grads, far_q, keys_grad, group,
):
    core, far = me[0] & 1, me[0] >> 1
    rows = mid_a.shape[0]
    width = far_q.shape[1]
    keys_grad[...] = near_keys[...]
    attend_back(1 - far, (mid_a, mid_b), core, qkv, probs, out_w, grads, far_q, keys_grad)
    bias_grad[...] = jnp.concatenate(
        [
            jnp.sum(far_q[...], axis=0, keepdims=True) + jnp.sum(near_q[...], axis=0, keepdims=True),
            jnp.sum(keys_grad[:, width:], axis=0, keepdims=True),
        ],
        axis=1,
    )
    for side, (flat, q_part) in enumerate(((flat_near, near_q), (flat_far, far_q))):
        for i in range(2):
            inside = pl.multiple_of((core ^ i) * rows, 16)
            place = pl.multiple_of((2 * (far ^ side) + (core ^ i)) * rows, 16)
            to = pl.ds(i * rows, rows)
            group[to, :width] = q_part[pl.ds(inside, rows), :].astype(BF)
            group[to, width:] = keys_grad[pl.ds(place, rows), :].astype(BF)
        for head in range(width // HD):
            for kind in range(3):
                at = (head * 3 + kind) * HD
                flat[:, at : at + HD] = group[:, kind * width + head * HD :][:, :HD]
    send[...] = mm(flat_far[rows:, :], in_w[...], NT).astype(BF)
    hold[...] = mm(flat_far[:rows, :], in_w[...], NT)


def first_back(me, proj, in_w, send, hold):
    rows = send.shape[0]
    send[...] = mm(proj[rows:, :], in_w[...], NT).astype(BF)
    hold[...] = mm(proj[:rows, :], in_w[...], NT)


def mixed_piece(me, norm_a, norm_b, proj_a, proj_b, heads_a, heads_b, mid_a, mid_b, out):
    width = proj_a.shape[1]
    out[:, :width] = (
        mm(norm_a[...], proj_a[...], TN) + mm(norm_b[...], proj_b[...], TN)
    ).astype(out.dtype)
    both = mm(heads_a[...], mid_a[...], TN) + mm(heads_b[...], mid_b[...], TN)
    half = both.shape[0] // 2
    out[:, width : width + half] = both[:half].astype(out.dtype)
    out[:, width + half :] = both[half:].astype(out.dtype)


def token_back(me, hold, near, far, tok, middle_grad, vectors, tokens_grad, sums, parts):
    parts[...] = jnp.zeros_like(parts)

    def step(at):
        first = hold[at, :] + near[at, :].astype(F32) + far[at, :].astype(F32)
        z, factor = normalise(tok[at, :].astype(F32))
        tokens_grad[at, :] = middle_grad[at, :] + norm_back(
            first, row(vectors, GAIN_ONE), z, factor
        )
        parts[0] += fold(first * z)
        parts[1] += fold(first)

    row_tiles(hold.shape[0], 48, step)
    for i in range(2):
        sums[i : i + 1, :] = jnp.sum(parts[i], axis=0, keepdims=True)


def place_pieces(order, me, *refs):
    parts, out, wide, sems = refs[:-3], refs[-3], refs[-2], refs[-1]
    piece = out.shape[0] // PIECES
    copies = []
    for i in range(PIECES):
        part, row = locate(parts, i * piece)
        wide[i] = part[row : row + piece, :].astype(F32)
        to = pl.ds(pl.multiple_of(piece_of(i, order, me[1]) * piece, piece), piece)
        copies.append(pltpu.make_async_copy(wide.at[i], out.at[to, :], sems.at[i]))
        copies[-1].start()
    for copy in copies:
        copy.wait()


def locate(parts, row):
    for part in parts:
        if row < part.shape[0]:
            return part, row
        row -= part.shape[0]


def place_half(half, count, order, other, me, first, second, *refs):
    in_out, out_out, wide, flat, sems = refs[count:]
    piece = in_out.shape[0] // PIECES
    middle = out_out.shape[0] // 2
    split = first.shape[1]
    rest = in_out.shape[1] - split
    copies = []
    for i in range(PIECES // 2):
        part = pl.ds(i * piece, piece)
        place = piece_of(half * PIECES // 2 + i, order, me[1])
        to = pl.ds(pl.multiple_of(place * piece, piece), piece)
        wide[i, :, :split] = first[part, :].astype(F32)
        copies.append(
            pltpu.make_async_copy(wide.at[i, :, :split], in_out.at[to, :split], sems.at[3 * i])
        )
        copies[-1].start()
        place = piece_of(half * PIECES // 2 + i, other, me[1])
        to = pl.ds(pl.multiple_of(place * piece, piece), piece)
        wide[i, :, split:] = second[part, :rest].astype(F32)
        flat[i, :middle, :] = second[part, rest : rest + middle].astype(F32)
        flat[i, middle:, :] = second[part, rest + middle :].astype(F32)
        copies.append(
            pltpu.make_async_copy(wide.at[i, :, split:], in_out.at[to, split:], sems.at[3 * i + 1])
        )
        copies[-1].start()
        copies.append(
            pltpu.make_async_copy(flat.at[i], out_out.at[:, to], sems.at[3 * i + 2])
        )
        copies[-1].start()
    for copy in copies:
        copy.wait()


def place_mixed(me, half, first, second, outs, into=()):
    ins = [pltpu.with_memory_space_constraint(x, pltpu.VMEM) for x in (first, second)]
    half_pieces = PIECES // 2
    tall, wide = outs[0].shape
    return pl.pallas_call(
        functools.partial(place_half, half, len(into), ORDER_A, ORDER_B),
        out_shape=[pltpu.HBM(x.shape, x.dtype) for x in outs],
        in_specs=[pl.BlockSpec(memory_space=pltpu.SMEM)]
        + [pl.BlockSpec(memory_space=pltpu.VMEM)] * 2
        + [pl.BlockSpec(memory_space=pltpu.HBM)] * len(into),
        out_specs=[pl.BlockSpec(memory_space=pltpu.HBM)] * 2,
        scratch_shapes=[
            pltpu.VMEM((half_pieces, tall // PIECES, wide), F32),
            pltpu.VMEM((half_pieces, outs[1].shape[0], tall // PIECES), F32),
            pltpu.SemaphoreType.DMA((3 * half_pieces,)),
        ],
        input_output_aliases={3: 0, 4: 1} if into else {},
        compiler_params=pltpu.CompilerParams(vmem_limit_bytes=16 * MIB),
        cost_estimate=pl.CostEstimate(
            flops=int(1e9 * WEIGHT), bytes_accessed=0, transcendentals=0
        ),
    )(me, *ins, *into)


def piece_of(position, order, me):
    relative = 0
    for step, bit in enumerate(order):
        relative = relative | (((position >> (len(order) - 1 - step)) & 1) << bit)
    return relative ^ (me & (PIECES - 1))


def pack(values):
    high = values.astype(BF)
    return jnp.concatenate([high, (values - high.astype(F32)).astype(BF)], axis=0)


def add_small(own, other):
    return pack(unpack(own) + unpack(other))


def unpack(packed):
    half = packed.shape[0] // 2
    return packed[:half].astype(F32) + packed[half:].astype(F32)


class Reduction:
    def __init__(self, send, order):
        self.send, self.order = send, order
        self.count = lax.axis_size("dp").bit_length() - 1
        self.bits = [*order, *range(len(order), self.count), *reversed(order)]
        self.values, self.small, self.came, self.at = None, None, None, 0

    def take(self, *earlier):
        self.came = swap(self.send, "dp", 1 << self.bits[self.at])
        if earlier:
            self.came = after(self.came, *earlier)
        return self.came

    def arrive(self, *earlier):
        found = self.step(*earlier)
        while len(self.order) <= self.at < self.count:
            found = self.step(found)
        return found

    def step(self, *earlier):
        if self.came is None:
            self.take()
        arrived = after(self.came, *earlier)
        self.came = None
        self.at += 1
        halving = len(self.order)
        if self.at < halving:
            dims = (self.values.shape[0] // 2, self.values.shape[1])
            leave(self.values)
            self.send, self.values = run(
                add_halves,
                (jnp.zeros((1,), jnp.int32), self.values, arrived),
                [shape(dims, BF), shape(dims)],
            )
            stay(self.values)
        elif self.at == halving:
            leave(self.values)
            self.values = add_round(self.values, arrived)
            self.send = self.values
        elif self.at <= self.count:
            self.values = (self.values.astype(F32) + arrived.astype(F32)).astype(BF)
            self.send = self.values
        else:
            rows = self.values.shape[0]
            if self.small is not None:
                self.small = pack(unpack(self.small) + unpack(arrived[rows:]))
            if self.at == len(self.bits):
                self.parts = (self.values, arrived)
                return arrived
            self.values = jnp.concatenate([self.values, arrived[:rows]], axis=0)
            self.send = self.values
            if self.small is not None:
                self.send = jnp.concatenate([self.values, self.small], axis=0)
        return self.send

    def join(self, small):
        for bit in range(len(self.order), self.count):
            small = pack(unpack(small) + unpack(swap(small, "dp", 1 << bit)))
        self.small = small
        self.send = jnp.concatenate([self.values, small], axis=0)


ORDER_A = (0, 1, 2)
ORDER_B = (1, 0, 2)


def weight_grad(me, lefts, rights, order, kept, low=0, wide=None):
    half = lefts[0].shape[1] // 2
    wide = wide or rights[0].shape[1]
    count = (len(lefts), len(rights))
    return run(
        functools.partial(weight_pieces, order, 0 if kept else PIECES // 2, low, count),
        (me, *lefts, *rights),
        [shape((half, wide), F32 if kept else BF)],
        scratch=[pltpu.VMEM((half, x.shape[0]), BF) for x in lefts],
        flops=2 * 960 * half * wide,
    )[0]


def mixed_grad(me, normed, proj, heads, mids, order, kept, low):
    half = normed[0].shape[1] // 2
    wide = proj[0].shape[1] - low + heads[0].shape[1]
    return run(
        functools.partial(mixed_pieces, order, 0 if kept else PIECES // 2, low),
        (me, *normed, *proj, *heads, *mids),
        [shape((half, wide), F32 if kept else BF)],
        scratch=[pltpu.VMEM((half, x.shape[0]), BF) for x in normed],
        flops=2 * 960 * half * wide,
    )[0]


def place(me, parts, order):
    rows, wide = 2 * parts[0].shape[0], parts[0].shape[1]
    return run_out(
        functools.partial(place_pieces, order),
        (me, *parts),
        [shape((rows, wide))],
        scratch=[
            pltpu.VMEM((PIECES, rows // PIECES, wide), F32),
            pltpu.SemaphoreType.DMA((PIECES,)),
        ],
    )[0]


def on_device(
    tokens,
    keep_mask,
    grad_out,
    in_weight,
    in_bias,
    out_weight,
    out_bias,
    up_weight,
    up_bias,
    down_weight,
    down_bias,
    gain_one,
    shift_one,
    gain_two,
    shift_two,
):
    rows, model = tokens.shape
    leave(*STAY)
    me = jnp.stack([lax.axis_index("tensor"), lax.axis_index("dp")]).astype(jnp.int32)
    images = keep_mask.shape[0]
    heads = in_weight.shape[1] // (3 * HD)
    width = heads * HD
    hidden = up_weight.shape[1]

    def line(values):
        return values.reshape(1, -1)

    side = 2 * rows
    block = 256
    project_flops = 2 * side * model * 3 * width
    attend_flops = 3 * heads * 4 * HALF * SLOTS * 128 + 2 * side * width * model
    back_flops = 3 * heads * 10 * HALF * SLOTS * 128 + 2 * side * width * model

    def act_grad_of(one, other):
        return run(
            act_back,
            (me, one, other, down_weight),
            [shape((side, hidden))],
            flops=2 * side * model * hidden,
        )[0]

    def feed(norms, act_grad, low, kinds):
        tall = rows * len(norms)
        return run(
            functools.partial(feed_forward, low, len(norms)),
            (me, *norms, up_weight, vectors, act_grad),
            [
                shape((tall, hidden), BF),
                shape((tall, hidden), BF),
                shape((1, hidden)),
                *[shape((rows, model), kind) for kind in kinds],
            ],
            scratch=[pltpu.VMEM((tall, model), F32), pltpu.VMEM((2, rows, block), F32)],
            flops=4 * tall * model * hidden,
        )

    def feed_back(me, *acts):
        return run(
            functools.partial(feed_out, len(acts)),
            (me, *acts, down_weight),
            [shape((rows, model), BF), shape((rows, model))],
            flops=2 * side * model * hidden,
        )

    tok_far = swap(tokens, "tensor", 2)
    tok_core = swap(tokens, "tensor", 1)
    keep_flat = keep_mask.reshape(-1).astype(F32)
    keep_own = lax.dynamic_slice_in_dim(keep_flat, me[0] * rows, rows)[:, None]
    cot = (grad_out.astype(F32) * keep_own).astype(BF)
    cot_core = swap(cot, "tensor", 1)
    pair = in_bias.reshape(heads, 2, HD)
    bias_full = jnp.concatenate([pair[:, :1], jnp.zeros((heads, 1, HD), F32), pair[:, 1:]], axis=1)
    bias_full = bias_full.reshape(1, 3 * width)
    vectors = jnp.stack(
        [gain_one, shift_one, out_bias, gain_two, shift_two, up_bias, down_bias, down_bias]
    )
    stay(in_weight, bias_full, vectors, tokens, cot)
    norm_near, proj_near = run(
        project_local,
        (me, tokens, tok_core, vectors, in_weight, bias_full),
        [shape((side, model), BF), shape((side, 3 * width), BF)],
        flops=project_flops,
    )
    stay(norm_near, out_weight)
    tok_far = after(tok_far, proj_near)

    tok_both = swap(tok_far, "tensor", 1)
    cot_far = swap(after(cot, tok_far), "tensor", 2)
    attend_outs = [
        shape((3 * heads, HALF, SLOTS), BF),
        shape((side, width), BF),
        shape((rows, model), BF),
        shape((rows, model), F32),
    ]
    norm_y, proj_y = run(
        project_one,
        (me, tok_far, vectors, in_weight, bias_full),
        [shape((rows, model), BF), shape((rows, 3 * width), BF)],
        flops=project_flops // 2,
    )
    stay(norm_y)
    norm_both, qkv, probs_far, heads_far, send, far_hold = run(
        attend_far,
        (
            me, proj_near, proj_y, tok_both, vectors, in_weight, bias_full, keep_mask, out_weight,
        ),
        [shape((rows, model), BF), shape((2 * side, 3 * width), BF), *attend_outs],
        flops=project_flops + attend_flops,
    )
    stay(norm_both, qkv, probs_far, heads_far, down_weight, up_weight)
    leave(bias_full)
    arrived = after(swap(send, "tensor", 1), cot_far)
    far_sum = add_round(far_hold, arrived)
    cot_far = after(cot_far, far_sum)
    cot_both = swap(cot_far, "tensor", 1)
    arrived_far = swap(far_sum, "tensor", 2)
    probs_near, heads_near, send, hold = run(
        attend_near,
        (after(me, far_sum), qkv, keep_mask, out_weight),
        attend_outs,
        flops=attend_flops,
    )
    stay(probs_near, heads_near, hold)
    act_grad_near = act_grad_of(cot, cot_core)
    stay(act_grad_near, cot_core)
    arrived_near = after(swap(send, "tensor", 1), arrived_far)
    middle, second = run(
        second_norm,
        (
            after(me, act_grad_near), tokens, hold, arrived_near, arrived_far, vectors,
        ),
        [shape((rows, model)), shape((rows, model), BF)],
    )

    leave(hold)
    stay(middle, second)

    second_far = swap(second, "tensor", 2)
    second_core = swap(second, "tensor", 1)
    act_near, pre_near, up_bias_near, near_hold, near_send = feed(
        (second, second_core), act_grad_near, 0, (F32, BF)
    )
    leave(act_grad_near)
    stay(act_near, pre_near, near_hold, second_core)
    act_grad_far = act_grad_of(cot_far, cot_both)
    stay(cot_far, cot_both, act_grad_far)
    second_far = after(second_far, act_grad_far)
    second_both = swap(second_far, "tensor", 1)
    act_y, pre_y, up_bias_y, far_hold = feed((second_far,), act_grad_far, 0, (F32,))
    stay(act_y, pre_y, second_far, far_hold)
    act_both, pre_both, up_bias_both, far_send = feed((second_both,), act_grad_far, rows, (BF,))
    leave(far_hold)
    far_sum = add_round(far_hold, swap(far_send, "tensor", 1))
    arrived_far = swap(far_sum, "tensor", 2)
    leave(act_grad_far, up_weight)
    stay(act_both, pre_both, second_both)
    acts, cots = (act_near, act_y, act_both), (cot, cot_core, cot_far, cot_both)
    down_send = weight_grad(after(me, far_sum), acts, cots, ORDER_A, False)
    down = Reduction(down_send, ORDER_A)
    seconds = (second, second_core, second_far, second_both)
    pres = (pre_near, pre_y, pre_both)
    up_send = weight_grad(after(me, down_send), seconds, pres, ORDER_B, False)
    up = Reduction(up_send, ORDER_B)
    arrived_near = swap(near_send, "tensor", 1)
    feed_send, feed_hold = feed_back(after(me, up_send), act_y, act_both)
    feed_far = add_round(feed_hold, swap(feed_send, "tensor", 1))
    middle_grad, middle_low, middle_sums = run(
        middle_back,
        (
            after(me, feed_hold), near_hold, arrived_near, arrived_far, middle, cot, vectors,
        ),
        [shape((rows, model)), shape((rows, model), BF), shape((4, model))],
        scratch=[pltpu.VMEM((4, 8, model), F32)],
    )

    mid_far = swap(middle_low, "tensor", 2)
    mid_core = swap(middle_low, "tensor", 1)
    grads = pltpu.VMEM((side, width), BF)
    leave(near_hold)
    stay(middle_grad, middle_low)
    down.values = weight_grad(after(me, middle_low), acts, cots, ORDER_A, True)
    leave(act_y, act_both, cot_core, cot_far, cot_both)
    stay(down.values)
    near_q, near_keys = run(
        back_near,
        (after(me, down.values), middle_low, mid_core, qkv, probs_near, out_weight),
        [shape((side, width)), shape((2 * side, 2 * width))],
        scratch=[grads],
        flops=back_flops,
    )
    leave(probs_near)
    stay(near_q, near_keys, mid_core)
    up.values = weight_grad(after(me, near_q), seconds, pres, ORDER_B, True)
    leave(second, second_core, second_far, second_both, pre_near, pre_y, pre_both)
    stay(up.values)
    mid_far = after(mid_far, up.values)
    mid_both = swap(mid_far, "tensor", 1)
    feed_far = swap(after(feed_far, mid_far), "tensor", 2)
    down.arrive(mid_far)
    up.arrive(mid_far)
    flat_near, flat_far, bias_grad, far_send, far_hold = run(
        back_far,
        (
            after(me, down.send, up.send), mid_far, mid_both, qkv, probs_far,
            out_weight, near_q, near_keys, in_weight,
        ),
        [
            shape((side, 3 * width), BF),
            shape((side, 3 * width), BF),
            shape((1, 2 * width)),
            shape((rows, model), BF),
            shape((rows, model)),
        ],
        scratch=[
            grads,
            pltpu.VMEM((side, width), F32),
            pltpu.VMEM((2 * side, 2 * width), F32),
            pltpu.VMEM((side, 3 * width), BF),
        ],
        flops=back_flops + project_flops,
    )
    leave(qkv, probs_far, near_q, near_keys, out_weight)
    stay(flat_near, flat_far, mid_far, mid_both)
    down.take(bias_grad)
    up.take(bias_grad)
    arrived = after(swap(far_send, "tensor", 1), feed_far, down.came, up.came)
    far_sum = add_round(far_hold, arrived)
    arrived_far = swap(far_sum, "tensor", 2)

    down.arrive(far_sum)
    up.arrive(far_sum)
    near_send, hold = run(
        first_back,
        (after(me, down.send, up.send), flat_near, in_weight),
        [shape((rows, model), BF), shape((rows, model))],
        flops=project_flops,
    )
    leave(in_weight)
    stay(hold)
    normed = (norm_near, norm_y, norm_both)
    split = (3 * width + width) // 2
    flat = (flat_near, flat_far)
    head_rows = (heads_near, heads_far)
    mids = (middle_low, mid_core, mid_far, mid_both)
    arrived_near = swap(near_send, "tensor", 1)
    first_send = weight_grad(after(me, hold), normed, flat, ORDER_A, False, 0, split)
    first = Reduction(first_send, ORDER_A)
    mixed_send = mixed_grad(
        after(me, first_send), normed, flat, head_rows, mids, ORDER_B, False, split
    )
    mixed = Reduction(mixed_send, ORDER_B)
    first.values = weight_grad(after(me, mixed_send), normed, flat, ORDER_A, True, 0, split)
    stay(first.values)
    mixed.values = mixed_grad(
        after(me, first.values, arrived_near), normed, flat, head_rows, mids, ORDER_B, True, split
    )
    leave(norm_near, norm_y, norm_both, flat_near, flat_far, heads_near, heads_far)
    leave(middle_low, mid_core, mid_far, mid_both)
    stay(mixed.values)
    tokens_grad, token_sums = run(
        token_back,
        (
            after(me, mixed.values), hold, arrived_near, arrived_far, tokens, middle_grad, vectors,
        ),
        [shape((rows, model)), shape((2, model))],
        scratch=[pltpu.VMEM((2, 8, model), F32)],
    )
    leave(hold, tokens, middle_grad, vectors)
    feed_send, feed_hold = feed_back(after(me, token_sums), act_near)
    feed_rows = feed_hold + swap(feed_send, "tensor", 1).astype(F32) + feed_far.astype(F32)
    output = (keep_own * (middle + feed_rows + down_bias)).astype(BF)
    leave(*STAY)
    stay(down.values, up.values, first.values, mixed.values)

    now = down.arrive(feed_hold)
    shared = pack(jnp.concatenate([middle_sums, token_sums], axis=0))
    shared = add_small(shared, after(swap(shared, "tensor", 1), now))
    now = first.arrive(now)
    now = mixed.arrive(now)
    shared = unpack(add_small(shared, after(swap(shared, "tensor", 2), now)))
    own = jnp.concatenate(
        [up_bias_near + up_bias_y + up_bias_both, jnp.pad(bias_grad, ((0, 0), (0, hidden - 2 * width)))], axis=0
    )
    small = jnp.concatenate([shared, own], axis=0)
    small = pack(jnp.concatenate([small[:, :split], small[:, split:]], axis=0))
    now = up.arrive(now)
    now = down.arrive(now)
    now = mixed.arrive(now)
    now = first.arrive(now)
    now = up.arrive(now)
    now = mixed.arrive(now)
    now = first.arrive(now)
    while first.at < first.count:
        now = first.arrive(now)
    first.join(small)
    now = down.arrive(now)
    now = up.arrive(now)
    now = mixed.arrive(now)
    now = first.arrive(now)
    now = first.arrive(now)
    now = mixed.arrive(now)
    now = down.arrive(now)
    down_sum = place(after(me, now), down.parts, ORDER_A)
    up.arrive(down_sum)
    up_sum = place(me, up.parts, ORDER_B)
    outs = [shape((model, 3 * width)), shape((width, model))]
    into = place_mixed(after(me, up_sum), 0, first.values, mixed.values, outs)
    now = mixed.arrive(into[1])
    first.arrive(now)
    small = unpack(first.small)
    small = jnp.concatenate([small[:8], small[8:]], axis=1)
    piece = model // PIECES
    in_sum, out_sum = place_mixed(me, 1, first.parts[1], mixed.parts[1], outs, into)
    in_bias_sum = small[7, : 2 * width].reshape(2, heads, HD).transpose(1, 0, 2).reshape(-1)
    return (
        output,
        tokens_grad,
        in_sum,
        in_bias_sum,
        out_sum,
        small[0],
        up_sum,
        small[6],
        down_sum,
        small[1],
        small[4],
        small[5],
        small[2],
        small[3],
    )


def solution(mesh):
    rows = P(("dp", "tensor"), None)
    placed = (
        rows,
        P("dp", None),
        rows,
        P(None, "tensor"),
        P("tensor"),
        P("tensor", None),
        P(),
        P(None, "tensor"),
        P("tensor"),
        P("tensor", None),
        P(),
        P(),
        P(),
        P(),
        P(),
    )
    given = (
        rows,
        rows,
        P(None, "tensor"),
        P("tensor"),
        P("tensor", None),
        P(),
        P(None, "tensor"),
        P("tensor"),
        P("tensor", None),
        P(),
        P(),
        P(),
        P(),
        P(),
    )
    return jax.shard_map(on_device, mesh=mesh, in_specs=placed, out_specs=given, check_vma=False)
```

```python
import functools

import jax
import jax.numpy as jnp
from jax import lax
from jax.experimental import pallas as pl
from jax.experimental.pallas import tpu as pltpu
from jax.sharding import PartitionSpec as P

HD = 64
SLOTS = 320
HALF = SLOTS // 2
PIECES = 8
EPSILON = 1e-06
BF = jnp.bfloat16
F32 = jnp.float32
MIB = 1 << 20


def mm(left, right, dims=((1,), (0,))):
    return lax.dot_general(left, right, (dims, ((), ())), preferred_element_type=F32)


NT = ((1,), (1,))
TN = ((0,), (0,))


def swap(values, axis, bit):
    count = lax.axis_size(axis)
    return lax.ppermute(values, axis, [(i, i ^ bit) for i in range(count)])


def after(values, *earlier):
    return lax.optimization_barrier((values, *earlier))[0]


def shape(dims, kind=F32):
    return jax.ShapeDtypeStruct(dims, kind)


STAY = []


def stay(*arrays):
    STAY.extend(arrays)


def leave(*arrays):
    for array in arrays:
        STAY[:] = [x for x in STAY if x is not array]


def run(body, operands, outs, scratch=(), flops=0, room=12):
    used = list(operands[1:])
    waiting = [x for x in STAY if all(x is not y for y in used)]
    ins = [pltpu.with_memory_space_constraint(x, pltpu.VMEM) for x in [*used, *waiting]]
    moved = sum(x.size * x.dtype.itemsize for x in [*used, *outs])

    def kernel(*refs):
        own = 1 + len(used)
        body(*refs[:own], *refs[own + len(waiting) :])

    return pl.pallas_call(
        kernel,
        out_shape=[pltpu.VMEM(x.shape, x.dtype) for x in outs],
        in_specs=[pl.BlockSpec(memory_space=pltpu.SMEM)]
        + [pl.BlockSpec(memory_space=pltpu.VMEM)] * len(ins),
        out_specs=[pl.BlockSpec(memory_space=pltpu.VMEM)] * len(outs),
        scratch_shapes=scratch,
        compiler_params=pltpu.CompilerParams(vmem_limit_bytes=room * MIB),
        cost_estimate=pl.CostEstimate(
            flops=int(flops * WEIGHT), bytes_accessed=0, transcendentals=0
        ),
    )(operands[0], *ins)


WEIGHT = 20


def add_low(me, left, right, out):
    out[...] = (left[...] + right[...].astype(F32)).astype(BF)


def add_round(left, right):
    return run(add_low, (jnp.zeros((1,), jnp.int32), left, right), [shape(left.shape, BF)])[0]


def add_halves(me, left, right, send, hold):
    middle = send.shape[0]
    send[...] = (left[middle:, :] + right[middle:, :].astype(F32)).astype(BF)
    hold[...] = left[:middle, :] + right[:middle, :].astype(F32)


def run_out(body, operands, outs, scratch=(), room=16):
    ins = [pltpu.with_memory_space_constraint(x, pltpu.VMEM) for x in operands[1:]]
    return pl.pallas_call(
        body,
        out_shape=[pltpu.HBM(x.shape, x.dtype) for x in outs],
        in_specs=[pl.BlockSpec(memory_space=pltpu.SMEM)]
        + [pl.BlockSpec(memory_space=pltpu.VMEM)] * len(ins),
        out_specs=[pl.BlockSpec(memory_space=pltpu.HBM)] * len(outs),
        scratch_shapes=scratch,
        compiler_params=pltpu.CompilerParams(vmem_limit_bytes=room * MIB),
        cost_estimate=pl.CostEstimate(
            flops=int(1e9 * WEIGHT), bytes_accessed=0, transcendentals=0
        ),
    )(operands[0], *ins)


def blocks(count, size, step):
    def one(i, carry):
        step(pl.ds(pl.multiple_of(i * size, size), size), i)
        return carry

    lax.fori_loop(0, count, one, 0)


def row_tiles(rows, size, step):
    def one(i, carry):
        step(pl.ds(pl.multiple_of(i * size, size), size))
        return carry

    lax.fori_loop(0, rows // size, one, 0)


def normalise(values):
    average = jnp.mean(values, axis=-1, keepdims=True)
    centred = values - average
    factor = lax.rsqrt(jnp.mean(centred * centred, axis=-1, keepdims=True) + EPSILON)
    return centred * factor, factor


def norm_back(grad, gain, z, factor):
    s = grad * gain
    return factor * (
        s - jnp.mean(s, axis=-1, keepdims=True) - z * jnp.mean(s * z, axis=-1, keepdims=True)
    )


def fold(values):
    return functools.reduce(
        lambda a, b: a + b, [values[i : i + 8] for i in range(0, values.shape[0], 8)]
    )


GAIN_ONE, SHIFT_ONE, OUT_BIAS, GAIN_TWO, SHIFT_TWO, UP_BIAS, DOWN_BIAS = range(7)


def row(vectors, number):
    return vectors[number : number + 1, :]


def project_side(blocks, vectors, weight, bias, normed, put):
    rows = blocks[0].shape[0]
    width = weight.shape[1] // 3
    for i, block in enumerate(blocks):

        def step(at, block=block, i=i):
            z, _ = normalise(block[at, :].astype(F32))
            tile = pl.ds(pl.multiple_of(at.start + i * rows, 16), at.size)
            normed[tile, :] = (z * row(vectors, GAIN_ONE) + row(vectors, SHIFT_ONE)).astype(BF)

        row_tiles(rows, 48, step)
        found = (mm(normed[i * rows : (i + 1) * rows, :], weight[...]) + bias[...]).astype(BF)
        kinds = [
            [found[:, (3 * head + kind) * HD :][:, :HD] for head in range(width // HD)]
            for kind in range(3)
        ]
        put(i, jnp.concatenate(sum(kinds, []), axis=1))


def project_local(me, tok_a, tok_b, vectors, weight, bias, normed, proj):
    rows = tok_a.shape[0]

    def put(i, values):
        proj[i * rows : (i + 1) * rows, :] = values

    project_side((tok_a, tok_b), vectors, weight, bias, normed, put)


def attend(side, qkv, keep, probs, heads_out):
    half_lane = lax.broadcasted_iota(jnp.int32, (1, 2 * HD), 1) // HD
    width = qkv.shape[1] // 3

    def one(j, carry):
        place = 3 * side + j
        image = place // 2
        queries = pl.ds(pl.multiple_of(place * HALF, 16), HALF)
        keys = pl.ds(pl.multiple_of(image * SLOTS, 16), SLOTS)
        live = keep[pl.ds(image, 1), :] > 0
        for pair in range(width // (2 * HD)):
            lanes = pl.ds(pair * 2 * HD, 2 * HD)
            q = qkv[queries, lanes] * 0.125
            k = qkv[keys, pl.ds(width + pair * 2 * HD, 2 * HD)]
            v = qkv[keys, pl.ds(2 * width + pair * 2 * HD, 2 * HD)]
            outs = []
            for e in range(2):
                scores = mm(jnp.where(half_lane == e, q, jnp.zeros_like(q)), k, NT)
                scores = jnp.where(live, scores, -1000000000.0)
                power = jnp.exp(scores - jnp.max(scores, axis=-1, keepdims=True))
                p = (power / jnp.sum(power, axis=-1, keepdims=True)).astype(BF)
                probs[j * 4 + pair * 2 + e] = p
                outs.append(mm(p, v))
            heads_out[pl.ds(pl.multiple_of(j * HALF, 16), HALF), lanes] = jnp.where(
                half_lane == 0, outs[0], outs[1]
            ).astype(BF)
        return carry

    lax.fori_loop(0, 3, one, 0)


def out_project(core, heads_out, weight, send, hold):
    rows = send.shape[0]
    send[...] = mm(
        heads_out[pl.ds(pl.multiple_of((1 - core) * rows, 16), rows), :], weight[...]
    ).astype(BF)
    hold[...] = mm(heads_out[pl.ds(pl.multiple_of(core * rows, 16), rows), :], weight[...])


def project_one(me, tok, vectors, weight, bias, normed, proj):
    def put(i, values):
        proj[...] = values

    project_side((tok,), vectors, weight, bias, normed, put)


def attend_far(
    me, near, first, tok, vectors, weight, bias, keep, out_w,
    normed, qkv, probs, heads_out, send, hold,
):
    rows = tok.shape[0]
    core, far = me[0] & 1, me[0] >> 1
    for i in range(2):
        at = pl.multiple_of((2 * far + (core ^ i)) * rows, 16)
        qkv[pl.ds(at, rows), :] = near[i * rows : (i + 1) * rows, :]
    at = pl.multiple_of((2 * (1 - far) + core) * rows, 16)
    qkv[pl.ds(at, rows), :] = first[...]

    def put(i, values):
        at = pl.multiple_of((2 * (1 - far) + (1 - core)) * rows, 16)
        qkv[pl.ds(at, rows), :] = values

    project_side((tok,), vectors, weight, bias, normed, put)
    attend(1 - far, qkv, keep, probs, heads_out)
    out_project(core, heads_out, out_w, send, hold)


def attend_near(me, qkv, keep, out_w, probs, heads_out, send, hold):
    core, far = me[0] & 1, me[0] >> 1
    attend(far, qkv, keep, probs, heads_out)
    out_project(core, heads_out, out_w, send, hold)


def second_norm(me, tok, hold, near, far, vectors, middle, second):
    def step(at):
        total = hold[at, :] + near[at, :].astype(F32) + far[at, :].astype(F32)
        values = tok[at, :].astype(F32) + total + row(vectors, OUT_BIAS)
        middle[at, :] = values
        z, _ = normalise(values)
        second[at, :] = (z * row(vectors, GAIN_TWO) + row(vectors, SHIFT_TWO)).astype(BF)

    row_tiles(tok.shape[0], 48, step)


def act_back(me, cot_a, cot_b, down, act_grad):
    rows = cot_a.shape[0]

    def step(at, i):
        act_grad[:rows, at] = mm(cot_a[...], down[at, :], NT)
        act_grad[rows:, at] = mm(cot_b[...], down[at, :], NT)

    blocks(down.shape[0] // 256, 256, step)


def feed_forward(low, count, me, *refs):
    norms = refs[:count]
    up, vectors, act_grad, act, pre_low, bias_grad = refs[count : count + 6]
    outs, total, pre = refs[count + 6 : 2 * count + 6], refs[-2], refs[-1]
    rows = norms[0].shape[0]
    wide = pre.shape[2]
    number = up.shape[1] // wide
    bias_grad[...] = jnp.zeros_like(bias_grad)
    total[...] = jnp.zeros_like(total)

    def columns(i):
        return pl.ds(pl.multiple_of(i * wide, wide), wide)

    def elements(slot, at, block):
        own_bias = vectors[UP_BIAS : UP_BIAS + 1, at]
        sums = None
        for i in range(0, rows, 16):
            to = pl.ds(block * rows + i, 16)
            x = pre[slot, i : i + 16, :] + own_bias
            share = 0.5 + 0.5 * lax.erf(x * 0.7071067811865476)
            slope = share + x * (0.3989422804014327 * jnp.exp(-0.5 * x * x))
            act[to, at] = (x * share).astype(BF)
            grad = act_grad[pl.ds(low + block * rows + i, 16), at] * slope
            pre_low[to, at] = grad.astype(BF)
            part = grad[:8] + grad[8:]
            sums = part if sums is None else sums + part
        bias_grad[:, at] += jnp.sum(sums, axis=0, keepdims=True)

    pre[0] = mm(norms[0][...], up[:, :wide])

    def one(i, carry):
        if count == 2:
            steps = ((i, 0), (i, 1), (jnp.minimum(i + 1, number - 1), 0))
        else:
            steps = ((2 * i, 0), (2 * i + 1, 0), (jnp.minimum(2 * i + 2, number - 1), 0))
        for slot in range(2):
            column, block = steps[slot]
            later, other = steps[slot + 1]
            pre[1 - slot] = mm(norms[other][...], up[:, columns(later)])
            elements(slot, columns(column), block)
            inside = pl.ds(block * rows, rows)
            total[inside, :] += mm(pre_low[inside, columns(column)], up[:, columns(column)], NT)
        return carry

    lax.fori_loop(0, number * count // 2, one, 0)
    for i, out in enumerate(outs):
        out[...] = total[i * rows : (i + 1) * rows, :].astype(out.dtype)


def feed_out(count, me, *refs):
    acts, (down, send, hold) = refs[:count], refs[count:]
    rows = send.shape[0]
    one = acts[-1][rows:, :] if count == 1 else acts[1][...]
    send[...] = mm(one, down[...]).astype(BF)
    hold[...] = mm(acts[0][:rows, :], down[...])


def gather_pieces(me, lefts, order, base, turned):
    piece = lefts[0].shape[1] // PIECES
    for i in range(PIECES // 2):
        at = pl.ds(pl.multiple_of(piece_of(base + i, order, me[1]) * piece, piece), piece)
        for left, to in zip(lefts, turned, strict=True):
            to[i * piece : (i + 1) * piece, :] = left[:, at].T


def segments(lefts, rights):
    found, left, right, a, b = [], 0, 0, 0, 0
    while left < len(lefts):
        rows = min(lefts[left].shape[0] - a, rights[right].shape[0] - b)
        found.append((left, a, right, b, rows))
        a, b = a + rows, b + rows
        if a == lefts[left].shape[0]:
            left, a = left + 1, 0
        if b == rights[right].shape[0]:
            right, b = right + 1, 0
    return found


def weight_pieces(order, base, low, count, me, *refs):
    lefts, rights = refs[: count[0]], refs[count[0] : sum(count)]
    out, turned = refs[sum(count)], refs[sum(count) + 1 :]
    gather_pieces(me, lefts, order, base, turned)

    def step(at, i):
        found = None
        from_ = pl.ds(pl.multiple_of(at.start + low, 128), at.size)
        for left, a, right, b, rows in segments(lefts, rights):
            part = mm(turned[left][:, a : a + rows], rights[right][b : b + rows, from_])
            found = part if found is None else found + part
        out[:, at] = found.astype(out.dtype)

    blocks(out.shape[1] // 256, 256, step)


def mixed_pieces(order, base, low, me, *refs):
    lefts, rights, heads, mids, out = refs[:3], refs[3:5], refs[5:7], refs[7:11], refs[11]
    turned = refs[12:]
    gather_pieces(me, lefts, order, base, turned)
    width = rights[0].shape[1] - low
    for at in range(0, width, 256):
        found = None
        for left, a, right, b, rows in segments(lefts, rights):
            part = mm(
                turned[left][:, a : a + rows],
                rights[right][b : b + rows, low + at : low + at + 256],
            )
            found = part if found is None else found + part
        out[:, at : at + 256] = found.astype(out.dtype)
    core = me[0] & 1
    rows = mids[0].shape[0]
    piece = mids[0].shape[1] // PIECES
    half = heads[0].shape[1] // 2
    for i in range(PIECES // 2):
        at = pl.ds(pl.multiple_of(piece_of(base + i, order, me[1]) * piece, piece), piece)
        both = None
        for k in range(4):
            inside = pl.ds(pl.multiple_of((core ^ (k % 2)) * rows, 16), rows)
            part = mm(heads[k // 2][inside, :], mids[k][:, at], TN)
            both = part if both is None else both + part
        to = pl.ds(i * piece, piece)
        out[to, width : width + half] = both[:half].astype(out.dtype)
        out[to, width + half :] = both[half:].astype(out.dtype)


def middle_back(me, hold, near, far, middle, cot_low, vectors, middle_grad, middle_low, sums, parts):
    parts[...] = jnp.zeros_like(parts)

    def step(at):
        second = hold[at, :] + near[at, :].astype(F32) + far[at, :].astype(F32)
        z, factor = normalise(middle[at, :])
        cot = cot_low[at, :].astype(F32)
        total = cot + norm_back(second, row(vectors, GAIN_TWO), z, factor)
        middle_grad[at, :] = total
        middle_low[at, :] = total.astype(BF)
        parts[0] += fold(total)
        parts[1] += fold(cot)
        parts[2] += fold(second * z)
        parts[3] += fold(second)

    row_tiles(hold.shape[0], 48, step)
    for i in range(4):
        sums[i : i + 1, :] = jnp.sum(parts[i], axis=0, keepdims=True)


def attend_back(side, mid_blocks, core, qkv, probs, out_w, grads, pg_q, keys_grad):
    rows = mid_blocks[0].shape[0]
    half_lane = lax.broadcasted_iota(jnp.int32, (1, 2 * HD), 1) // HD
    width = qkv.shape[1] // 3
    for i, block in enumerate(mid_blocks):
        at = pl.multiple_of((core ^ i) * rows, 16)
        grads[pl.ds(at, rows), :] = mm(block[...], out_w[...], NT).astype(BF)

    def one(j, carry):
        place = 3 * side + j
        image = place // 2
        inside = pl.ds(pl.multiple_of(j * HALF, 16), HALF)
        queries = pl.ds(pl.multiple_of(place * HALF, 16), HALF)
        keys = pl.ds(pl.multiple_of(image * SLOTS, 16), SLOTS)
        for pair in range(width // (2 * HD)):
            lanes = pl.ds(pair * 2 * HD, 2 * HD)
            q = qkv[queries, lanes]
            k = qkv[keys, pl.ds(width + pair * 2 * HD, 2 * HD)]
            v = qkv[keys, pl.ds(2 * width + pair * 2 * HD, 2 * HD)]
            g = grads[inside, lanes]
            found = []
            for e in range(2):
                p = probs[j * 4 + pair * 2 + e]
                wide = p.astype(F32)
                prob_grad = mm(jnp.where(half_lane == e, g, jnp.zeros_like(g)), v, NT)
                delta = jnp.sum(wide * prob_grad, axis=-1, keepdims=True)
                score_grad = (wide * (prob_grad - delta) * 0.125).astype(BF)
                found.append(
                    (mm(score_grad, k), mm(score_grad, q, TN), mm(p, g, TN))
                )
            q_grad, k_grad, v_grad = (
                jnp.where(half_lane == 0, a, b) for a, b in zip(*found, strict=True)
            )
            pg_q[inside, lanes] = q_grad
            keys_grad[keys, lanes] += k_grad
            keys_grad[keys, pl.ds(width + pair * 2 * HD, 2 * HD)] += v_grad
        return carry

    lax.fori_loop(0, 3, one, 0)


def back_near(me, mid_a, mid_b, qkv, probs, out_w, pg_q, keys_grad, grads):
    core, far = me[0] & 1, me[0] >> 1
    keys_grad[...] = jnp.zeros_like(keys_grad)
    attend_back(far, (mid_a, mid_b), core, qkv, probs, out_w, grads, pg_q, keys_grad)


def back_far(
    me, mid_a, mid_b, qkv, probs, out_w, near_q, near_keys, in_w,
    flat_near, flat_far, bias_grad, send, hold, grads, far_q, keys_grad, group,
):
    core, far = me[0] & 1, me[0] >> 1
    rows = mid_a.shape[0]
    width = far_q.shape[1]
    keys_grad[...] = near_keys[...]
    attend_back(1 - far, (mid_a, mid_b), core, qkv, probs, out_w, grads, far_q, keys_grad)
    bias_grad[...] = jnp.concatenate(
        [
            jnp.sum(far_q[...], axis=0, keepdims=True) + jnp.sum(near_q[...], axis=0, keepdims=True),
            jnp.sum(keys_grad[:, width:], axis=0, keepdims=True),
        ],
        axis=1,
    )
    for side, (flat, q_part) in enumerate(((flat_near, near_q), (flat_far, far_q))):
        for i in range(2):
            inside = pl.multiple_of((core ^ i) * rows, 16)
            place = pl.multiple_of((2 * (far ^ side) + (core ^ i)) * rows, 16)
            to = pl.ds(i * rows, rows)
            group[to, :width] = q_part[pl.ds(inside, rows), :].astype(BF)
            group[to, width:] = keys_grad[pl.ds(place, rows), :].astype(BF)
        for head in range(width // HD):
            for kind in range(3):
                at = (head * 3 + kind) * HD
                flat[:, at : at + HD] = group[:, kind * width + head * HD :][:, :HD]
    send[...] = mm(flat_far[rows:, :], in_w[...], NT).astype(BF)
    hold[...] = mm(flat_far[:rows, :], in_w[...], NT)


def first_back(me, proj, in_w, send, hold):
    rows = send.shape[0]
    send[...] = mm(proj[rows:, :], in_w[...], NT).astype(BF)
    hold[...] = mm(proj[:rows, :], in_w[...], NT)


def mixed_piece(me, norm_a, norm_b, proj_a, proj_b, heads_a, heads_b, mid_a, mid_b, out):
    width = proj_a.shape[1]
    out[:, :width] = (
        mm(norm_a[...], proj_a[...], TN) + mm(norm_b[...], proj_b[...], TN)
    ).astype(out.dtype)
    both = mm(heads_a[...], mid_a[...], TN) + mm(heads_b[...], mid_b[...], TN)
    half = both.shape[0] // 2
    out[:, width : width + half] = both[:half].astype(out.dtype)
    out[:, width + half :] = both[half:].astype(out.dtype)


def token_back(me, hold, near, far, tok, middle_grad, vectors, tokens_grad, sums, parts):
    parts[...] = jnp.zeros_like(parts)

    def step(at):
        first = hold[at, :] + near[at, :].astype(F32) + far[at, :].astype(F32)
        z, factor = normalise(tok[at, :].astype(F32))
        tokens_grad[at, :] = middle_grad[at, :] + norm_back(
            first, row(vectors, GAIN_ONE), z, factor
        )
        parts[0] += fold(first * z)
        parts[1] += fold(first)

    row_tiles(hold.shape[0], 48, step)
    for i in range(2):
        sums[i : i + 1, :] = jnp.sum(parts[i], axis=0, keepdims=True)


def place_pieces(order, me, *refs):
    parts, out, wide, sems = refs[:-3], refs[-3], refs[-2], refs[-1]
    piece = out.shape[0] // PIECES
    copies = []
    for i in range(PIECES):
        part, row = locate(parts, i * piece)
        wide[i] = part[row : row + piece, :].astype(F32)
        to = pl.ds(pl.multiple_of(piece_of(i, order, me[1]) * piece, piece), piece)
        copies.append(pltpu.make_async_copy(wide.at[i], out.at[to, :], sems.at[i]))
        copies[-1].start()
    for copy in copies:
        copy.wait()


def locate(parts, row):
    for part in parts:
        if row < part.shape[0]:
            return part, row
        row -= part.shape[0]


def place_half(half, count, order, other, me, first, second, *refs):
    in_out, out_out, wide, flat, sems = refs[count:]
    piece = in_out.shape[0] // PIECES
    middle = out_out.shape[0] // 2
    split = first.shape[1]
    rest = in_out.shape[1] - split
    copies = []
    for i in range(PIECES // 2):
        part = pl.ds(i * piece, piece)
        place = piece_of(half * PIECES // 2 + i, order, me[1])
        to = pl.ds(pl.multiple_of(place * piece, piece), piece)
        wide[i, :, :split] = first[part, :].astype(F32)
        copies.append(
            pltpu.make_async_copy(wide.at[i, :, :split], in_out.at[to, :split], sems.at[3 * i])
        )
        copies[-1].start()
        place = piece_of(half * PIECES // 2 + i, other, me[1])
        to = pl.ds(pl.multiple_of(place * piece, piece), piece)
        wide[i, :, split:] = second[part, :rest].astype(F32)
        flat[i, :middle, :] = second[part, rest : rest + middle].astype(F32)
        flat[i, middle:, :] = second[part, rest + middle :].astype(F32)
        copies.append(
            pltpu.make_async_copy(wide.at[i, :, split:], in_out.at[to, split:], sems.at[3 * i + 1])
        )
        copies[-1].start()
        copies.append(
            pltpu.make_async_copy(flat.at[i], out_out.at[:, to], sems.at[3 * i + 2])
        )
        copies[-1].start()
    for copy in copies:
        copy.wait()


def place_mixed(me, half, first, second, outs, into=()):
    ins = [pltpu.with_memory_space_constraint(x, pltpu.VMEM) for x in (first, second)]
    half_pieces = PIECES // 2
    tall, wide = outs[0].shape
    return pl.pallas_call(
        functools.partial(place_half, half, len(into), ORDER_A, ORDER_B),
        out_shape=[pltpu.HBM(x.shape, x.dtype) for x in outs],
        in_specs=[pl.BlockSpec(memory_space=pltpu.SMEM)]
        + [pl.BlockSpec(memory_space=pltpu.VMEM)] * 2
        + [pl.BlockSpec(memory_space=pltpu.HBM)] * len(into),
        out_specs=[pl.BlockSpec(memory_space=pltpu.HBM)] * 2,
        scratch_shapes=[
            pltpu.VMEM((half_pieces, tall // PIECES, wide), F32),
            pltpu.VMEM((half_pieces, outs[1].shape[0], tall // PIECES), F32),
            pltpu.SemaphoreType.DMA((3 * half_pieces,)),
        ],
        input_output_aliases={3: 0, 4: 1} if into else {},
        compiler_params=pltpu.CompilerParams(vmem_limit_bytes=16 * MIB),
        cost_estimate=pl.CostEstimate(
            flops=int(1e9 * WEIGHT), bytes_accessed=0, transcendentals=0
        ),
    )(me, *ins, *into)


def piece_of(position, order, me):
    relative = 0
    for step, bit in enumerate(order):
        relative = relative | (((position >> (len(order) - 1 - step)) & 1) << bit)
    return relative ^ (me & (PIECES - 1))


def pack(values):
    high = lax.reduce_precision(values, exponent_bits=8, mantissa_bits=7)
    return jnp.concatenate([high.astype(BF), (values - high).astype(BF)], axis=0)


def add_small(own, other):
    return pack(unpack(own) + unpack(other))


def unpack(packed):
    half = packed.shape[0] // 2
    return packed[:half].astype(F32) + packed[half:].astype(F32)


class Reduction:
    def __init__(self, send, order):
        self.send, self.order = send, order
        self.count = lax.axis_size("dp").bit_length() - 1
        self.bits = [*order, *range(len(order), self.count), *reversed(order)]
        self.values, self.small, self.came, self.at = None, None, None, 0

    def take(self, *earlier):
        self.came = swap(self.send, "dp", 1 << self.bits[self.at])
        if earlier:
            self.came = after(self.came, *earlier)
        return self.came

    def arrive(self, *earlier):
        found = self.step(*earlier)
        while len(self.order) <= self.at < self.count:
            found = self.step(found)
        return found

    def step(self, *earlier):
        if self.came is None:
            self.take()
        arrived = after(self.came, *earlier)
        self.came = None
        self.at += 1
        halving = len(self.order)
        if self.at < halving:
            dims = (self.values.shape[0] // 2, self.values.shape[1])
            leave(self.values)
            self.send, self.values = run(
                add_halves,
                (jnp.zeros((1,), jnp.int32), self.values, arrived),
                [shape(dims, BF), shape(dims)],
            )
            stay(self.values)
        elif self.at == halving:
            leave(self.values)
            self.values = add_round(self.values, arrived)
            self.send = self.values
        elif self.at <= self.count:
            self.values = (self.values.astype(F32) + arrived.astype(F32)).astype(BF)
            self.send = self.values
        else:
            rows = self.values.shape[0]
            if self.small is not None:
                self.small = pack(unpack(self.small) + unpack(arrived[rows:]))
            if self.at == len(self.bits):
                self.parts = (self.values, arrived)
                return arrived
            self.values = jnp.concatenate([self.values, arrived[:rows]], axis=0)
            self.send = self.values
            if self.small is not None:
                self.send = jnp.concatenate([self.values, self.small], axis=0)
        return self.send

    def join(self, small):
        for bit in range(len(self.order), self.count):
            small = pack(unpack(small) + unpack(swap(small, "dp", 1 << bit)))
        self.small = small
        self.send = jnp.concatenate([self.values, small], axis=0)


ORDER_A = (0, 1, 2)
ORDER_B = (1, 0, 2)


def weight_grad(me, lefts, rights, order, kept, low=0, wide=None):
    half = lefts[0].shape[1] // 2
    wide = wide or rights[0].shape[1]
    count = (len(lefts), len(rights))
    return run(
        functools.partial(weight_pieces, order, 0 if kept else PIECES // 2, low, count),
        (me, *lefts, *rights),
        [shape((half, wide), F32 if kept else BF)],
        scratch=[pltpu.VMEM((half, x.shape[0]), BF) for x in lefts],
        flops=2 * 960 * half * wide,
    )[0]


def mixed_grad(me, normed, proj, heads, mids, order, kept, low):
    half = normed[0].shape[1] // 2
    wide = proj[0].shape[1] - low + heads[0].shape[1]
    return run(
        functools.partial(mixed_pieces, order, 0 if kept else PIECES // 2, low),
        (me, *normed, *proj, *heads, *mids),
        [shape((half, wide), F32 if kept else BF)],
        scratch=[pltpu.VMEM((half, x.shape[0]), BF) for x in normed],
        flops=2 * 960 * half * wide,
    )[0]


def place(me, parts, order):
    rows, wide = 2 * parts[0].shape[0], parts[0].shape[1]
    return run_out(
        functools.partial(place_pieces, order),
        (me, *parts),
        [shape((rows, wide))],
        scratch=[
            pltpu.VMEM((PIECES, rows // PIECES, wide), F32),
            pltpu.SemaphoreType.DMA((PIECES,)),
        ],
    )[0]


def on_device(
    tokens,
    keep_mask,
    grad_out,
    in_weight,
    in_bias,
    out_weight,
    out_bias,
    up_weight,
    up_bias,
    down_weight,
    down_bias,
    gain_one,
    shift_one,
    gain_two,
    shift_two,
):
    rows, model = tokens.shape
    leave(*STAY)
    me = jnp.stack([lax.axis_index("tensor"), lax.axis_index("dp")]).astype(jnp.int32)
    images = keep_mask.shape[0]
    heads = in_weight.shape[1] // (3 * HD)
    width = heads * HD
    hidden = up_weight.shape[1]

    def line(values):
        return values.reshape(1, -1)

    side = 2 * rows
    block = 512
    project_flops = 2 * side * model * 3 * width
    attend_flops = 3 * heads * 4 * HALF * SLOTS * 128 + 2 * side * width * model
    back_flops = 3 * heads * 10 * HALF * SLOTS * 128 + 2 * side * width * model

    def act_grad_of(one, other):
        return run(
            act_back,
            (me, one, other, down_weight),
            [shape((side, hidden))],
            flops=2 * side * model * hidden,
        )[0]

    def feed(norms, act_grad, low, kinds):
        tall = rows * len(norms)
        return run(
            functools.partial(feed_forward, low, len(norms)),
            (me, *norms, up_weight, vectors, act_grad),
            [
                shape((tall, hidden), BF),
                shape((tall, hidden), BF),
                shape((1, hidden)),
                *[shape((rows, model), kind) for kind in kinds],
            ],
            scratch=[pltpu.VMEM((tall, model), F32), pltpu.VMEM((2, rows, block), F32)],
            flops=4 * tall * model * hidden,
        )

    def feed_back(me, *acts):
        return run(
            functools.partial(feed_out, len(acts)),
            (me, *acts, down_weight),
            [shape((rows, model), BF), shape((rows, model))],
            flops=2 * side * model * hidden,
        )

    tok_far = swap(tokens, "tensor", 2)
    tok_core = swap(tokens, "tensor", 1)
    keep_flat = keep_mask.reshape(-1).astype(F32)
    keep_own = lax.dynamic_slice_in_dim(keep_flat, me[0] * rows, rows)[:, None]
    cot = (grad_out.astype(F32) * keep_own).astype(BF)
    cot_core = swap(cot, "tensor", 1)
    pair = in_bias.reshape(heads, 2, HD)
    bias_full = jnp.concatenate([pair[:, :1], jnp.zeros((heads, 1, HD), F32), pair[:, 1:]], axis=1)
    bias_full = bias_full.reshape(1, 3 * width)
    vectors = jnp.stack(
        [gain_one, shift_one, out_bias, gain_two, shift_two, up_bias, down_bias, down_bias]
    )
    stay(in_weight, bias_full, vectors, tokens, cot)
    norm_near, proj_near = run(
        project_local,
        (me, tokens, tok_core, vectors, in_weight, bias_full),
        [shape((side, model), BF), shape((side, 3 * width), BF)],
        flops=project_flops,
    )
    stay(norm_near, out_weight)
    tok_far = after(tok_far, proj_near)

    tok_both = swap(tok_far, "tensor", 1)
    cot_far = swap(after(cot, tok_far), "tensor", 2)
    attend_outs = [
        shape((3 * heads, HALF, SLOTS), BF),
        shape((side, width), BF),
        shape((rows, model), BF),
        shape((rows, model), F32),
    ]
    norm_y, proj_y = run(
        project_one,
        (me, tok_far, vectors, in_weight, bias_full),
        [shape((rows, model), BF), shape((rows, 3 * width), BF)],
        flops=project_flops // 2,
    )
    stay(norm_y)
    norm_both, qkv, probs_far, heads_far, send, far_hold = run(
        attend_far,
        (
            me, proj_near, proj_y, tok_both, vectors, in_weight, bias_full, keep_mask, out_weight,
        ),
        [shape((rows, model), BF), shape((2 * side, 3 * width), BF), *attend_outs],
        flops=project_flops + attend_flops,
    )
    stay(norm_both, qkv, probs_far, heads_far, down_weight, up_weight)
    leave(bias_full)
    arrived = after(swap(send, "tensor", 1), cot_far)
    far_sum = add_round(far_hold, arrived)
    cot_far = after(cot_far, far_sum)
    cot_both = swap(cot_far, "tensor", 1)
    arrived_far = swap(far_sum, "tensor", 2)
    probs_near, heads_near, send, hold = run(
        attend_near,
        (after(me, far_sum), qkv, keep_mask, out_weight),
        attend_outs,
        flops=attend_flops,
    )
    stay(probs_near, heads_near, hold)
    act_grad_near = act_grad_of(cot, cot_core)
    stay(act_grad_near, cot_core)
    arrived_near = after(swap(send, "tensor", 1), arrived_far)
    middle, second = run(
        second_norm,
        (
            after(me, act_grad_near), tokens, hold, arrived_near, arrived_far, vectors,
        ),
        [shape((rows, model)), shape((rows, model), BF)],
    )

    leave(hold)
    stay(middle, second)

    second_far = swap(second, "tensor", 2)
    second_core = swap(second, "tensor", 1)
    act_near, pre_near, up_bias_near, near_hold, near_send = feed(
        (second, second_core), act_grad_near, 0, (F32, BF)
    )
    leave(act_grad_near)
    stay(act_near, pre_near, near_hold, second_core)
    act_grad_far = act_grad_of(cot_far, cot_both)
    stay(cot_far, cot_both, act_grad_far)
    second_far = after(second_far, act_grad_far)
    second_both = swap(second_far, "tensor", 1)
    act_y, pre_y, up_bias_y, far_hold = feed((second_far,), act_grad_far, 0, (F32,))
    stay(act_y, pre_y, second_far, far_hold)
    act_both, pre_both, up_bias_both, far_send = feed((second_both,), act_grad_far, rows, (BF,))
    leave(far_hold)
    far_sum = add_round(far_hold, swap(far_send, "tensor", 1))
    arrived_far = swap(far_sum, "tensor", 2)
    leave(act_grad_far, up_weight)
    stay(act_both, pre_both, second_both)
    acts, cots = (act_near, act_y, act_both), (cot, cot_core, cot_far, cot_both)
    down_send = weight_grad(after(me, far_sum), acts, cots, ORDER_A, False)
    down = Reduction(down_send, ORDER_A)
    seconds = (second, second_core, second_far, second_both)
    pres = (pre_near, pre_y, pre_both)
    up_send = weight_grad(after(me, down_send), seconds, pres, ORDER_B, False)
    up = Reduction(up_send, ORDER_B)
    arrived_near = swap(near_send, "tensor", 1)
    feed_send, feed_hold = feed_back(after(me, up_send), act_y, act_both)
    feed_far = add_round(feed_hold, swap(feed_send, "tensor", 1))
    middle_grad, middle_low, middle_sums = run(
        middle_back,
        (
            after(me, feed_hold), near_hold, arrived_near, arrived_far, middle, cot, vectors,
        ),
        [shape((rows, model)), shape((rows, model), BF), shape((4, model))],
        scratch=[pltpu.VMEM((4, 8, model), F32)],
    )

    mid_far = swap(middle_low, "tensor", 2)
    mid_core = swap(middle_low, "tensor", 1)
    grads = pltpu.VMEM((side, width), BF)
    leave(near_hold)
    stay(middle_grad, middle_low)
    down.values = weight_grad(after(me, middle_low), acts, cots, ORDER_A, True)
    leave(act_y, act_both, cot_core, cot_far, cot_both)
    stay(down.values)
    near_q, near_keys = run(
        back_near,
        (after(me, down.values), middle_low, mid_core, qkv, probs_near, out_weight),
        [shape((side, width)), shape((2 * side, 2 * width))],
        scratch=[grads],
        flops=back_flops,
    )
    leave(probs_near)
    stay(near_q, near_keys, mid_core)
    up.values = weight_grad(after(me, near_q), seconds, pres, ORDER_B, True)
    leave(second, second_core, second_far, second_both, pre_near, pre_y, pre_both)
    stay(up.values)
    mid_far = after(mid_far, up.values)
    mid_both = swap(mid_far, "tensor", 1)
    feed_far = swap(after(feed_far, mid_far), "tensor", 2)
    down.arrive(mid_far)
    up.arrive(mid_far)
    flat_near, flat_far, bias_grad, far_send, far_hold = run(
        back_far,
        (
            after(me, down.send, up.send), mid_far, mid_both, qkv, probs_far,
            out_weight, near_q, near_keys, in_weight,
        ),
        [
            shape((side, 3 * width), BF),
            shape((side, 3 * width), BF),
            shape((1, 2 * width)),
            shape((rows, model), BF),
            shape((rows, model)),
        ],
        scratch=[
            grads,
            pltpu.VMEM((side, width), F32),
            pltpu.VMEM((2 * side, 2 * width), F32),
            pltpu.VMEM((side, 3 * width), BF),
        ],
        flops=back_flops + project_flops,
    )
    leave(qkv, probs_far, near_q, near_keys, out_weight)
    stay(flat_near, flat_far, mid_far, mid_both)
    down.take(bias_grad)
    up.take(bias_grad)
    arrived = after(swap(far_send, "tensor", 1), feed_far, down.came, up.came)
    far_sum = add_round(far_hold, arrived)
    arrived_far = swap(far_sum, "tensor", 2)

    down.arrive(far_sum)
    up.arrive(far_sum)
    near_send, hold = run(
        first_back,
        (after(me, down.send, up.send), flat_near, in_weight),
        [shape((rows, model), BF), shape((rows, model))],
        flops=project_flops,
    )
    leave(in_weight)
    stay(hold)
    normed = (norm_near, norm_y, norm_both)
    split = (3 * width + width) // 2
    flat = (flat_near, flat_far)
    head_rows = (heads_near, heads_far)
    mids = (middle_low, mid_core, mid_far, mid_both)
    arrived_near = swap(near_send, "tensor", 1)
    first_send = weight_grad(after(me, hold), normed, flat, ORDER_A, False, 0, split)
    first = Reduction(first_send, ORDER_A)
    mixed_send = mixed_grad(
        after(me, first_send), normed, flat, head_rows, mids, ORDER_B, False, split
    )
    mixed = Reduction(mixed_send, ORDER_B)
    first.values = weight_grad(after(me, mixed_send), normed, flat, ORDER_A, True, 0, split)
    stay(first.values)
    mixed.values = mixed_grad(
        after(me, first.values, arrived_near), normed, flat, head_rows, mids, ORDER_B, True, split
    )
    leave(norm_near, norm_y, norm_both, flat_near, flat_far, heads_near, heads_far)
    leave(middle_low, mid_core, mid_far, mid_both)
    stay(mixed.values)
    tokens_grad, token_sums = run(
        token_back,
        (
            after(me, mixed.values), hold, arrived_near, arrived_far, tokens, middle_grad, vectors,
        ),
        [shape((rows, model)), shape((2, model))],
        scratch=[pltpu.VMEM((2, 8, model), F32)],
    )
    leave(hold, tokens, middle_grad, vectors)
    feed_send, feed_hold = feed_back(after(me, token_sums), act_near)
    feed_rows = feed_hold + swap(feed_send, "tensor", 1).astype(F32) + feed_far.astype(F32)
    output = (keep_own * (middle + feed_rows + down_bias)).astype(BF)
    leave(*STAY)
    stay(down.values, up.values, first.values, mixed.values)

    now = down.arrive(feed_hold)
    shared = pack(jnp.concatenate([middle_sums, token_sums], axis=0))
    shared = add_small(shared, after(swap(shared, "tensor", 1), now))
    now = first.arrive(now)
    now = mixed.arrive(now)
    shared = unpack(add_small(shared, after(swap(shared, "tensor", 2), now)))
    own = jnp.concatenate(
        [up_bias_near + up_bias_y + up_bias_both, jnp.pad(bias_grad, ((0, 0), (0, hidden - 2 * width)))], axis=0
    )
    small = jnp.concatenate([shared, own], axis=0)
    small = pack(jnp.concatenate([small[:, :split], small[:, split:]], axis=0))
    now = up.arrive(now)
    now = down.arrive(now)
    now = mixed.arrive(now)
    now = first.arrive(now)
    now = up.arrive(now)
    now = mixed.arrive(now)
    now = first.arrive(now)
    while first.at < first.count:
        now = first.arrive(now)
    first.join(small)
    now = down.arrive(now)
    now = up.arrive(now)
    now = mixed.arrive(now)
    now = first.arrive(now)
    now = first.arrive(now)
    now = mixed.arrive(now)
    now = down.arrive(now)
    down_sum = place(after(me, now), down.parts, ORDER_A)
    up.arrive(down_sum)
    up_sum = place(me, up.parts, ORDER_B)
    outs = [shape((model, 3 * width)), shape((width, model))]
    into = place_mixed(after(me, up_sum), 0, first.values, mixed.values, outs)
    now = mixed.arrive(into[1])
    first.arrive(now)
    small = unpack(first.small)
    small = jnp.concatenate([small[:8], small[8:]], axis=1)
    piece = model // PIECES
    in_sum, out_sum = place_mixed(me, 1, first.parts[1], mixed.parts[1], outs, into)
    in_bias_sum = small[7, : 2 * width].reshape(2, heads, HD).transpose(1, 0, 2).reshape(-1)
    return (
        output,
        tokens_grad,
        in_sum,
        in_bias_sum,
        out_sum,
        small[0],
        up_sum,
        small[6],
        down_sum,
        small[1],
        small[4],
        small[5],
        small[2],
        small[3],
    )


def solution(mesh):
    rows = P(("dp", "tensor"), None)
    placed = (
        rows,
        P("dp", None),
        rows,
        P(None, "tensor"),
        P("tensor"),
        P("tensor", None),
        P(),
        P(None, "tensor"),
        P("tensor"),
        P("tensor", None),
        P(),
        P(),
        P(),
        P(),
        P(),
    )
    given = (
        rows,
        rows,
        P(None, "tensor"),
        P("tensor"),
        P("tensor", None),
        P(),
        P(None, "tensor"),
        P("tensor"),
        P("tensor", None),
        P(),
        P(),
        P(),
        P(),
        P(),
    )
    return jax.shard_map(on_device, mesh=mesh, in_specs=placed, out_specs=given, check_vma=False)
```

```python
import functools

import jax
import jax.numpy as jnp
from jax import lax
from jax.experimental import pallas as pl
from jax.experimental.pallas import tpu as pltpu
from jax.sharding import PartitionSpec as P

HD = 64
SLOTS = 320
HALF = SLOTS // 2
PIECES = 8
EPSILON = 1e-06
BF = jnp.bfloat16
F32 = jnp.float32
MIB = 1 << 20


def mm(left, right, dims=((1,), (0,))):
    return lax.dot_general(left, right, (dims, ((), ())), preferred_element_type=F32)


NT = ((1,), (1,))
TN = ((0,), (0,))


def swap(values, axis, bit):
    count = lax.axis_size(axis)
    return lax.ppermute(values, axis, [(i, i ^ bit) for i in range(count)])


def after(values, *earlier):
    return lax.optimization_barrier((values, *earlier))[0]


def shape(dims, kind=F32):
    return jax.ShapeDtypeStruct(dims, kind)


STAY = []


def stay(*arrays):
    STAY.extend(arrays)


def leave(*arrays):
    for array in arrays:
        STAY[:] = [x for x in STAY if x is not array]


def run(body, operands, outs, scratch=(), flops=0, room=12):
    used = list(operands[1:])
    waiting = [x for x in STAY if all(x is not y for y in used)]
    ins = [pltpu.with_memory_space_constraint(x, pltpu.VMEM) for x in [*used, *waiting]]
    moved = sum(x.size * x.dtype.itemsize for x in [*used, *outs])

    def kernel(*refs):
        own = 1 + len(used)
        body(*refs[:own], *refs[own + len(waiting) :])

    return pl.pallas_call(
        kernel,
        out_shape=[pltpu.VMEM(x.shape, x.dtype) for x in outs],
        in_specs=[pl.BlockSpec(memory_space=pltpu.SMEM)]
        + [pl.BlockSpec(memory_space=pltpu.VMEM)] * len(ins),
        out_specs=[pl.BlockSpec(memory_space=pltpu.VMEM)] * len(outs),
        scratch_shapes=scratch,
        compiler_params=pltpu.CompilerParams(vmem_limit_bytes=room * MIB),
        cost_estimate=pl.CostEstimate(
            flops=int(flops * WEIGHT), bytes_accessed=0, transcendentals=0
        ),
    )(operands[0], *ins)


WEIGHT = 20


def add_low(me, left, right, out):
    out[...] = (left[...] + right[...].astype(F32)).astype(BF)


def add_round(left, right):
    return run(add_low, (jnp.zeros((1,), jnp.int32), left, right), [shape(left.shape, BF)])[0]


def add_halves(me, left, right, send, hold):
    middle = send.shape[0]
    send[...] = (left[middle:, :] + right[middle:, :].astype(F32)).astype(BF)
    hold[...] = left[:middle, :] + right[:middle, :].astype(F32)


def run_out(body, operands, outs, scratch=(), room=16):
    ins = [pltpu.with_memory_space_constraint(x, pltpu.VMEM) for x in operands[1:]]
    return pl.pallas_call(
        body,
        out_shape=[pltpu.HBM(x.shape, x.dtype) for x in outs],
        in_specs=[pl.BlockSpec(memory_space=pltpu.SMEM)]
        + [pl.BlockSpec(memory_space=pltpu.VMEM)] * len(ins),
        out_specs=[pl.BlockSpec(memory_space=pltpu.HBM)] * len(outs),
        scratch_shapes=scratch,
        compiler_params=pltpu.CompilerParams(vmem_limit_bytes=room * MIB),
        cost_estimate=pl.CostEstimate(
            flops=int(1e9 * WEIGHT), bytes_accessed=0, transcendentals=0
        ),
    )(operands[0], *ins)


def blocks(count, size, step):
    def one(i, carry):
        step(pl.ds(pl.multiple_of(i * size, size), size), i)
        return carry

    lax.fori_loop(0, count, one, 0)


def row_tiles(rows, size, step):
    def one(i, carry):
        step(pl.ds(pl.multiple_of(i * size, size), size))
        return carry

    lax.fori_loop(0, rows // size, one, 0)


def normalise(values):
    average = jnp.mean(values, axis=-1, keepdims=True)
    centred = values - average
    factor = lax.rsqrt(jnp.mean(centred * centred, axis=-1, keepdims=True) + EPSILON)
    return centred * factor, factor


def norm_back(grad, gain, z, factor):
    s = grad * gain
    return factor * (
        s - jnp.mean(s, axis=-1, keepdims=True) - z * jnp.mean(s * z, axis=-1, keepdims=True)
    )


def fold(values):
    return functools.reduce(
        lambda a, b: a + b, [values[i : i + 8] for i in range(0, values.shape[0], 8)]
    )


GAIN_ONE, SHIFT_ONE, OUT_BIAS, GAIN_TWO, SHIFT_TWO, UP_BIAS, DOWN_BIAS = range(7)


def row(vectors, number):
    return vectors[number : number + 1, :]


def project_side(blocks, vectors, weight, bias, normed, put):
    rows = blocks[0].shape[0]
    width = weight.shape[1] // 3
    for i, block in enumerate(blocks):

        def step(at, block=block, i=i):
            z, _ = normalise(block[at, :].astype(F32))
            tile = pl.ds(pl.multiple_of(at.start + i * rows, 16), at.size)
            normed[tile, :] = (z * row(vectors, GAIN_ONE) + row(vectors, SHIFT_ONE)).astype(BF)

        row_tiles(rows, 48, step)
        found = (mm(normed[i * rows : (i + 1) * rows, :], weight[...]) + bias[...]).astype(BF)
        kinds = [
            [found[:, (3 * head + kind) * HD :][:, :HD] for head in range(width // HD)]
            for kind in range(3)
        ]
        put(i, jnp.concatenate(sum(kinds, []), axis=1))


def project_local(me, tok_a, tok_b, vectors, weight, bias, normed, proj):
    rows = tok_a.shape[0]

    def put(i, values):
        proj[i * rows : (i + 1) * rows, :] = values

    project_side((tok_a, tok_b), vectors, weight, bias, normed, put)


def attend(side, qkv, keep, probs, heads_out):
    half_lane = lax.broadcasted_iota(jnp.int32, (1, 2 * HD), 1) // HD
    width = qkv.shape[1] // 3

    def one(j, carry):
        place = 3 * side + j
        image = place // 2
        queries = pl.ds(pl.multiple_of(place * HALF, 16), HALF)
        keys = pl.ds(pl.multiple_of(image * SLOTS, 16), SLOTS)
        live = keep[pl.ds(image, 1), :] > 0
        for pair in range(width // (2 * HD)):
            lanes = pl.ds(pair * 2 * HD, 2 * HD)
            q = qkv[queries, lanes] * 0.125
            k = qkv[keys, pl.ds(width + pair * 2 * HD, 2 * HD)]
            v = qkv[keys, pl.ds(2 * width + pair * 2 * HD, 2 * HD)]
            outs = []
            for e in range(2):
                scores = mm(jnp.where(half_lane == e, q, jnp.zeros_like(q)), k, NT)
                scores = jnp.where(live, scores, -1000000000.0)
                power = jnp.exp(scores - jnp.max(scores, axis=-1, keepdims=True))
                p = (power / jnp.sum(power, axis=-1, keepdims=True)).astype(BF)
                probs[j * 4 + pair * 2 + e] = p
                outs.append(mm(p, v))
            heads_out[pl.ds(pl.multiple_of(j * HALF, 16), HALF), lanes] = jnp.where(
                half_lane == 0, outs[0], outs[1]
            ).astype(BF)
        return carry

    lax.fori_loop(0, 3, one, 0)


def out_project(core, heads_out, weight, send, hold):
    rows = send.shape[0]
    send[...] = mm(
        heads_out[pl.ds(pl.multiple_of((1 - core) * rows, 16), rows), :], weight[...]
    ).astype(BF)
    hold[...] = mm(heads_out[pl.ds(pl.multiple_of(core * rows, 16), rows), :], weight[...])


def project_one(me, tok, vectors, weight, bias, normed, proj):
    def put(i, values):
        proj[...] = values

    project_side((tok,), vectors, weight, bias, normed, put)


def attend_far(
    me, near, first, tok, vectors, weight, bias, keep, out_w,
    normed, qkv, probs, heads_out, send, hold,
):
    rows = tok.shape[0]
    core, far = me[0] & 1, me[0] >> 1
    for i in range(2):
        at = pl.multiple_of((2 * far + (core ^ i)) * rows, 16)
        qkv[pl.ds(at, rows), :] = near[i * rows : (i + 1) * rows, :]
    at = pl.multiple_of((2 * (1 - far) + core) * rows, 16)
    qkv[pl.ds(at, rows), :] = first[...]

    def put(i, values):
        at = pl.multiple_of((2 * (1 - far) + (1 - core)) * rows, 16)
        qkv[pl.ds(at, rows), :] = values

    project_side((tok,), vectors, weight, bias, normed, put)
    attend(1 - far, qkv, keep, probs, heads_out)
    out_project(core, heads_out, out_w, send, hold)


def attend_near(me, qkv, keep, out_w, probs, heads_out, send, hold):
    core, far = me[0] & 1, me[0] >> 1
    attend(far, qkv, keep, probs, heads_out)
    out_project(core, heads_out, out_w, send, hold)


def second_norm(me, tok, hold, near, far, vectors, middle, second):
    def step(at):
        total = hold[at, :] + near[at, :].astype(F32) + far[at, :].astype(F32)
        values = tok[at, :].astype(F32) + total + row(vectors, OUT_BIAS)
        middle[at, :] = values
        z, _ = normalise(values)
        second[at, :] = (z * row(vectors, GAIN_TWO) + row(vectors, SHIFT_TWO)).astype(BF)

    row_tiles(tok.shape[0], 48, step)


def act_back(me, cot_a, cot_b, down, act_grad):
    rows = cot_a.shape[0]

    def step(at, i):
        act_grad[:rows, at] = mm(cot_a[...], down[at, :], NT)
        act_grad[rows:, at] = mm(cot_b[...], down[at, :], NT)

    blocks(down.shape[0] // 256, 256, step)


def feed_forward(low, count, me, *refs):
    norms = refs[:count]
    up, vectors, act_grad, act, pre_low, bias_grad = refs[count : count + 6]
    outs, total, pre = refs[count + 6 : 2 * count + 6], refs[-2], refs[-1]
    rows = norms[0].shape[0]
    wide = pre.shape[2]
    number = up.shape[1] // wide
    bias_grad[...] = jnp.zeros_like(bias_grad)
    total[...] = jnp.zeros_like(total)

    def columns(i):
        return pl.ds(pl.multiple_of(i * wide, wide), wide)

    def elements(slot, at, block):
        own_bias = vectors[UP_BIAS : UP_BIAS + 1, at]
        sums = None
        for i in range(0, rows, 16):
            to = pl.ds(block * rows + i, 16)
            x = pre[slot, i : i + 16, :] + own_bias
            share = 0.5 + 0.5 * lax.erf(x * 0.7071067811865476)
            slope = share + x * (0.3989422804014327 * jnp.exp(-0.5 * x * x))
            act[to, at] = (x * share).astype(BF)
            grad = act_grad[pl.ds(low + block * rows + i, 16), at] * slope
            pre_low[to, at] = grad.astype(BF)
            part = grad[:8] + grad[8:]
            sums = part if sums is None else sums + part
        bias_grad[:, at] += jnp.sum(sums, axis=0, keepdims=True)

    pre[0] = mm(norms[0][...], up[:, :wide])

    def one(i, carry):
        if count == 2:
            steps = ((i, 0), (i, 1), (jnp.minimum(i + 1, number - 1), 0))
        else:
            steps = ((2 * i, 0), (2 * i + 1, 0), (jnp.minimum(2 * i + 2, number - 1), 0))
        for slot in range(2):
            column, block = steps[slot]
            later, other = steps[slot + 1]
            pre[1 - slot] = mm(norms[other][...], up[:, columns(later)])
            elements(slot, columns(column), block)
            inside = pl.ds(block * rows, rows)
            total[inside, :] += mm(pre_low[inside, columns(column)], up[:, columns(column)], NT)
        return carry

    lax.fori_loop(0, number * count // 2, one, 0)
    for i, out in enumerate(outs):
        out[...] = total[i * rows : (i + 1) * rows, :].astype(out.dtype)


def feed_out(count, me, *refs):
    acts, (down, send, hold) = refs[:count], refs[count:]
    rows = send.shape[0]
    one = acts[-1][rows:, :] if count == 1 else acts[1][...]
    send[...] = mm(one, down[...]).astype(BF)
    hold[...] = mm(acts[0][:rows, :], down[...])


def gather_pieces(me, lefts, order, base, turned):
    piece = lefts[0].shape[1] // PIECES
    for i in range(PIECES // 2):
        at = pl.ds(pl.multiple_of(piece_of(base + i, order, me[1]) * piece, piece), piece)
        for left, to in zip(lefts, turned, strict=True):
            to[i * piece : (i + 1) * piece, :] = left[:, at].T


def segments(lefts, rights):
    found, left, right, a, b = [], 0, 0, 0, 0
    while left < len(lefts):
        rows = min(lefts[left].shape[0] - a, rights[right].shape[0] - b)
        found.append((left, a, right, b, rows))
        a, b = a + rows, b + rows
        if a == lefts[left].shape[0]:
            left, a = left + 1, 0
        if b == rights[right].shape[0]:
            right, b = right + 1, 0
    return found


def weight_pieces(order, base, low, count, me, *refs):
    lefts, rights = refs[: count[0]], refs[count[0] : sum(count)]
    out, turned = refs[sum(count)], refs[sum(count) + 1 :]
    gather_pieces(me, lefts, order, base, turned)

    def step(at, i):
        found = None
        from_ = pl.ds(pl.multiple_of(at.start + low, 128), at.size)
        for left, a, right, b, rows in segments(lefts, rights):
            part = mm(turned[left][:, a : a + rows], rights[right][b : b + rows, from_])
            found = part if found is None else found + part
        out[:, at] = found.astype(out.dtype)

    blocks(out.shape[1] // 256, 256, step)


def mixed_pieces(order, base, low, me, *refs):
    lefts, rights, heads, mids, out = refs[:3], refs[3:5], refs[5:7], refs[7:11], refs[11]
    turned = refs[12:]
    gather_pieces(me, lefts, order, base, turned)
    width = rights[0].shape[1] - low
    for at in range(0, width, 256):
        found = None
        for left, a, right, b, rows in segments(lefts, rights):
            part = mm(
                turned[left][:, a : a + rows],
                rights[right][b : b + rows, low + at : low + at + 256],
            )
            found = part if found is None else found + part
        out[:, at : at + 256] = found.astype(out.dtype)
    core = me[0] & 1
    rows = mids[0].shape[0]
    piece = mids[0].shape[1] // PIECES
    half = heads[0].shape[1] // 2
    for i in range(PIECES // 2):
        at = pl.ds(pl.multiple_of(piece_of(base + i, order, me[1]) * piece, piece), piece)
        both = None
        for k in range(4):
            inside = pl.ds(pl.multiple_of((core ^ (k % 2)) * rows, 16), rows)
            part = mm(heads[k // 2][inside, :], mids[k][:, at], TN)
            both = part if both is None else both + part
        to = pl.ds(i * piece, piece)
        out[to, width : width + half] = both[:half].astype(out.dtype)
        out[to, width + half :] = both[half:].astype(out.dtype)


def middle_back(me, hold, near, far, middle, cot_low, vectors, middle_grad, middle_low, sums, parts):
    parts[...] = jnp.zeros_like(parts)

    def step(at):
        second = hold[at, :] + near[at, :].astype(F32) + far[at, :].astype(F32)
        z, factor = normalise(middle[at, :])
        cot = cot_low[at, :].astype(F32)
        total = cot + norm_back(second, row(vectors, GAIN_TWO), z, factor)
        middle_grad[at, :] = total
        middle_low[at, :] = total.astype(BF)
        parts[0] += fold(total)
        parts[1] += fold(cot)
        parts[2] += fold(second * z)
        parts[3] += fold(second)

    row_tiles(hold.shape[0], 48, step)
    for i in range(4):
        sums[i : i + 1, :] = jnp.sum(parts[i], axis=0, keepdims=True)


def attend_back(side, mid_blocks, core, qkv, probs, out_w, grads, pg_q, keys_grad):
    rows = mid_blocks[0].shape[0]
    half_lane = lax.broadcasted_iota(jnp.int32, (1, 2 * HD), 1) // HD
    width = qkv.shape[1] // 3
    for i, block in enumerate(mid_blocks):
        at = pl.multiple_of((core ^ i) * rows, 16)
        grads[pl.ds(at, rows), :] = mm(block[...], out_w[...], NT).astype(BF)

    def one(j, carry):
        place = 3 * side + j
        image = place // 2
        inside = pl.ds(pl.multiple_of(j * HALF, 16), HALF)
        queries = pl.ds(pl.multiple_of(place * HALF, 16), HALF)
        keys = pl.ds(pl.multiple_of(image * SLOTS, 16), SLOTS)
        for pair in range(width // (2 * HD)):
            lanes = pl.ds(pair * 2 * HD, 2 * HD)
            q = qkv[queries, lanes]
            k = qkv[keys, pl.ds(width + pair * 2 * HD, 2 * HD)]
            v = qkv[keys, pl.ds(2 * width + pair * 2 * HD, 2 * HD)]
            g = grads[inside, lanes]
            found = []
            for e in range(2):
                p = probs[j * 4 + pair * 2 + e]
                wide = p.astype(F32)
                prob_grad = mm(jnp.where(half_lane == e, g, jnp.zeros_like(g)), v, NT)
                delta = jnp.sum(wide * prob_grad, axis=-1, keepdims=True)
                score_grad = (wide * (prob_grad - delta) * 0.125).astype(BF)
                found.append(
                    (mm(score_grad, k), mm(score_grad, q, TN), mm(p, g, TN))
                )
            q_grad, k_grad, v_grad = (
                jnp.where(half_lane == 0, a, b) for a, b in zip(*found, strict=True)
            )
            pg_q[inside, lanes] = q_grad
            keys_grad[keys, lanes] += k_grad
            keys_grad[keys, pl.ds(width + pair * 2 * HD, 2 * HD)] += v_grad
        return carry

    lax.fori_loop(0, 3, one, 0)


def back_near(me, mid_a, mid_b, qkv, probs, out_w, pg_q, keys_grad, grads):
    core, far = me[0] & 1, me[0] >> 1
    keys_grad[...] = jnp.zeros_like(keys_grad)
    attend_back(far, (mid_a, mid_b), core, qkv, probs, out_w, grads, pg_q, keys_grad)


def back_far(
    me, mid_a, mid_b, qkv, probs, out_w, near_q, near_keys, in_w,
    flat_near, flat_far, bias_grad, send, hold, grads, far_q, keys_grad, group,
):
    core, far = me[0] & 1, me[0] >> 1
    rows = mid_a.shape[0]
    width = far_q.shape[1]
    keys_grad[...] = near_keys[...]
    attend_back(1 - far, (mid_a, mid_b), core, qkv, probs, out_w, grads, far_q, keys_grad)
    bias_grad[...] = jnp.concatenate(
        [
            jnp.sum(far_q[...], axis=0, keepdims=True) + jnp.sum(near_q[...], axis=0, keepdims=True),
            jnp.sum(keys_grad[:, width:], axis=0, keepdims=True),
        ],
        axis=1,
    )
    for side, (flat, q_part) in enumerate(((flat_near, near_q), (flat_far, far_q))):
        for i in range(2):
            inside = pl.multiple_of((core ^ i) * rows, 16)
            place = pl.multiple_of((2 * (far ^ side) + (core ^ i)) * rows, 16)
            to = pl.ds(i * rows, rows)
            group[to, :width] = q_part[pl.ds(inside, rows), :].astype(BF)
            group[to, width:] = keys_grad[pl.ds(place, rows), :].astype(BF)
        for head in range(width // HD):
            for kind in range(3):
                at = (head * 3 + kind) * HD
                flat[:, at : at + HD] = group[:, kind * width + head * HD :][:, :HD]
    send[...] = mm(flat_far[rows:, :], in_w[...], NT).astype(BF)
    hold[...] = mm(flat_far[:rows, :], in_w[...], NT)


def first_back(me, proj, in_w, send, hold):
    rows = send.shape[0]
    send[...] = mm(proj[rows:, :], in_w[...], NT).astype(BF)
    hold[...] = mm(proj[:rows, :], in_w[...], NT)


def mixed_piece(me, norm_a, norm_b, proj_a, proj_b, heads_a, heads_b, mid_a, mid_b, out):
    width = proj_a.shape[1]
    out[:, :width] = (
        mm(norm_a[...], proj_a[...], TN) + mm(norm_b[...], proj_b[...], TN)
    ).astype(out.dtype)
    both = mm(heads_a[...], mid_a[...], TN) + mm(heads_b[...], mid_b[...], TN)
    half = both.shape[0] // 2
    out[:, width : width + half] = both[:half].astype(out.dtype)
    out[:, width + half :] = both[half:].astype(out.dtype)


def token_back(me, hold, near, far, tok, middle_grad, vectors, tokens_grad, sums, parts):
    parts[...] = jnp.zeros_like(parts)

    def step(at):
        first = hold[at, :] + near[at, :].astype(F32) + far[at, :].astype(F32)
        z, factor = normalise(tok[at, :].astype(F32))
        tokens_grad[at, :] = middle_grad[at, :] + norm_back(
            first, row(vectors, GAIN_ONE), z, factor
        )
        parts[0] += fold(first * z)
        parts[1] += fold(first)

    row_tiles(hold.shape[0], 48, step)
    for i in range(2):
        sums[i : i + 1, :] = jnp.sum(parts[i], axis=0, keepdims=True)


def place_pieces(order, me, *refs):
    parts, out, wide, sems = refs[:-3], refs[-3], refs[-2], refs[-1]
    piece = out.shape[0] // PIECES
    copies = []
    for i in range(PIECES):
        part, row = locate(parts, i * piece)
        wide[i] = part[row : row + piece, :].astype(F32)
        to = pl.ds(pl.multiple_of(piece_of(i, order, me[1]) * piece, piece), piece)
        copies.append(pltpu.make_async_copy(wide.at[i], out.at[to, :], sems.at[i]))
        copies[-1].start()
    for copy in copies:
        copy.wait()


def locate(parts, row):
    for part in parts:
        if row < part.shape[0]:
            return part, row
        row -= part.shape[0]


def place_half(half, count, order, other, me, first, second, *refs):
    in_out, out_out, wide, flat, sems = refs[count:]
    piece = in_out.shape[0] // PIECES
    middle = out_out.shape[0] // 2
    split = first.shape[1]
    rest = in_out.shape[1] - split
    copies = []
    for i in range(PIECES // 2):
        part = pl.ds(i * piece, piece)
        place = piece_of(half * PIECES // 2 + i, order, me[1])
        to = pl.ds(pl.multiple_of(place * piece, piece), piece)
        wide[i, :, :split] = first[part, :].astype(F32)
        copies.append(
            pltpu.make_async_copy(wide.at[i, :, :split], in_out.at[to, :split], sems.at[3 * i])
        )
        copies[-1].start()
        place = piece_of(half * PIECES // 2 + i, other, me[1])
        to = pl.ds(pl.multiple_of(place * piece, piece), piece)
        wide[i, :, split:] = second[part, :rest].astype(F32)
        flat[i, :middle, :] = second[part, rest : rest + middle].astype(F32)
        flat[i, middle:, :] = second[part, rest + middle :].astype(F32)
        copies.append(
            pltpu.make_async_copy(wide.at[i, :, split:], in_out.at[to, split:], sems.at[3 * i + 1])
        )
        copies[-1].start()
        copies.append(
            pltpu.make_async_copy(flat.at[i], out_out.at[:, to], sems.at[3 * i + 2])
        )
        copies[-1].start()
    for copy in copies:
        copy.wait()


def place_mixed(me, half, first, second, outs, into=()):
    ins = [pltpu.with_memory_space_constraint(x, pltpu.VMEM) for x in (first, second)]
    half_pieces = PIECES // 2
    tall, wide = outs[0].shape
    return pl.pallas_call(
        functools.partial(place_half, half, len(into), ORDER_A, ORDER_B),
        out_shape=[pltpu.HBM(x.shape, x.dtype) for x in outs],
        in_specs=[pl.BlockSpec(memory_space=pltpu.SMEM)]
        + [pl.BlockSpec(memory_space=pltpu.VMEM)] * 2
        + [pl.BlockSpec(memory_space=pltpu.HBM)] * len(into),
        out_specs=[pl.BlockSpec(memory_space=pltpu.HBM)] * 2,
        scratch_shapes=[
            pltpu.VMEM((half_pieces, tall // PIECES, wide), F32),
            pltpu.VMEM((half_pieces, outs[1].shape[0], tall // PIECES), F32),
            pltpu.SemaphoreType.DMA((3 * half_pieces,)),
        ],
        input_output_aliases={3: 0, 4: 1} if into else {},
        compiler_params=pltpu.CompilerParams(vmem_limit_bytes=16 * MIB),
        cost_estimate=pl.CostEstimate(
            flops=int(1e9 * WEIGHT), bytes_accessed=0, transcendentals=0
        ),
    )(me, *ins, *into)


def piece_of(position, order, me):
    relative = 0
    for step, bit in enumerate(order):
        relative = relative | (((position >> (len(order) - 1 - step)) & 1) << bit)
    return relative ^ (me & (PIECES - 1))


def pack(values):
    high = lax.reduce_precision(values, exponent_bits=8, mantissa_bits=7)
    return jnp.concatenate([high.astype(BF), (values - high).astype(BF)], axis=0)


def add_small(own, other):
    return pack(unpack(own) + unpack(other))


def unpack(packed):
    half = packed.shape[0] // 2
    return packed[:half].astype(F32) + packed[half:].astype(F32)


class Reduction:
    def __init__(self, send, order):
        self.send, self.order = send, order
        self.count = lax.axis_size("dp").bit_length() - 1
        self.bits = [*order, *range(len(order), self.count), *reversed(order)]
        self.values, self.small, self.came, self.at = None, None, None, 0

    def take(self, *earlier):
        self.came = swap(self.send, "dp", 1 << self.bits[self.at])
        if earlier:
            self.came = after(self.came, *earlier)
        return self.came

    def arrive(self, *earlier):
        found = self.step(*earlier)
        while len(self.order) <= self.at < self.count:
            found = self.step(found)
        return found

    def step(self, *earlier):
        if self.came is None:
            self.take()
        arrived = after(self.came, *earlier)
        self.came = None
        self.at += 1
        halving = len(self.order)
        if self.at < halving:
            dims = (self.values.shape[0] // 2, self.values.shape[1])
            leave(self.values)
            self.send, self.values = run(
                add_halves,
                (jnp.zeros((1,), jnp.int32), self.values, arrived),
                [shape(dims, BF), shape(dims)],
            )
            stay(self.values)
        elif self.at == halving:
            leave(self.values)
            self.values = add_round(self.values, arrived)
            self.send = self.values
        elif self.at <= self.count:
            self.values = (self.values.astype(F32) + arrived.astype(F32)).astype(BF)
            self.send = self.values
        else:
            rows = self.values.shape[0]
            if self.small is not None:
                self.small = pack(unpack(self.small) + unpack(arrived[rows:]))
            if self.at == len(self.bits):
                self.parts = (self.values, arrived)
                return arrived
            self.values = jnp.concatenate([self.values, arrived[:rows]], axis=0)
            self.send = self.values
            if self.small is not None:
                self.send = jnp.concatenate([self.values, self.small], axis=0)
        return self.send

    def join(self, small):
        for bit in range(len(self.order), self.count):
            small = pack(unpack(small) + unpack(swap(small, "dp", 1 << bit)))
        self.small = small
        self.send = jnp.concatenate([self.values, small], axis=0)


ORDER_A = (0, 1, 2)
ORDER_B = (1, 0, 2)


def weight_grad(me, lefts, rights, order, kept, low=0, wide=None):
    half = lefts[0].shape[1] // 2
    wide = wide or rights[0].shape[1]
    count = (len(lefts), len(rights))
    return run(
        functools.partial(weight_pieces, order, 0 if kept else PIECES // 2, low, count),
        (me, *lefts, *rights),
        [shape((half, wide), F32 if kept else BF)],
        scratch=[pltpu.VMEM((half, x.shape[0]), BF) for x in lefts],
        flops=2 * 960 * half * wide,
    )[0]


def mixed_grad(me, normed, proj, heads, mids, order, kept, low):
    half = normed[0].shape[1] // 2
    wide = proj[0].shape[1] - low + heads[0].shape[1]
    return run(
        functools.partial(mixed_pieces, order, 0 if kept else PIECES // 2, low),
        (me, *normed, *proj, *heads, *mids),
        [shape((half, wide), F32 if kept else BF)],
        scratch=[pltpu.VMEM((half, x.shape[0]), BF) for x in normed],
        flops=2 * 960 * half * wide,
    )[0]


def place(me, parts, order):
    rows, wide = 2 * parts[0].shape[0], parts[0].shape[1]
    return run_out(
        functools.partial(place_pieces, order),
        (me, *parts),
        [shape((rows, wide))],
        scratch=[
            pltpu.VMEM((PIECES, rows // PIECES, wide), F32),
            pltpu.SemaphoreType.DMA((PIECES,)),
        ],
    )[0]


def on_device(
    tokens,
    keep_mask,
    grad_out,
    in_weight,
    in_bias,
    out_weight,
    out_bias,
    up_weight,
    up_bias,
    down_weight,
    down_bias,
    gain_one,
    shift_one,
    gain_two,
    shift_two,
):
    rows, model = tokens.shape
    leave(*STAY)
    me = jnp.stack([lax.axis_index("tensor"), lax.axis_index("dp")]).astype(jnp.int32)
    images = keep_mask.shape[0]
    heads = in_weight.shape[1] // (3 * HD)
    width = heads * HD
    hidden = up_weight.shape[1]

    def line(values):
        return values.reshape(1, -1)

    side = 2 * rows
    block = 256
    project_flops = 2 * side * model * 3 * width
    attend_flops = 3 * heads * 4 * HALF * SLOTS * 128 + 2 * side * width * model
    back_flops = 3 * heads * 10 * HALF * SLOTS * 128 + 2 * side * width * model

    def act_grad_of(one, other):
        return run(
            act_back,
            (me, one, other, down_weight),
            [shape((side, hidden))],
            flops=2 * side * model * hidden,
        )[0]

    def feed(norms, act_grad, low, kinds):
        tall = rows * len(norms)
        return run(
            functools.partial(feed_forward, low, len(norms)),
            (me, *norms, up_weight, vectors, act_grad),
            [
                shape((tall, hidden), BF),
                shape((tall, hidden), BF),
                shape((1, hidden)),
                *[shape((rows, model), kind) for kind in kinds],
            ],
            scratch=[pltpu.VMEM((tall, model), F32), pltpu.VMEM((2, rows, block), F32)],
            flops=4 * tall * model * hidden,
        )

    def feed_back(me, *acts):
        return run(
            functools.partial(feed_out, len(acts)),
            (me, *acts, down_weight),
            [shape((rows, model), BF), shape((rows, model))],
            flops=2 * side * model * hidden,
        )

    tok_far = swap(tokens, "tensor", 2)
    tok_core = swap(tokens, "tensor", 1)
    keep_flat = keep_mask.reshape(-1).astype(F32)
    keep_own = lax.dynamic_slice_in_dim(keep_flat, me[0] * rows, rows)[:, None]
    cot = (grad_out.astype(F32) * keep_own).astype(BF)
    cot_core = swap(cot, "tensor", 1)
    pair = in_bias.reshape(heads, 2, HD)
    bias_full = jnp.concatenate([pair[:, :1], jnp.zeros((heads, 1, HD), F32), pair[:, 1:]], axis=1)
    bias_full = bias_full.reshape(1, 3 * width)
    vectors = jnp.stack(
        [gain_one, shift_one, out_bias, gain_two, shift_two, up_bias, down_bias, down_bias]
    )
    stay(in_weight, bias_full, vectors, tokens, cot)
    norm_near, proj_near = run(
        project_local,
        (me, tokens, tok_core, vectors, in_weight, bias_full),
        [shape((side, model), BF), shape((side, 3 * width), BF)],
        flops=project_flops,
    )
    stay(norm_near, out_weight)
    tok_far = after(tok_far, proj_near)

    tok_both = swap(tok_far, "tensor", 1)
    cot_far = swap(after(cot, tok_far), "tensor", 2)
    attend_outs = [
        shape((3 * heads, HALF, SLOTS), BF),
        shape((side, width), BF),
        shape((rows, model), BF),
        shape((rows, model), F32),
    ]
    norm_y, proj_y = run(
        project_one,
        (me, tok_far, vectors, in_weight, bias_full),
        [shape((rows, model), BF), shape((rows, 3 * width), BF)],
        flops=project_flops // 2,
    )
    stay(norm_y)
    norm_both, qkv, probs_far, heads_far, send, far_hold = run(
        attend_far,
        (
            me, proj_near, proj_y, tok_both, vectors, in_weight, bias_full, keep_mask, out_weight,
        ),
        [shape((rows, model), BF), shape((2 * side, 3 * width), BF), *attend_outs],
        flops=project_flops + attend_flops,
    )
    stay(norm_both, qkv, probs_far, heads_far, down_weight, up_weight)
    leave(bias_full)
    arrived = after(swap(send, "tensor", 1), cot_far)
    far_sum = add_round(far_hold, arrived)
    cot_far = after(cot_far, far_sum)
    cot_both = swap(cot_far, "tensor", 1)
    arrived_far = swap(far_sum, "tensor", 2)
    probs_near, heads_near, send, hold = run(
        attend_near,
        (after(me, far_sum), qkv, keep_mask, out_weight),
        attend_outs,
        flops=attend_flops,
    )
    stay(probs_near, heads_near, hold)
    act_grad_near = act_grad_of(cot, cot_core)
    stay(act_grad_near, cot_core)
    arrived_near = after(swap(send, "tensor", 1), arrived_far)
    middle, second = run(
        second_norm,
        (
            after(me, act_grad_near), tokens, hold, arrived_near, arrived_far, vectors,
        ),
        [shape((rows, model)), shape((rows, model), BF)],
    )

    leave(hold)
    stay(middle, second)

    second_far = swap(second, "tensor", 2)
    second_core = swap(second, "tensor", 1)
    act_near, pre_near, up_bias_near, near_hold, near_send = feed(
        (second, second_core), act_grad_near, 0, (F32, BF)
    )
    leave(act_grad_near)
    stay(act_near, pre_near, near_hold, second_core)
    act_grad_far = act_grad_of(cot_far, cot_both)
    stay(cot_far, cot_both, act_grad_far)
    second_far = after(second_far, act_grad_far)
    second_both = swap(second_far, "tensor", 1)
    act_y, pre_y, up_bias_y, far_hold = feed((second_far,), act_grad_far, 0, (F32,))
    stay(act_y, pre_y, second_far, far_hold)
    act_both, pre_both, up_bias_both, far_send = feed((second_both,), act_grad_far, rows, (BF,))
    leave(far_hold)
    far_sum = add_round(far_hold, swap(far_send, "tensor", 1))
    arrived_far = swap(far_sum, "tensor", 2)
    leave(act_grad_far, up_weight)
    stay(act_both, pre_both, second_both)
    acts, cots = (act_near, act_y, act_both), (cot, cot_core, cot_far, cot_both)
    down_send = weight_grad(after(me, far_sum), acts, cots, ORDER_A, False)
    down = Reduction(down_send, ORDER_A)
    seconds = (second, second_core, second_far, second_both)
    pres = (pre_near, pre_y, pre_both)
    up_send = weight_grad(after(me, down_send), seconds, pres, ORDER_B, False)
    up = Reduction(up_send, ORDER_B)
    arrived_near = swap(near_send, "tensor", 1)
    feed_send, feed_hold = feed_back(after(me, up_send), act_y, act_both)
    feed_far = add_round(feed_hold, swap(feed_send, "tensor", 1))
    middle_grad, middle_low, middle_sums = run(
        middle_back,
        (
            after(me, feed_hold), near_hold, arrived_near, arrived_far, middle, cot, vectors,
        ),
        [shape((rows, model)), shape((rows, model), BF), shape((4, model))],
        scratch=[pltpu.VMEM((4, 8, model), F32)],
    )

    mid_far = swap(middle_low, "tensor", 2)
    mid_core = swap(middle_low, "tensor", 1)
    grads = pltpu.VMEM((side, width), BF)
    leave(near_hold)
    stay(middle_grad, middle_low)
    down.values = weight_grad(after(me, middle_low), acts, cots, ORDER_A, True)
    leave(act_y, act_both, cot_core, cot_far, cot_both)
    stay(down.values)
    near_q, near_keys = run(
        back_near,
        (after(me, down.values), middle_low, mid_core, qkv, probs_near, out_weight),
        [shape((side, width)), shape((2 * side, 2 * width))],
        scratch=[grads],
        flops=back_flops,
    )
    leave(probs_near)
    stay(near_q, near_keys, mid_core)
    up.values = weight_grad(after(me, near_q), seconds, pres, ORDER_B, True)
    leave(second, second_core, second_far, second_both, pre_near, pre_y, pre_both)
    stay(up.values)
    mid_far = after(mid_far, up.values)
    mid_both = swap(mid_far, "tensor", 1)
    feed_far = swap(after(feed_far, mid_far), "tensor", 2)
    down.arrive(mid_far)
    up.arrive(mid_far)
    flat_near, flat_far, bias_grad, far_send, far_hold = run(
        back_far,
        (
            after(me, down.send, up.send), mid_far, mid_both, qkv, probs_far,
            out_weight, near_q, near_keys, in_weight,
        ),
        [
            shape((side, 3 * width), BF),
            shape((side, 3 * width), BF),
            shape((1, 2 * width)),
            shape((rows, model), BF),
            shape((rows, model)),
        ],
        scratch=[
            grads,
            pltpu.VMEM((side, width), F32),
            pltpu.VMEM((2 * side, 2 * width), F32),
            pltpu.VMEM((side, 3 * width), BF),
        ],
        flops=back_flops + project_flops,
    )
    leave(qkv, probs_far, near_q, near_keys, out_weight)
    stay(flat_near, flat_far, mid_far, mid_both)
    down.take(bias_grad)
    up.take(bias_grad)
    arrived = after(swap(far_send, "tensor", 1), feed_far, down.came, up.came)
    far_sum = add_round(far_hold, arrived)
    arrived_far = swap(far_sum, "tensor", 2)

    down.arrive(far_sum)
    up.arrive(far_sum)
    near_send, hold = run(
        first_back,
        (after(me, down.send, up.send), flat_near, in_weight),
        [shape((rows, model), BF), shape((rows, model))],
        flops=project_flops,
    )
    leave(in_weight)
    stay(hold)
    normed = (norm_near, norm_y, norm_both)
    split = (3 * width + width) // 2
    flat = (flat_near, flat_far)
    head_rows = (heads_near, heads_far)
    mids = (middle_low, mid_core, mid_far, mid_both)
    arrived_near = swap(near_send, "tensor", 1)
    first_send = weight_grad(after(me, hold), normed, flat, ORDER_A, False, 0, split)
    first = Reduction(first_send, ORDER_A)
    mixed_send = mixed_grad(
        after(me, first_send), normed, flat, head_rows, mids, ORDER_B, False, split
    )
    mixed = Reduction(mixed_send, ORDER_B)
    first.values = weight_grad(after(me, mixed_send), normed, flat, ORDER_A, True, 0, split)
    stay(first.values)
    mixed.values = mixed_grad(
        after(me, first.values, arrived_near), normed, flat, head_rows, mids, ORDER_B, True, split
    )
    leave(norm_near, norm_y, norm_both, flat_near, flat_far, heads_near, heads_far)
    leave(middle_low, mid_core, mid_far, mid_both)
    stay(mixed.values)
    tokens_grad, token_sums = run(
        token_back,
        (
            after(me, mixed.values), hold, arrived_near, arrived_far, tokens, middle_grad, vectors,
        ),
        [shape((rows, model)), shape((2, model))],
        scratch=[pltpu.VMEM((2, 8, model), F32)],
    )
    leave(hold, tokens, middle_grad, vectors)
    feed_send, feed_hold = feed_back(after(me, token_sums), act_near)
    feed_rows = feed_hold + swap(feed_send, "tensor", 1).astype(F32) + feed_far.astype(F32)
    output = (keep_own * (middle + feed_rows + down_bias)).astype(BF)
    leave(*STAY)
    stay(down.values, up.values, first.values, mixed.values)

    now = down.arrive(feed_hold)
    shared = pack(jnp.concatenate([middle_sums, token_sums], axis=0))
    shared = add_small(shared, after(swap(shared, "tensor", 1), now))
    now = first.arrive(now)
    now = mixed.arrive(now)
    shared = unpack(add_small(shared, after(swap(shared, "tensor", 2), now)))
    own = jnp.concatenate(
        [up_bias_near + up_bias_y + up_bias_both, jnp.pad(bias_grad, ((0, 0), (0, hidden - 2 * width)))], axis=0
    )
    small = jnp.concatenate([shared, own], axis=0)
    small = pack(jnp.concatenate([small[:, :split], small[:, split:]], axis=0))
    now = up.arrive(now)
    now = down.arrive(now)
    now = mixed.arrive(now)
    now = first.arrive(now)
    now = up.arrive(now)
    now = mixed.arrive(now)
    now = first.arrive(now)
    while first.at < first.count:
        now = first.arrive(now)
    first.join(small)
    now = down.arrive(now)
    now = up.arrive(now)
    now = mixed.arrive(now)
    now = first.arrive(now)
    now = first.arrive(now)
    now = mixed.arrive(now)
    now = down.arrive(now)
    down_sum = place(after(me, now), down.parts, ORDER_A)
    up.arrive(down_sum)
    up_sum = place(me, up.parts, ORDER_B)
    outs = [shape((model, 3 * width)), shape((width, model))]
    into = place_mixed(after(me, up_sum), 0, first.values, mixed.values, outs)
    now = mixed.arrive(into[1])
    first.arrive(now)
    small = unpack(first.small)
    small = jnp.concatenate([small[:8], small[8:]], axis=1)
    piece = model // PIECES
    in_sum, out_sum = place_mixed(me, 1, first.parts[1], mixed.parts[1], outs, into)
    in_bias_sum = small[7, : 2 * width].reshape(2, heads, HD).transpose(1, 0, 2).reshape(-1)
    return (
        output,
        tokens_grad,
        in_sum,
        in_bias_sum,
        out_sum,
        small[0],
        up_sum,
        small[6],
        down_sum,
        small[1],
        small[4],
        small[5],
        small[2],
        small[3],
    )


def solution(mesh):
    rows = P(("dp", "tensor"), None)
    placed = (
        rows,
        P("dp", None),
        rows,
        P(None, "tensor"),
        P("tensor"),
        P("tensor", None),
        P(),
        P(None, "tensor"),
        P("tensor"),
        P("tensor", None),
        P(),
        P(),
        P(),
        P(),
        P(),
    )
    given = (
        rows,
        rows,
        P(None, "tensor"),
        P("tensor"),
        P("tensor", None),
        P(),
        P(None, "tensor"),
        P("tensor"),
        P("tensor", None),
        P(),
        P(),
        P(),
        P(),
        P(),
    )
    return jax.shard_map(on_device, mesh=mesh, in_specs=placed, out_specs=given, check_vma=False)
```
